32 devices in a mesh: dp: 4 (over x, core), head: 2 (over y), ctx: 4 (over z).
Axes of the slice: x: 2, y: 2, z: 4, core: 2. Of those that a mesh axis runs over, the one named last changes fastest.
Arguments:
- q_latent: bfloat16 [4, 64, 1536], P('dp'), may hold values from -6 to 6
- hidden: bfloat16 [4, 64, 7168], P('dp'), may hold values from -96 to 96
- main_queries: bfloat16 [4, 64, 128, 576], P('dp', 'ctx', 'head'), may hold values from -36 to 36
- main_keys: bfloat16 [4, 4096, 576], P('dp', 'ctx'), may hold values from -6 to 6
- index_keys: bfloat16 [4, 4096, 128], P('dp', 'ctx'), may hold values from -96 to 96
- positions: int32 [4, 64], P('dp'), may hold values from 2048 to 4095, as said below
- w_query: bfloat16 [1536, 8192], P('ctx', 'head'), may hold values from -0.15625 to 0.15625
- w_weights: bfloat16 [7168, 64], P('ctx', 'head'), may hold values from -0.0625 to 0.0625
Outputs:
- grad_query: float32 [1536, 8192], P('ctx', 'head')
- grad_weights: float32 [7168, 64], P('ctx', 'head')
- cross_entropy: float32 [4, 64], P('dp')
The draws below stay inside these ranges and needn't reach their ends.
Inputs may be any that keep to these rules, and one draw needn't show every extreme that they name: `positions`: in each sequence some query sits at the last key and some at the lowest position.
All inputs are finite; a program needn't handle non-finite values.
Results may differ from the reference program's by a relative error of at most 0.0075.
The reference program's roundings to bfloat16 on the way (of `index_query`, `score_grad`, `query_grad` and `weight_grad`) count: a program that leaves them out, or rounds other values in their place, can miss the bound.
Values may be sent and summed in bfloat16 or wider, within the bound.
No kernel may reach another device: no remote copies, remote signals or barrier semaphores. Data moves between devices by JAX's collectives and lax.ppermute only.
A program may use at most 128 MiB of HBM per device.

```python
import jax
import jax.numpy as jnp
from jax import lax

D = 7168
DQ = 1536
HI = 64
DI = 128
HM = 128
DL = 576
Q = 64
CONTEXT = 4096
SEQS = 4


def draw_main_keys(key, part):
    key = jax.random.fold_in(key, 11)
    values = jnp.clip(jax.random.normal(key, (SEQS, CONTEXT, DL), jnp.float32), -6.0, 6.0)
    return values.astype(jnp.bfloat16)


def draw_main_queries(key, part):
    key = jax.random.fold_in(key, 12)
    values = 4.0 * jnp.clip(jax.random.normal(key, (SEQS, Q, HM, DL), jnp.float32), -9.0, 9.0)
    return values.astype(jnp.bfloat16)


def draw_index_keys(key, part):
    key = jax.random.fold_in(key, 13)
    value_key = jax.random.fold_in(key, 2)
    values = jnp.clip(jax.random.normal(value_key, (SEQS, CONTEXT, DI), jnp.float32), -6.0, 6.0)
    return values.astype(jnp.bfloat16)


def draw_hidden(key, part):
    key = jax.random.fold_in(key, 14)
    value_key = jax.random.fold_in(key, 0)
    values = jnp.clip(jax.random.normal(value_key, (SEQS, Q, D), jnp.float32), -6.0, 6.0)
    return values.astype(jnp.bfloat16)


def draw_positions(key, part):
    key = jax.random.fold_in(key, 15)
    offset_key, row_key = jax.random.split(key)
    offsets = jax.random.randint(offset_key, (SEQS, Q), 0, CONTEXT // 2, jnp.int32)
    row_keys = jax.random.split(row_key, SEQS)
    picked = jax.vmap(lambda one: jax.random.permutation(one, Q)[:2])(row_keys)
    columns = jnp.arange(Q, dtype=jnp.int32)[None, :]
    offsets = jnp.where(columns == picked[:, 0:1], 0, offsets)
    offsets = jnp.where(columns == picked[:, 1:2], CONTEXT // 2 - 1, offsets)
    return (CONTEXT - 1 - offsets).astype(jnp.int32)


def block_scale(rng, shape, cuts, least, top_value):
    def one(axis_at, shards_of):
        steps = jax.random.uniform(jax.random.fold_in(jax.random.fold_in(rng, 6), axis_at), (shards_of,), jnp.float32, least / len(cuts), top_value / len(cuts))
        return jnp.repeat(jnp.exp(steps), shape[axis_at] // shards_of).reshape((-1,) + (1,) * (len(shape) - axis_at - 1))

    level = one(*cuts[0])
    for cut in cuts[1:]:
        level = level * one(*cut)
    return level


def scatter_about(key, dims, width, most, cuts=(), held_as=jnp.bfloat16):
    result = width * jax.random.normal(key, dims, jnp.float32)
    if cuts:
        result = result * block_scale(key, dims, cuts, -0.22, 0.18)
    return jnp.clip(result, -most, most).astype(held_as)


def setup_inputs(seed: int = 0) -> dict:
    seeds = jax.random.split(jax.random.key(seed), 9)
    return {
        "q_latent": scatter_about(seeds[0], (SEQS, Q, DQ), 1.0, 6.0, ((0, 4),)),
        "hidden": draw_hidden(jax.random.fold_in(seeds[8], 71), 0),
        "main_queries": draw_main_queries(jax.random.fold_in(seeds[8], 71), 0),
        "main_keys": draw_main_keys(jax.random.fold_in(seeds[8], 71), 0),
        "index_keys": draw_index_keys(jax.random.fold_in(seeds[8], 71), 0),
        "positions": draw_positions(jax.random.fold_in(seeds[8], 71), 0),
        "w_query": scatter_about(seeds[6], (DQ, HI * DI), DQ ** -0.5, 0.15625, ((0, 4), (1, 2))),
        "w_weights": scatter_about(seeds[7], (D, HI), D ** -0.5, 0.0625, ((0, 4), (1, 2))),
    }


score_scale = 192.0 ** -0.5
masked_floor = -1e30


def main_target(queries, key_rows, visible):
    key_float = key_rows.astype(jnp.float32)
    blocks = queries.reshape(Q, HM // 8, 8, DL).transpose(1, 0, 2, 3)

    def per_block(block):
        scores = jnp.einsum('qhd,sd->qhs', block.astype(jnp.float32), key_float) * score_scale
        scores = jnp.where(visible[:, None, :], scores, masked_floor)
        row_max = jnp.max(scores, axis=2, keepdims=True)
        shifted = jnp.where(visible[:, None, :], jnp.exp(scores - row_max), 0.0)
        return jnp.sum(shifted / jnp.sum(shifted, axis=2, keepdims=True), axis=1)

    return jnp.sum(lax.map(per_block, blocks), axis=0) / HM


def reference(q_latent, hidden, main_queries, main_keys, index_keys, positions, w_query, w_weights):
    index_scale = (HI * DI) ** -0.5
    grad_query = jnp.zeros((DQ, HI * DI), jnp.float32)
    grad_weights = jnp.zeros((D, HI), jnp.float32)
    losses = []
    for sequence in range(SEQS):
        latent = q_latent[sequence]
        activations = hidden[sequence]
        index_query = jnp.dot(latent, w_query, preferred_element_type=jnp.float32).astype(jnp.bfloat16)
        head_weights = jnp.dot(activations, w_weights, preferred_element_type=jnp.float32)
        visible = jnp.arange(CONTEXT, dtype=jnp.int32)[None, :] <= positions[sequence][:, None]
        key_float = index_keys[sequence].astype(jnp.float32)
        query_blocks = index_query.reshape(Q, HI // 8, 8, DI).transpose(1, 0, 2, 3)
        weight_blocks = head_weights.reshape(Q, HI // 8, 8).transpose(1, 0, 2)

        def add_logits(running, inputs):
            block, weights = inputs
            affinity = jnp.einsum('qjd,sd->qjs', block.astype(jnp.float32), key_float)
            return running + jnp.sum(weights[:, :, None] * jnp.maximum(affinity, 0.0), axis=1) * index_scale, None

        logits, _ = lax.scan(add_logits, jnp.zeros((Q, CONTEXT), jnp.float32), (query_blocks, weight_blocks))
        target = main_target(main_queries[sequence], main_keys[sequence], visible)
        row_max = jnp.max(jnp.where(visible, logits, masked_floor), axis=1, keepdims=True)
        shifted = jnp.where(visible, jnp.exp(logits - row_max), 0.0)
        row_sum = jnp.sum(shifted, axis=1, keepdims=True)
        index_probs = shifted / row_sum
        log_probs = logits - (row_max + jnp.log(row_sum))
        losses.append(-jnp.sum(jnp.where(visible, target * log_probs, 0.0), axis=1))
        delta = jnp.where(visible, index_probs - target, 0.0)

        def per_block(inputs):
            block, weights = inputs
            affinity = jnp.einsum('qjd,sd->qjs', block.astype(jnp.float32), key_float)
            score_grad = jnp.where(affinity > 0, delta[:, None, :] * weights[:, :, None] * index_scale, 0.0).astype(jnp.bfloat16)
            query_grad = jnp.einsum('qjs,sd->qjd', score_grad.astype(jnp.float32), key_float)
            weight_grad = jnp.sum(delta[:, None, :] * jnp.maximum(affinity, 0.0), axis=2) * index_scale
            return query_grad, weight_grad

        query_grad, weight_grad = lax.map(per_block, (query_blocks, weight_blocks))
        query_grad = query_grad.transpose(1, 0, 2, 3).reshape(Q, HI * DI).astype(jnp.bfloat16)
        weight_grad = weight_grad.transpose(1, 0, 2).reshape(Q, HI).astype(jnp.bfloat16)
        grad_query = grad_query + jnp.dot(latent.T, query_grad, preferred_element_type=jnp.float32)
        grad_weights = grad_weights + jnp.dot(activations.T, weight_grad, preferred_element_type=jnp.float32)
    return grad_query, grad_weights, jnp.stack(losses)
```

```python
import jax
import jax.numpy as jnp
from jax import lax
from jax.sharding import PartitionSpec as P

HI = 64
DI = 128
HM = 128

score_scale = 192.0 ** (-0.5)
index_scale = (HI * DI) ** (-0.5)
masked_floor = -1e30


def folded_ring(size):
    return list(range(0, 1)) + list(range(1, size, 2)) + list(range(2, size, 2))[::-1]


def per_device(
    q_latent, hidden, main_queries, main_keys, index_keys, positions, w_query, w_weights
):
    n = lax.axis_size("ctx")
    z = lax.axis_index("ctx")
    y = lax.axis_index("head")
    dp_size = lax.axis_size("dp")
    dp = lax.axis_index("dp")
    ring = folded_ring(n)
    place_of = [ring.index(k) for k in range(n)]
    ring_table = jnp.array(ring, jnp.int32)
    place = jnp.array(place_of, jnp.int32)[z]
    ring_pairs = [(ring[k], ring[(k + 1) % n]) for k in range(n)]

    def at_place(k):
        return ring_table[lax.rem(k + 2 * n, n)]

    def onward(x):
        return lax.ppermute(x, "ctx", ring_pairs)

    def swap_head(x):
        return lax.ppermute(x, "head", [(0, 1), (1, 0)])

    latent = q_latent[0]
    activations = hidden[0]
    rows = main_keys.shape[1]
    half = rows // 2
    rows_latent = w_query.shape[0]
    rows_hidden = w_weights.shape[0]
    heads_here = w_weights.shape[1]
    queries_here = main_queries.shape[1]
    query_pos = lax.dynamic_slice_in_dim(positions[0], z * queries_here, queries_here)
    own_latent = lax.dynamic_slice_in_dim(latent, z * rows_latent, rows_latent, 1)
    own_hidden = lax.dynamic_slice_in_dim(activations, z * rows_hidden, rows_hidden, 1)

    key_part = lax.dynamic_slice_in_dim(main_keys[0], y * half, half)
    index_part = lax.dynamic_slice_in_dim(index_keys[0], y * half, half)
    other_queries = swap_head(main_queries[0])
    index_mine = [index_part]
    for _ in range(n - 1):
        index_mine.append(onward(index_mine[-1]))
    keys_mine = [key_part]
    for _ in range(n - 1):
        keys_mine.append(onward(keys_mine[-1]))
    index_own = jnp.concatenate(index_mine)
    index_other = swap_head(index_own)
    sources = jnp.stack([at_place(place - t) for t in range(n)])
    base = sources[:, None] * rows + jnp.arange(half, dtype=jnp.int32)[None, :]
    pos_own = (base + y * half).reshape(-1)
    pos_other = (base + (1 - y) * half).reshape(-1)
    visible_own = pos_own[None, :] <= query_pos[:, None]
    visible_other = pos_other[None, :] <= query_pos[:, None]

    query_sum = jnp.dot(own_latent, w_query, preferred_element_type=jnp.float32)
    weight_sum = jnp.dot(own_hidden, w_weights, preferred_element_type=jnp.float32)
    weight_sum = jnp.pad(weight_sum, ((0, 0), (0, 128 - heads_here)))
    partial = jnp.concatenate([query_sum, weight_sum], axis=1)
    width = query_sum.shape[1]

    def partial_of(k):
        return lax.dynamic_slice_in_dim(partial, at_place(k) * queries_here, queries_here)

    total = partial_of(place - 1)
    for t in range(1, n):
        total = onward(total) + partial_of(place - t - 1)
    index_query = total[:, :width].astype(jnp.bfloat16).reshape(queries_here, heads_here, DI)
    head_weights = total[:, width : width + heads_here]

    def affinity_to(keys):
        return jnp.einsum("qjd,sd->qjs", index_query, keys, preferred_element_type=jnp.float32)

    def part_logits(keys):
        reached = jnp.maximum(affinity_to(keys), 0.0)
        return jnp.sum(head_weights[:, :, None] * reached, axis=1) * index_scale

    part_own, part_other = part_logits(index_own), part_logits(index_other)
    from_other, from_own = swap_head((part_own, part_other))
    logits_own = part_own + from_own
    logits_other = part_other + from_other

    all_queries = jnp.concatenate([main_queries[0], other_queries], axis=1)
    scores = jnp.concatenate(
        [
            jnp.einsum("qhd,sd->qhs", all_queries, k, preferred_element_type=jnp.float32)
            for k in keys_mine
        ],
        axis=2,
    )
    scores = jnp.where(visible_own[:, None, :], scores * score_scale, masked_floor)
    top = jnp.max(scores, axis=2)
    shifted = jnp.exp(scores - top[:, :, None])
    mass = jnp.sum(shifted, axis=2)
    half_heads = main_queries.shape[2]
    other_top, other_mass = swap_head((top, mass))
    other_top = jnp.concatenate([other_top[:, half_heads:], other_top[:, :half_heads]], axis=1)
    other_mass = jnp.concatenate([other_mass[:, half_heads:], other_mass[:, :half_heads]], axis=1)
    joint = jnp.maximum(top, other_top)
    mass = mass * jnp.exp(top - joint) + other_mass * jnp.exp(other_top - joint)
    factor = jnp.exp(top - joint) / mass / HM
    target_own = jnp.sum(shifted * factor[:, :, None], axis=1)
    target_own = jnp.where(visible_own, target_own, 0.0)
    target_other = swap_head(target_own)

    floor_own = jnp.where(visible_own, logits_own, masked_floor)
    floor_other = jnp.where(visible_other, logits_other, masked_floor)
    high = jnp.maximum(jnp.max(floor_own, axis=1), jnp.max(floor_other, axis=1))
    exp_own = jnp.exp(floor_own - high[:, None])
    exp_other = jnp.exp(floor_other - high[:, None])
    index_total = jnp.sum(exp_own, axis=1) + jnp.sum(exp_other, axis=1)
    level = (high + jnp.log(index_total))[:, None]

    def loss_part(visible, target, logits):
        return jnp.sum(jnp.where(visible, target * (logits - level), 0.0), axis=1)

    loss = -(
        loss_part(visible_own, target_own, logits_own)
        + loss_part(visible_other, target_other, logits_other)
    )
    delta_own = jnp.where(visible_own, exp_own / index_total[:, None] - target_own, 0.0)
    delta_other = jnp.where(visible_other, exp_other / index_total[:, None] - target_other, 0.0)

    def grads(delta, keys):
        affinity = affinity_to(keys)
        score_grad = jnp.where(
            affinity > 0, delta[:, None, :] * head_weights[:, :, None] * index_scale, 0.0
        ).astype(jnp.bfloat16)
        query_grad = jnp.einsum("qjs,sd->qjd", score_grad, keys, preferred_element_type=jnp.float32)
        weight_grad = jnp.sum(delta[:, None, :] * jnp.maximum(affinity, 0.0), axis=2)
        return query_grad, weight_grad

    query_a, weight_a = grads(delta_own, index_own)
    query_b, weight_b = grads(delta_other, index_other)
    query_grad = (query_a + query_b).reshape(queries_here, width).astype(jnp.bfloat16)
    weight_grad = ((weight_a + weight_b) * index_scale).astype(jnp.bfloat16)
    loss_high = loss.astype(jnp.bfloat16)
    loss_low = (loss - loss_high.astype(jnp.float32)).astype(jnp.bfloat16)
    tail = jnp.concatenate([weight_grad, loss_high[:, None], loss_low[:, None]], axis=1)
    tail = jnp.pad(tail, ((0, 0), (0, 128 - tail.shape[1])))
    piece = jnp.concatenate([query_grad, tail], axis=1)

    pieces = [piece]
    for t in range(1, n):
        pairs = [(k, (k + t) % n) for k in range(n)]
        pieces.append(lax.ppermute(piece, "ctx", pairs))
    stacked = jnp.stack(pieces)
    sequence = jnp.concatenate(
        [lax.dynamic_index_in_dim(stacked, lax.rem(z - k + n, n), 0, False) for k in range(n)]
    )

    def across_dp(x):
        whole, bit = x[None], dp_size // 2
        while bit:
            other = lax.ppermute(whole, "dp", [(k, k ^ bit) for k in range(dp_size)])
            upper = (dp & bit) != 0
            whole = jnp.concatenate([jnp.where(upper, other, whole), jnp.where(upper, whole, other)])
            bit //= 2
        return whole

    latents = across_dp(own_latent)
    hiddens = across_dp(own_hidden)
    everything = across_dp(sequence)
    grad_query = jnp.einsum(
        "bqr,bqc->rc", latents, everything[:, :, :width], preferred_element_type=jnp.float32
    )
    grad_weights = jnp.einsum(
        "bqr,bqc->rc",
        hiddens,
        everything[:, :, width : width + heads_here],
        preferred_element_type=jnp.float32,
    )
    low = sequence[:, width + heads_here : width + heads_here + 2].astype(jnp.float32)
    cross_entropy = low[:, 0] + low[:, 1]
    return (grad_query, grad_weights, cross_entropy[None, :])


def solution(mesh):
    return jax.shard_map(
        per_device,
        mesh=mesh,
        in_specs=(
            P("dp", None, None),
            P("dp", None, None),
            P("dp", "ctx", "head", None),
            P("dp", "ctx", None),
            P("dp", "ctx", None),
            P("dp", None),
            P("ctx", "head"),
            P("ctx", "head"),
        ),
        out_specs=(P("ctx", "head"), P("ctx", "head"), P("dp", None)),
        check_vma=False,
    )
```

```python
import functools
import math

import jax
import jax.numpy as jnp
from jax import lax
from jax.experimental import pallas as pl
from jax.experimental.pallas import tpu as pltpu
from jax.sharding import PartitionSpec as P

HI = 64
DI = 128
HM = 128

index_scale = (HI * DI) ** (-0.5)
exponent_scale = 192.0 ** (-0.5) / math.log(2.0)
masked_floor = -1e30
lanes = 128
f32 = jnp.float32
bf16 = jnp.bfloat16
vmem_limit = 56 * 2**20


def folded_ring(size):
    return [0] + list(range(1, size, 2)) + list(range(2, size, 2))[::-1]


def params():
    return pltpu.CompilerParams(vmem_limit_bytes=vmem_limit)


def in_smem():
    return pl.BlockSpec(memory_space=pltpu.SMEM)


def in_vmem():
    return pl.BlockSpec(memory_space=pltpu.VMEM)


def times(a, b, axis_a, axis_b):
    return lax.dot_general(a, b, (((axis_a,), (axis_b,)), ((), ())), preferred_element_type=f32)


def project_kernel(latent, weight, hidden, hidden_weight, out):
    width = weight.shape[1]
    heads = hidden_weight.shape[0]
    for at in range(0, width, 512):
        out[:, at : at + 512] = times(latent[...], weight[:, at : at + 512], 1, 0)
    mixed = times(hidden[...], hidden_weight[...], 1, 1)
    out[:, width : width + heads] = mixed
    out[:, width + heads :] = jnp.zeros((out.shape[0], lanes - heads), f32)


def project(latent, weight, hidden, hidden_weight):
    count, width = latent.shape[0], weight.shape[1]
    return pl.pallas_call(
        project_kernel,
        out_shape=jax.ShapeDtypeStruct((count, width + lanes), f32),
        in_specs=[in_vmem()] * 4,
        out_specs=in_vmem(),
        compiler_params=params(),
        cost_estimate=pl.CostEstimate(
            flops=2 * count * weight.size, bytes_accessed=2 * weight.size, transcendentals=0
        ),
        name="project",
    )(latent, weight, hidden, hidden_weight)


def score_kernel(first, limits, mine, other, keys, top_before, mass_before, weights, top, top_all, mass_all, mass):
    count, heads, depth = mine.shape
    span = keys.shape[1]
    key_at = lax.broadcasted_iota(jnp.int32, (1, span), 1)
    row_at = lax.broadcasted_iota(jnp.int32, (heads, lanes), 0)
    lane_at = lax.broadcasted_iota(jnp.int32, (heads, lanes), 1)
    group = min(8, count)
    for at in range(0, count, group):
        for source, offset in ((mine, 0), (other, heads)):
            rows = source[at : at + group].reshape(group * heads, depth)
            scores = times(rows, keys[...], 1, 0)
            diagonal = lane_at == row_at + offset
            for k in range(group):
                q = at + k
                visible = key_at <= limits[q]
                one = jnp.where(visible, scores[k * heads : (k + 1) * heads], masked_floor)
                high = jnp.max(one, axis=1, keepdims=True)
                shifted = jnp.exp2((one - high) * exponent_scale)
                total = jnp.sum(shifted, axis=1, keepdims=True)
                weights[q, offset : offset + heads] = shifted.astype(bf16)
                high_row = jnp.sum(jnp.where(diagonal, high, 0.0), axis=0, keepdims=True)
                total_row = jnp.sum(jnp.where(diagonal, total, 0.0), axis=0, keepdims=True)
                if offset == 0:
                    top[q : q + 1, :] = high_row
                    mass[q : q + 1, :] = total_row
                else:
                    top[q : q + 1, :] += high_row
                    mass[q : q + 1, :] += total_row
    if first:
        top_all[...] = top[...]
        mass_all[...] = mass[...]
    else:
        before, now = top_before[...], top[...]
        joint = jnp.maximum(before, now)
        top_all[...] = joint
        mass_all[...] = mass_before[...] * jnp.exp2((before - joint) * exponent_scale) + mass[
            ...
        ] * jnp.exp2((now - joint) * exponent_scale)


def score(limits, mine, other, keys, before):
    count, heads, depth = mine.shape
    span = keys.shape[1]
    stats = jax.ShapeDtypeStruct((count, lanes), f32)
    first = before is None
    if first:
        before = (jnp.zeros((count, lanes), f32),) * 2
    return pl.pallas_call(
        functools.partial(score_kernel, first),
        out_shape=(jax.ShapeDtypeStruct((count, 2 * heads, span), bf16), stats, stats, stats),
        in_specs=[in_smem()] + [in_vmem()] * 5,
        out_specs=(in_vmem(),) * 4,
        scratch_shapes=[pltpu.VMEM((count, lanes), f32)],
        compiler_params=params(),
        cost_estimate=pl.CostEstimate(
            flops=4 * count * heads * depth * span,
            bytes_accessed=2 * (2 * mine.size + keys.size + 2 * count * heads * span),
            transcendentals=2 * count * heads * span,
        ),
        name="score",
    )(limits, mine, other, keys, *before)


def target_kernel(blocks, *refs):
    weights, tops = refs[:blocks], refs[blocks : 2 * blocks]
    top, mass, other_top, other_mass, out = refs[2 * blocks :]
    count, heads, span = weights[0].shape
    far_top = pltpu.roll(other_top[...], heads // 2, 1)
    far_mass = pltpu.roll(other_mass[...], heads // 2, 1)
    joint = jnp.maximum(top[...], far_top)
    total = mass[...] * jnp.exp2((top[...] - joint) * exponent_scale) + far_mass * jnp.exp2(
        (far_top - joint) * exponent_scale
    )
    row_at = lax.broadcasted_iota(jnp.int32, (heads, lanes), 0)
    lane_at = lax.broadcasted_iota(jnp.int32, (heads, lanes), 1)
    diagonal = row_at == lane_at
    inverse = 1.0 / (total * HM)
    for t in range(blocks):
        factor = jnp.exp2((tops[t][...] - joint) * exponent_scale) * inverse
        for q in range(count):
            column = jnp.sum(
                jnp.where(diagonal, factor[q : q + 1, :], 0.0), axis=1, keepdims=True
            )
            mixed = weights[t][q].astype(f32) * column
            out[q : q + 1, t * span : (t + 1) * span] = jnp.sum(mixed, axis=0, keepdims=True)


def make_target(weights, tops, top, mass, other_top, other_mass):
    blocks = len(weights)
    count, heads, span = weights[0].shape
    group = min(8, count)

    def stat_spec():
        return pl.BlockSpec((group, lanes), lambda i: (i, 0))

    return pl.pallas_call(
        functools.partial(target_kernel, blocks),
        grid=(count // group,),
        out_shape=jax.ShapeDtypeStruct((count, blocks * span), f32),
        in_specs=[pl.BlockSpec((group, heads, span), lambda i: (i, 0, 0))] * blocks
        + [stat_spec() for _ in range(blocks + 4)],
        out_specs=pl.BlockSpec((group, blocks * span), lambda i: (i, 0)),
        compiler_params=params(),
        cost_estimate=pl.CostEstimate(
            flops=2 * blocks * count * heads * span,
            bytes_accessed=2 * blocks * count * heads * span,
            transcendentals=0,
        ),
        name="target",
    )(*weights, *tops, top, mass, other_top, other_mass)


def query_rows(total, heads):
    return jnp.concatenate(
        [total[:, j * DI : (j + 1) * DI].astype(bf16) for j in range(heads)], axis=0
    )


def logits_kernel(heads, total, own, other, out):
    count = total.shape[0]
    query = query_rows(total, heads)
    columns = [total[:, heads * DI + j : heads * DI + j + 1] for j in range(heads)]
    span = 512
    for part, keys in enumerate((own, other)):
        for at in range(0, keys.shape[0], span):
            affinity = times(query, keys[at : at + span, :], 1, 1)
            running = jnp.zeros((count, span), f32)
            for j in range(heads):
                reached = jnp.maximum(affinity[j * count : (j + 1) * count], 0.0)
                running = running + columns[j] * reached
            out[part, :, at : at + span] = running * index_scale


def make_logits(heads, total, own, other):
    count, length = total.shape[0], own.shape[0]
    return pl.pallas_call(
        functools.partial(logits_kernel, heads),
        out_shape=jax.ShapeDtypeStruct((2, count, length), f32),
        in_specs=[in_vmem()] * 3,
        out_specs=in_vmem(),
        compiler_params=params(),
        cost_estimate=pl.CostEstimate(
            flops=4 * count * heads * DI * length,
            bytes_accessed=4 * (total.size + 2 * count * length) + 4 * length * DI,
            transcendentals=0,
        ),
        name="logits",
    )(total, own, other)


def gradient_kernel(
    heads, blocks, bases, positions, total, own, other, part, far, target_own, target_other, out, logit, flow
):
    count = total.shape[0]
    span = own.shape[0] // blocks
    query = query_rows(total, heads)
    position = positions[:, 0:1]
    key_at = lax.broadcasted_iota(jnp.int32, (count, span), 1)
    sides = ((own, target_own), (other, target_other))

    def seen(side, t):
        return key_at + bases[side, t] <= position

    highs = []
    for side in range(2):
        high = jnp.full((count, span), masked_floor, f32)
        for t in range(blocks):
            at = slice(t * span, (t + 1) * span)
            value = part[side, :, at] + far[1 - side, :, at]
            logit[side, :, at] = value
            high = jnp.maximum(high, jnp.where(seen(side, t), value, masked_floor))
        highs.append(jnp.max(high, axis=1, keepdims=True))
    high = jnp.maximum(highs[0], highs[1])
    sums = []
    for side in range(2):
        running = jnp.zeros((count, span), f32)
        for t in range(blocks):
            at = slice(t * span, (t + 1) * span)
            grown = jnp.exp(logit[side, :, at] - high)
            running = running + jnp.where(seen(side, t), grown, 0.0)
        sums.append(jnp.sum(running, axis=1, keepdims=True))
    mass = sums[0] + sums[1]
    level = high + jnp.log(mass)
    inverse = 1.0 / mass
    columns = [
        total[:, heads * DI + j : heads * DI + j + 1] * index_scale for j in range(heads)
    ]
    losses = []
    query_sum = jnp.zeros((heads * count, DI), f32)
    flow[...] = jnp.zeros(flow.shape, f32)
    for side, (keys, target) in enumerate(sides):
        running = jnp.zeros((count, span), f32)
        for t in range(blocks):
            at = slice(t * span, (t + 1) * span)
            visible = seen(side, t)
            value = logit[side, :, at]
            wanted = target[:, at]
            running = running + jnp.where(visible, wanted * (value - level), 0.0)
            grown = jnp.exp(value - high) * inverse
            delta = jnp.where(visible, grown - wanted, 0.0)
            affinity = times(query, keys[at, :], 1, 1)
            grads = []
            for j in range(heads):
                rows = slice(j * count, (j + 1) * count)
                one = affinity[rows]
                grads.append(jnp.where(one > 0, delta * columns[j], 0.0).astype(bf16))
                product = delta * jnp.maximum(one, 0.0)
                folded = product[:, :lanes]
                for k in range(lanes, span, lanes):
                    folded = folded + product[:, k : k + lanes]
                flow[rows, :] += folded
            query_sum = query_sum + times(jnp.concatenate(grads, axis=0), keys[at, :], 1, 0)
        losses.append(jnp.sum(running, axis=1, keepdims=True))
    loss = -(losses[0] + losses[1])
    lane_at = lax.broadcasted_iota(jnp.int32, (count, lanes), 1)
    tail = jnp.zeros((count, lanes), f32)
    for j in range(heads):
        rows = slice(j * count, (j + 1) * count)
        out[:, j * DI : (j + 1) * DI] = query_sum[rows].astype(bf16)
        column = jnp.sum(flow[rows, :], axis=1, keepdims=True) * index_scale
        tail = jnp.where(lane_at == j, column, tail)
    loss_high = loss.astype(bf16).astype(f32)
    tail = jnp.where(lane_at == heads, loss_high, tail)
    tail = jnp.where(lane_at == heads + 1, loss - loss_high, tail)
    out[:, heads * DI :] = tail.astype(bf16)


def gradients(heads, blocks, bases, positions, total, own, other, part, far, target_own, target_other):
    count, length = total.shape[0], own.shape[0]
    return pl.pallas_call(
        functools.partial(gradient_kernel, heads, blocks),
        out_shape=jax.ShapeDtypeStruct((count, heads * DI + lanes), bf16),
        in_specs=[in_smem()] + [in_vmem()] * 8,
        out_specs=in_vmem(),
        scratch_shapes=[
            pltpu.VMEM((2, count, length), f32),
            pltpu.VMEM((heads * count, lanes), f32),
        ],
        compiler_params=params(),
        cost_estimate=pl.CostEstimate(
            flops=8 * count * heads * DI * length,
            bytes_accessed=4 * (total.size + 6 * count * length) + 4 * length * DI,
            transcendentals=4 * count * length,
        ),
        name="gradient",
    )(bases, positions, total, own, other, part, far, target_own, target_other)


def outer_kernel(parts, blocks, place, latents, hiddens, *refs):
    bodies, tails = refs[:parts], refs[parts : 2 * parts]
    grad, grad_mixed, rows, tail_rows = refs[2 * parts :]
    count = bodies[0].shape[1]
    for k in range(parts):
        for t in range(blocks):
            to = pl.ds(pl.multiple_of(place[k, t] * count, count), count)
            rows[to, :] = bodies[k][t]

    grad[...] = times(latents[...], rows[...], 0, 0)

    @pl.when(pl.program_id(0) == 0)
    def _():
        for k in range(parts):
            for t in range(blocks):
                to = pl.ds(pl.multiple_of(place[k, t] * count, count), count)
                tail_rows[to, :] = tails[k][t]
        mixed = times(tail_rows[...], hiddens[...], 0, 0)
        grad_mixed[...] = mixed[: grad_mixed.shape[0]]


def outer(heads, place, latents, hiddens, parts):
    blocks, count, _ = parts[0].shape
    total = latents.shape[0]
    width = heads * DI
    span = 512
    row_count, hidden_count = latents.shape[1], hiddens.shape[1]
    body = [pl.BlockSpec((blocks, count, span), lambda i: (0, 0, i)) for _ in parts]
    tail = [
        pl.BlockSpec((blocks, count, lanes), lambda i: (0, 0, width // lanes)) for _ in parts
    ]
    return pl.pallas_call(
        functools.partial(outer_kernel, len(parts), blocks),
        grid=(width // span,),
        out_shape=(
            jax.ShapeDtypeStruct((row_count, width), f32),
            jax.ShapeDtypeStruct((heads, hidden_count), f32),
        ),
        in_specs=[
            in_smem(),
            pl.BlockSpec((total, row_count), lambda i: (0, 0)),
            pl.BlockSpec((total, hidden_count), lambda i: (0, 0)),
        ]
        + body
        + tail,
        out_specs=(
            pl.BlockSpec((row_count, span), lambda i: (0, i)),
            pl.BlockSpec((heads, hidden_count), lambda i: (0, 0)),
        ),
        scratch_shapes=[pltpu.VMEM((total, span), bf16), pltpu.VMEM((total, lanes), bf16)],
        compiler_params=params(),
        cost_estimate=pl.CostEstimate(
            flops=2 * total * row_count * width,
            bytes_accessed=4 * row_count * width + 2 * total * width,
            transcendentals=0,
        ),
        name="outer",
    )(place, latents, hiddens, *parts, *parts)


def per_device(
    q_latent, hidden, main_queries, main_keys, index_keys, positions, w_query, w_weights
):
    n = lax.axis_size("ctx")
    z = lax.axis_index("ctx")
    y = lax.axis_index("head")
    dp_size = lax.axis_size("dp")
    dp = lax.axis_index("dp")
    ring = folded_ring(n)
    place_of = [ring.index(k) for k in range(n)]
    ring_table = jnp.array(ring, jnp.int32)
    place = jnp.array(place_of, jnp.int32)[z]
    ring_pairs = [(ring[k], ring[(k + 1) % n]) for k in range(n)]

    def at_place(k):
        return ring_table[lax.rem(k + 2 * n, n)]

    def onward(x):
        return lax.ppermute(x, "ctx", ring_pairs)

    def swap_head(x):
        return lax.ppermute(x, "head", [(0, 1), (1, 0)])

    rows = main_keys.shape[1]
    half = rows // 2
    rows_latent = w_query.shape[0]
    rows_hidden = w_weights.shape[0]
    heads_here = w_weights.shape[1]
    width = heads_here * DI
    queries_here = main_queries.shape[1]
    query_pos = lax.dynamic_slice_in_dim(positions[0], z * queries_here, queries_here)
    own_latent = lax.dynamic_slice_in_dim(q_latent[0], z * rows_latent, rows_latent, 1)
    own_hidden = lax.dynamic_slice_in_dim(hidden[0], z * rows_hidden, rows_hidden, 1)

    queries = main_queries[0]
    other_queries = swap_head(queries)
    key_part = lax.dynamic_slice_in_dim(main_keys[0].T, y * half, half, 1)
    keys_mine = [key_part]
    for _ in range(n - 1):
        keys_mine.append(onward(keys_mine[-1]))
    index_mine = [lax.dynamic_slice_in_dim(index_keys[0], y * half, half)]
    for _ in range(n - 1):
        index_mine.append(onward(index_mine[-1]))
    index_own = jnp.concatenate(index_mine)
    index_other = swap_head(index_own)
    sources = jnp.stack([at_place(place - t) for t in range(n)]) * rows
    base_own = sources + y * half
    bases = jnp.stack([base_own, sources + (1 - y) * half])

    partial = project(own_latent, w_query, own_hidden, w_weights.T)

    def partial_of(k):
        return lax.dynamic_slice_in_dim(partial, at_place(k) * queries_here, queries_here)

    total = partial_of(place - 1)
    for t in range(1, n):
        total = onward(total) + partial_of(place - t - 1)

    part = make_logits(heads_here, total, index_own, index_other)
    far = swap_head(part)

    weights, tops, before = [], [], None
    for t in range(n):
        limits = query_pos - base_own[t]
        numer, top, *before = score(limits, queries, other_queries, keys_mine[t], before)
        weights.append(numer)
        tops.append(top)
    far_top, far_mass = swap_head(jnp.stack(before))
    target_own = make_target(weights, tops, *before, far_top, far_mass)
    target_other = swap_head(target_own)

    position_rows = jnp.broadcast_to(query_pos[:, None], (queries_here, lanes))
    piece = gradients(
        heads_here,
        n,
        bases,
        position_rows,
        total,
        index_own,
        index_other,
        part,
        far,
        target_own,
        target_other,
    )

    pieces = [piece]
    for t in range(1, n):
        pairs = [(k, (k + t) % n) for k in range(n)]
        pieces.append(lax.ppermute(piece, "ctx", pairs))
    sequence = jnp.stack(pieces)

    def swap_dp(x, bit):
        return lax.ppermute(x, "dp", [(k, k ^ bit) for k in range(dp_size)])

    gathered = [sequence]
    bit = dp_size // 2
    while bit:
        gathered = gathered + [swap_dp(x, bit) for x in gathered]
        bit //= 2
    flips = [0]
    bit = dp_size // 2
    while bit:
        flips = flips + [k ^ bit for k in flips]
        bit //= 2
    steps = lax.rem(z - jnp.arange(n, dtype=jnp.int32) + n, n)
    where_from = jnp.stack([(dp ^ k) * n + steps for k in flips])
    both = lax.all_gather(jnp.concatenate([own_latent, own_hidden], axis=1), "dp")
    both = both.reshape(-1, rows_latent + rows_hidden)
    if queries_here % 16:
        flat = jnp.concatenate(gathered)
        order = jnp.argsort(where_from.reshape(-1))
        gathered = [flat[order].reshape(1, -1, flat.shape[2])]
        where_from = jnp.zeros((1, 1), jnp.int32)
    grad_query, grad_weights = outer(
        heads_here, where_from, both[:, :rows_latent], both[:, rows_latent:], gathered
    )
    low = sequence[:, :, width + heads_here : width + heads_here + 2].astype(f32)
    low = low[:, :, 0] + low[:, :, 1]
    losses = jnp.concatenate([low[steps[k]] for k in range(n)])
    return (grad_query, grad_weights.T, losses[None, :])


def solution(mesh):
    return jax.shard_map(
        per_device,
        mesh=mesh,
        in_specs=(
            P("dp", None, None),
            P("dp", None, None),
            P("dp", "ctx", "head", None),
            P("dp", "ctx", None),
            P("dp", "ctx", None),
            P("dp", None),
            P("ctx", "head"),
            P("ctx", "head"),
        ),
        out_specs=(P("ctx", "head"), P("ctx", "head"), P("dp", None)),
        check_vma=False,
    )
```

```python
import functools
import math

import jax
import jax.numpy as jnp
import numpy as np
from jax import lax
from jax.experimental import pallas as pl
from jax.experimental.pallas import tpu as pltpu
from jax.sharding import PartitionSpec as P

HI = 64
DI = 128
HM = 128

index_scale = (HI * DI) ** (-0.5)
exponent_scale = 192.0 ** (-0.5) / math.log(2.0)
masked_floor = -1e30
lanes = 128
f32 = jnp.float32
bf16 = jnp.bfloat16
vmem_limit = 24 * 2**20


def folded_ring(size):
    return [0] + list(range(1, size, 2)) + list(range(2, size, 2))[::-1]


def params():
    return pltpu.CompilerParams(vmem_limit_bytes=vmem_limit)


def in_smem():
    return pl.BlockSpec(memory_space=pltpu.SMEM)


def in_vmem():
    return pl.BlockSpec(memory_space=pltpu.VMEM)


def times(a, b, axis_a, axis_b):
    return lax.dot_general(a, b, (((axis_a,), (axis_b,)), ((), ())), preferred_element_type=f32)


def device_table(n, heads, dp_size, rows):
    ring = folded_ring(n)
    half = rows // heads
    flips = dp_flips(dp_size)
    table = []
    for z in range(n):
        place = ring.index(z)
        behind = [ring[(place - t) % n] for t in range(n)]
        for y in range(heads):
            for dp in range(dp_size):
                row = [z] + [ring[(place - 1 - t) % n] for t in range(n)]
                row += [k * rows + y * half for k in behind]
                row += [k * rows + (1 - y) * half for k in behind]
                row += [(dp ^ k) * n + (z - t) % n for k in flips for t in range(n)]
                row += [flips.index(dp ^ b) for b in range(dp_size)]
                table.append(row)
    return np.array(table, np.int32)


def dp_flips(dp_size):
    flips, bit = [0], dp_size // 2
    while bit:
        flips, bit = flips + [k ^ bit for k in flips], bit // 2
    return flips


def project_kernel(aligned, info, latent, weight, hidden, hidden_weight, *outs):
    *parts, kept = outs
    width = weight.shape[1]
    heads = hidden_weight.shape[0]
    count = parts[0].shape[0]
    if aligned:
        starts = [pl.multiple_of(info[1 + k] * count, count) for k in range(len(parts))]
        rows = jnp.concatenate([latent[pl.ds(k, count), :] for k in starts], axis=0)
        mixed_rows = jnp.concatenate([hidden[pl.ds(k, count), :] for k in starts], axis=0)
    else:
        rows, mixed_rows = latent[...], hidden[...]
    for at in range(0, width, 512):
        product = times(rows, weight[:, at : at + 512], 1, 0)
        for k, out in enumerate(parts):
            out[:, at : at + 512] = product[k * count : (k + 1) * count]
    mixed = times(mixed_rows, hidden_weight[...], 1, 1)
    for k, out in enumerate(parts):
        out[:, width : width + heads] = mixed[k * count : (k + 1) * count]
        out[:, width + heads :] = jnp.zeros((count, lanes - heads), f32)
    kept[:, : latent.shape[1]] = latent[...]
    kept[:, latent.shape[1] :] = hidden[...]


def project(info, count, latent, weight, hidden, hidden_weight):
    queries, width = latent.shape[0], weight.shape[1]
    depth, hidden_depth = weight.shape[0], hidden_weight.shape[1]
    blocks = queries // count
    aligned = count % 16 == 0 and depth % lanes == 0 and hidden_depth % lanes == 0
    columns = lambda i, info: (0, info[0])
    whole = lambda i, info: (0, 0)
    kept = None
    if not aligned:
        latent = lax.dynamic_slice_in_dim(latent, info[0] * depth, depth, 1)
        hidden = lax.dynamic_slice_in_dim(hidden, info[0] * hidden_depth, hidden_depth, 1)
        kept = jnp.concatenate([latent, hidden], axis=1)
        order = info[1 : 1 + blocks]
        latent = latent.reshape(blocks, count, depth)[order].reshape(queries, depth)
        hidden = hidden.reshape(blocks, count, hidden_depth)[order].reshape(queries, hidden_depth)
        columns = whole
    *parts, kept_here = pl.pallas_call(
        functools.partial(project_kernel, aligned),
        grid_spec=pltpu.PrefetchScalarGridSpec(
            num_scalar_prefetch=1,
            grid=(1,),
            in_specs=[
                pl.BlockSpec((queries, depth), columns),
                pl.BlockSpec((depth, width), whole),
                pl.BlockSpec((queries, hidden_depth), columns),
                pl.BlockSpec(hidden_weight.shape, whole),
            ],
            out_specs=[pl.BlockSpec((count, width + lanes), whole)] * blocks
            + [pl.BlockSpec((queries, depth + hidden_depth), whole)],
        ),
        out_shape=[jax.ShapeDtypeStruct((count, width + lanes), f32)] * blocks
        + [jax.ShapeDtypeStruct((queries, depth + hidden_depth), bf16)],
        compiler_params=params(),
        cost_estimate=pl.CostEstimate(
            flops=2 * queries * weight.size, bytes_accessed=2 * weight.size, transcendentals=0
        ),
        name="project",
    )(info, latent, weight, hidden, hidden_weight)
    return parts, kept_here if aligned else kept


def score_kernel(
    t, base_at, info, positions, mine, other, keys, top_before, mass_before, weights, top, top_all, mass_all, mass
):
    count, heads, depth = mine.shape
    limits = [positions[info[0] * count + q] - info[base_at] for q in range(count)]
    span = keys.shape[1]
    key_at = lax.broadcasted_iota(jnp.int32, (1, span), 1)
    row_at = lax.broadcasted_iota(jnp.int32, (heads, lanes), 0)
    lane_at = lax.broadcasted_iota(jnp.int32, (heads, lanes), 1)
    group = min(8, count)
    for at in range(0, count, group):
        for source, offset in ((mine, 0), (other, heads)):
            rows = source[at : at + group].reshape(group * heads, depth)
            scores = times(rows, keys[...], 1, 0)
            diagonal = lane_at == row_at + offset
            for k in range(group):
                q = at + k
                visible = key_at <= limits[q]
                one = jnp.where(visible, scores[k * heads : (k + 1) * heads], masked_floor)
                high = jnp.max(one, axis=1, keepdims=True)
                shifted = jnp.exp2((one - high) * exponent_scale)
                total = jnp.sum(shifted, axis=1, keepdims=True)
                weights[q, offset : offset + heads] = shifted.astype(bf16)
                high_row = jnp.sum(jnp.where(diagonal, high, 0.0), axis=0, keepdims=True)
                total_row = jnp.sum(jnp.where(diagonal, total, 0.0), axis=0, keepdims=True)
                if offset == 0:
                    top[q : q + 1, :] = high_row
                    mass[q : q + 1, :] = total_row
                else:
                    top[q : q + 1, :] += high_row
                    mass[q : q + 1, :] += total_row
    if t == 0:
        top_all[...] = top[...]
        mass_all[...] = mass[...]
    else:
        before, now = top_before[...], top[...]
        joint = jnp.maximum(before, now)
        top_all[...] = joint
        mass_all[...] = mass_before[...] * jnp.exp2((before - joint) * exponent_scale) + mass[
            ...
        ] * jnp.exp2((now - joint) * exponent_scale)


def score(t, n, info, positions, mine, other, keys, before):
    count, heads, depth = mine.shape
    span = keys.shape[1]
    stats = jax.ShapeDtypeStruct((count, lanes), f32)
    if before is None:
        before = (jnp.zeros((count, lanes), f32),) * 2
    return pl.pallas_call(
        functools.partial(score_kernel, t, 1 + n + t),
        out_shape=(jax.ShapeDtypeStruct((count, 2 * heads, span), bf16), stats, stats, stats),
        in_specs=[in_smem()] * 2 + [in_vmem()] * 5,
        out_specs=(in_vmem(),) * 4,
        scratch_shapes=[pltpu.VMEM((count, lanes), f32)],
        compiler_params=params(),
        cost_estimate=pl.CostEstimate(
            flops=4 * count * heads * depth * span,
            bytes_accessed=2 * (2 * mine.size + keys.size + 2 * count * heads * span),
            transcendentals=2 * count * heads * span,
        ),
        name="score",
    )(info, positions, mine, other, keys, *before)


def target_kernel(blocks, *refs):
    weights, tops = refs[:blocks], refs[blocks : 2 * blocks]
    top, mass, other_top, other_mass, out = refs[2 * blocks :]
    count, heads, span = weights[0].shape
    far_top = pltpu.roll(other_top[...], heads // 2, 1)
    far_mass = pltpu.roll(other_mass[...], heads // 2, 1)
    joint = jnp.maximum(top[...], far_top)
    total = mass[...] * jnp.exp2((top[...] - joint) * exponent_scale) + far_mass * jnp.exp2(
        (far_top - joint) * exponent_scale
    )
    row_at = lax.broadcasted_iota(jnp.int32, (heads, lanes), 0)
    lane_at = lax.broadcasted_iota(jnp.int32, (heads, lanes), 1)
    diagonal = row_at == lane_at
    inverse = 1.0 / (total * HM)
    for t in range(blocks):
        factor = jnp.exp2((tops[t][...] - joint) * exponent_scale) * inverse
        for q in range(count):
            column = jnp.sum(
                jnp.where(diagonal, factor[q : q + 1, :], 0.0), axis=1, keepdims=True
            )
            mixed = weights[t][q].astype(f32) * column
            out[q : q + 1, t * span : (t + 1) * span] = jnp.sum(mixed, axis=0, keepdims=True)


def make_target(weights, tops, top, mass, other_top, other_mass):
    blocks = len(weights)
    count, heads, span = weights[0].shape
    group = min(8, count)

    def stat_spec():
        return pl.BlockSpec((group, lanes), lambda i: (i, 0))

    return pl.pallas_call(
        functools.partial(target_kernel, blocks),
        grid=(count // group,),
        out_shape=jax.ShapeDtypeStruct((count, blocks * span), f32),
        in_specs=[pl.BlockSpec((group, heads, span), lambda i: (i, 0, 0))] * blocks
        + [stat_spec() for _ in range(blocks + 4)],
        out_specs=pl.BlockSpec((group, blocks * span), lambda i: (i, 0)),
        compiler_params=params(),
        cost_estimate=pl.CostEstimate(
            flops=2 * blocks * count * heads * span,
            bytes_accessed=2 * blocks * count * heads * span,
            transcendentals=0,
        ),
        name="target",
    )(*weights, *tops, top, mass, other_top, other_mass)


def query_rows(total, heads):
    return jnp.concatenate(
        [total[:, j * DI : (j + 1) * DI].astype(bf16) for j in range(heads)], axis=0
    )


def logits_kernel(heads, received, here, own, other, out):
    count = received.shape[0]
    total = received[...] + here[...]
    query = query_rows(total, heads)
    columns = [total[:, heads * DI + j : heads * DI + j + 1] for j in range(heads)]
    span = 512
    for part, keys in enumerate((own, other)):
        for at in range(0, keys.shape[0], span):
            affinity = times(query, keys[at : at + span, :], 1, 1)
            running = jnp.zeros((count, span), f32)
            for j in range(heads):
                reached = jnp.maximum(affinity[j * count : (j + 1) * count], 0.0)
                running = running + columns[j] * reached
            out[part, :, at : at + span] = running * index_scale


def make_logits(heads, received, here, own, other):
    count, length = received.shape[0], own.shape[0]
    return pl.pallas_call(
        functools.partial(logits_kernel, heads),
        out_shape=jax.ShapeDtypeStruct((2, count, length), f32),
        in_specs=[in_vmem()] * 4,
        out_specs=in_vmem(),
        compiler_params=params(),
        cost_estimate=pl.CostEstimate(
            flops=4 * count * heads * DI * length,
            bytes_accessed=4 * (2 * received.size + 2 * count * length) + 4 * length * DI,
            transcendentals=0,
        ),
        name="logits",
    )(received, here, own, other)


def gradient_kernel(
    heads, blocks, info, positions, received, here, own, other, part, far, target_own, target_other, out, logit, flow
):
    count = received.shape[0]
    total = received[...] + here[...]
    span = own.shape[0] // blocks
    query = query_rows(total, heads)
    row_at = lax.broadcasted_iota(jnp.int32, (count, lanes), 0)
    position = jnp.zeros((count, lanes), jnp.int32)
    for q in range(count):
        position = jnp.where(row_at == q, positions[info[0] * count + q], position)
    position = position[:, 0:1]
    key_at = lax.broadcasted_iota(jnp.int32, (count, span), 1)
    sides = ((own, target_own), (other, target_other))

    def seen(side, t):
        return key_at + info[1 + (1 + side) * blocks + t] <= position

    highs = []
    for side in range(2):
        high = jnp.full((count, span), masked_floor, f32)
        for t in range(blocks):
            at = slice(t * span, (t + 1) * span)
            value = part[side, :, at] + far[1 - side, :, at]
            logit[side, :, at] = value
            high = jnp.maximum(high, jnp.where(seen(side, t), value, masked_floor))
        highs.append(jnp.max(high, axis=1, keepdims=True))
    high = jnp.maximum(highs[0], highs[1])
    sums = []
    for side in range(2):
        running = jnp.zeros((count, span), f32)
        for t in range(blocks):
            at = slice(t * span, (t + 1) * span)
            grown = jnp.exp(logit[side, :, at] - high)
            running = running + jnp.where(seen(side, t), grown, 0.0)
        sums.append(jnp.sum(running, axis=1, keepdims=True))
    mass = sums[0] + sums[1]
    level = high + jnp.log(mass)
    inverse = 1.0 / mass
    columns = [
        total[:, heads * DI + j : heads * DI + j + 1] * index_scale for j in range(heads)
    ]
    losses = []
    query_sum = jnp.zeros((heads * count, DI), f32)
    flow[...] = jnp.zeros(flow.shape, f32)
    for side, (keys, target) in enumerate(sides):
        running = jnp.zeros((count, span), f32)
        for t in range(blocks):
            at = slice(t * span, (t + 1) * span)
            visible = seen(side, t)
            value = logit[side, :, at]
            wanted = target[:, at]
            running = running + jnp.where(visible, wanted * (value - level), 0.0)
            grown = jnp.exp(value - high) * inverse
            delta = jnp.where(visible, grown - wanted, 0.0)
            affinity = times(query, keys[at, :], 1, 1)
            grads = []
            for j in range(heads):
                rows = slice(j * count, (j + 1) * count)
                one = affinity[rows]
                grads.append(jnp.where(one > 0, delta * columns[j], 0.0).astype(bf16))
                product = delta * jnp.maximum(one, 0.0)
                folded = product[:, :lanes]
                for k in range(lanes, span, lanes):
                    folded = folded + product[:, k : k + lanes]
                flow[rows, :] += folded
            query_sum = query_sum + times(jnp.concatenate(grads, axis=0), keys[at, :], 1, 0)
        losses.append(jnp.sum(running, axis=1, keepdims=True))
    loss = -(losses[0] + losses[1])
    lane_at = lax.broadcasted_iota(jnp.int32, (count, lanes), 1)
    tail = jnp.zeros((count, lanes), f32)
    for j in range(heads):
        rows = slice(j * count, (j + 1) * count)
        out[:, j * DI : (j + 1) * DI] = query_sum[rows].astype(bf16)
        column = jnp.sum(flow[rows, :], axis=1, keepdims=True) * index_scale
        tail = jnp.where(lane_at == j, column, tail)
    loss_high = loss.astype(bf16).astype(f32)
    tail = jnp.where(lane_at == heads, loss_high, tail)
    tail = jnp.where(lane_at == heads + 1, loss - loss_high, tail)
    out[:, heads * DI :] = tail.astype(bf16)


def gradients(heads, blocks, info, positions, received, here, own, other, part, far, target_own, target_other):
    count, length = received.shape[0], own.shape[0]
    return pl.pallas_call(
        functools.partial(gradient_kernel, heads, blocks),
        out_shape=jax.ShapeDtypeStruct((count, heads * DI + lanes), bf16),
        in_specs=[in_smem()] * 2 + [in_vmem()] * 8,
        out_specs=in_vmem(),
        scratch_shapes=[
            pltpu.VMEM((2, count, length), f32),
            pltpu.VMEM((heads * count, lanes), f32),
        ],
        compiler_params=params(),
        cost_estimate=pl.CostEstimate(
            flops=8 * count * heads * DI * length,
            bytes_accessed=4 * (2 * received.size + 6 * count * length) + 4 * length * DI,
            transcendentals=4 * count * length,
        ),
        name="gradient",
    )(info, positions, received, here, own, other, part, far, target_own, target_other)


def outer_kernel(parts, blocks, at, info, latents, hiddens, *refs):
    bodies, tails = refs[:parts], refs[parts : 2 * parts]
    grad, grad_mixed, rows, tail_rows = refs[2 * parts :]
    count = bodies[0].shape[1]
    for k in range(parts):
        for t in range(blocks):
            to = pl.ds(pl.multiple_of(info[at + k * blocks + t] * count, count), count)
            rows[to, :] = bodies[k][t]

    grad[...] = times(latents[...], rows[...], 1, 0)

    @pl.when(pl.program_id(0) == 0)
    def _():
        for k in range(parts):
            for t in range(blocks):
                to = pl.ds(pl.multiple_of(info[at + k * blocks + t] * count, count), count)
                tail_rows[to, :] = tails[k][t]
        mixed = times(tail_rows[...], hiddens[...], 0, 0)
        grad_mixed[...] = mixed[: grad_mixed.shape[0]]


def outer(heads, at, info, latents, hiddens, parts):
    blocks, count, _ = parts[0].shape
    row_count, total = latents.shape
    width = heads * DI
    span = 512
    hidden_count = hiddens.shape[1]
    body = [pl.BlockSpec((blocks, count, span), lambda i: (0, 0, i)) for _ in parts]
    tail = [
        pl.BlockSpec((blocks, count, lanes), lambda i: (0, 0, width // lanes)) for _ in parts
    ]
    return pl.pallas_call(
        functools.partial(outer_kernel, len(parts), blocks, at),
        grid=(width // span,),
        out_shape=(
            jax.ShapeDtypeStruct((row_count, width), f32),
            jax.ShapeDtypeStruct((heads, hidden_count), f32),
        ),
        in_specs=[
            in_smem(),
            pl.BlockSpec((row_count, total), lambda i: (0, 0)),
            pl.BlockSpec((total, hidden_count), lambda i: (0, 0)),
        ]
        + body
        + tail,
        out_specs=(
            pl.BlockSpec((row_count, span), lambda i: (0, i)),
            pl.BlockSpec((heads, hidden_count), lambda i: (0, 0)),
        ),
        scratch_shapes=[pltpu.VMEM((total, span), bf16), pltpu.VMEM((total, lanes), bf16)],
        compiler_params=params(),
        cost_estimate=pl.CostEstimate(
            flops=2 * total * row_count * width,
            bytes_accessed=4 * row_count * width + 2 * total * width,
            transcendentals=0,
        ),
        name="outer",
    )(info, latents, hiddens, *parts, *parts)


def per_device(
    q_latent, hidden, main_queries, main_keys, index_keys, positions, w_query, w_weights
):
    n = lax.axis_size("ctx")
    z = lax.axis_index("ctx")
    head_size = lax.axis_size("head")
    y = lax.axis_index("head")
    dp_size = lax.axis_size("dp")
    dp = lax.axis_index("dp")
    ring = folded_ring(n)
    rows = main_keys.shape[1]
    half = rows // head_size
    rows_latent = w_query.shape[0]
    heads_here = w_weights.shape[1]
    width = heads_here * DI
    queries_here = main_queries.shape[1]
    sequence_positions = positions[0]

    def onward(x, t=1):
        return lax.ppermute(x, "ctx", [(ring[k], ring[(k + t) % n]) for k in range(n)])

    def swap_head(x):
        return lax.ppermute(x, "head", [(0, 1), (1, 0)])

    def swap_dp(x, bit):
        return lax.ppermute(x, "dp", [(k, k ^ bit) for k in range(dp_size)])

    def over_dp(x):
        gathered, bit = [x], dp_size // 2
        while bit:
            gathered, bit = gathered + [swap_dp(one, bit) for one in gathered], bit // 2
        return gathered

    table = jnp.array(device_table(n, head_size, dp_size, rows))
    info = lax.dynamic_index_in_dim(table, (z * head_size + y) * dp_size + dp, 0, False)

    keys_mine = [lax.dynamic_slice_in_dim(main_keys[0].T, y * half, half, 1)]
    keys_mine.append(onward(keys_mine[0]))
    queries = main_queries[0]
    other_queries = swap_head(queries)
    index_part = lax.dynamic_slice_in_dim(index_keys[0], y * half, half)
    index_own = jnp.concatenate([index_part] + [onward(index_part, t) for t in range(1, n)])
    index_other = swap_head(index_own)
    parts, kept = project(
        info, queries_here, q_latent[0], w_query, hidden[0], w_weights.T
    )
    received = onward(parts[0])
    weights, tops, before = [], [], None

    def score_next(keys):
        nonlocal before
        t = len(weights)
        numer, top, *before = score(
            t, n, info, sequence_positions, queries, other_queries, keys, before
        )
        weights.append(numer)
        tops.append(top)

    for t in range(1, n - 1):
        summed = received + parts[t]
        if t == 2:
            score_next(keys_mine[0])
            keys, summed, before = lax.optimization_barrier((keys_mine[t], summed, before))
        else:
            keys, summed = lax.optimization_barrier((keys_mine[t], summed))
        keys_mine[t] = keys
        keys_mine.append(onward(keys))
        received = onward(summed)
    while len(weights) < n - 1:
        score_next(keys_mine[len(weights)])

    part = make_logits(heads_here, received, parts[n - 1], index_own, index_other)
    far = swap_head(part)
    latents = jnp.stack(over_dp(kept))
    from_dp = info[1 + 3 * n + n * dp_size :]
    latents = jnp.concatenate([latents[from_dp[b]] for b in range(dp_size)])
    latents, hiddens = latents[:, :rows_latent].T, latents[:, rows_latent:]

    score_next(keys_mine[n - 1])
    far_top, far_mass = swap_head(jnp.stack(before))
    target_own = make_target(weights, tops, *before, far_top, far_mass)
    target_other = swap_head(target_own)
    piece = gradients(
        heads_here,
        n,
        info,
        sequence_positions,
        received,
        parts[n - 1],
        index_own,
        index_other,
        part,
        far,
        target_own,
        target_other,
    )

    pieces = [piece]
    for t in range(1, n):
        pairs = [(k, (k + t) % n) for k in range(n)]
        pieces.append(lax.ppermute(piece, "ctx", pairs))
    sequence = jnp.stack(pieces)
    gathered = over_dp(sequence)
    order_at = 1 + 3 * n
    if queries_here % 16:
        flat = jnp.concatenate(gathered)
        order = jnp.argsort(info[order_at : order_at + n * dp_size])
        outer_info = jnp.zeros((1,), jnp.int32)
        gathered = [flat[order].reshape(1, -1, flat.shape[2])]
        order_at = 0
    else:
        outer_info = info
    grad_query, grad_weights = outer(
        heads_here, order_at, outer_info, latents, hiddens, gathered
    )
    low = sequence[:, :, width + heads_here : width + heads_here + 2].astype(f32)
    low = low[:, :, 0] + low[:, :, 1]
    steps = lax.rem(z - jnp.arange(n, dtype=jnp.int32) + n, n)
    losses = jnp.concatenate([low[steps[k]] for k in range(n)])
    return (grad_query, grad_weights.T, losses[None, :])


def solution(mesh):
    return jax.shard_map(
        per_device,
        mesh=mesh,
        in_specs=(
            P("dp", None, None),
            P("dp", None, None),
            P("dp", "ctx", "head", None),
            P("dp", "ctx", None),
            P("dp", "ctx", None),
            P("dp", None),
            P("ctx", "head"),
            P("ctx", "head"),
        ),
        out_specs=(P("ctx", "head"), P("ctx", "head"), P("dp", None)),
        check_vma=False,
    )
```

```python
import functools
import math

import jax
import jax.numpy as jnp
import numpy as np
from jax import lax
from jax.experimental import pallas as pl
from jax.experimental.pallas import tpu as pltpu
from jax.sharding import PartitionSpec as P

HI = 64
DI = 128
HM = 128

index_scale = (HI * DI) ** (-0.5)
exponent_scale = 192.0 ** (-0.5) / math.log(2.0)
masked_floor = -1e30
lanes = 128
f32 = jnp.float32
bf16 = jnp.bfloat16
vmem_limit = 24 * 2**20


def folded_ring(size):
    return [0] + list(range(1, size, 2)) + list(range(2, size, 2))[::-1]


def params():
    return pltpu.CompilerParams(vmem_limit_bytes=vmem_limit)


def in_smem():
    return pl.BlockSpec(memory_space=pltpu.SMEM)


def in_vmem():
    return pl.BlockSpec(memory_space=pltpu.VMEM)


def times(a, b, axis_a, axis_b):
    return lax.dot_general(a, b, (((axis_a,), (axis_b,)), ((), ())), preferred_element_type=f32)


def device_table(n, heads, dp_size, rows):
    ring = folded_ring(n)
    half = rows // heads
    flips = dp_flips(dp_size)
    table = []
    for z in range(n):
        place = ring.index(z)
        behind = [ring[(place - t) % n] for t in range(n)]
        for y in range(heads):
            for dp in range(dp_size):
                row = [z] + [ring[(place - 1 - t) % n] for t in range(n)]
                row += [k * rows + y * half for k in behind]
                row += [k * rows + (1 - y) * half for k in behind]
                row += [(dp ^ k) * n + (z - t) % n for k in flips for t in range(n)]
                row += [dp ^ k for k in flips]
                table.append(row)
    return np.array(table, np.int32)


def dp_flips(dp_size):
    flips, bit = [0], dp_size // 2
    while bit:
        flips, bit = flips + [k ^ bit for k in flips], bit // 2
    return flips


def project_kernel(aligned, info, latent, weight, hidden, hidden_weight, *outs):
    *parts, kept = outs
    width = weight.shape[1]
    heads = hidden_weight.shape[0]
    count = parts[0].shape[0]
    if aligned:
        starts = [pl.multiple_of(info[1 + k] * count, count) for k in range(len(parts))]
        rows = jnp.concatenate([latent[pl.ds(k, count), :] for k in starts], axis=0)
        mixed_rows = jnp.concatenate([hidden[pl.ds(k, count), :] for k in starts], axis=0)
    else:
        rows, mixed_rows = latent[...], hidden[...]
    for at in range(0, width, 512):
        product = times(rows, weight[:, at : at + 512], 1, 0)
        for k, out in enumerate(parts):
            out[:, at : at + 512] = product[k * count : (k + 1) * count]
    mixed = times(mixed_rows, hidden_weight[...], 1, 1)
    for k, out in enumerate(parts):
        out[:, width : width + heads] = mixed[k * count : (k + 1) * count]
        out[:, width + heads :] = jnp.zeros((count, lanes - heads), f32)
    kept[:, : latent.shape[1]] = latent[...]
    kept[:, latent.shape[1] :] = hidden[...]


def project(info, count, latent, weight, hidden, hidden_weight):
    queries, width = latent.shape[0], weight.shape[1]
    depth, hidden_depth = weight.shape[0], hidden_weight.shape[1]
    blocks = queries // count
    aligned = count % 16 == 0 and depth % lanes == 0 and hidden_depth % lanes == 0
    columns = lambda i, info: (0, info[0])
    whole = lambda i, info: (0, 0)
    kept = None
    if not aligned:
        latent = lax.dynamic_slice_in_dim(latent, info[0] * depth, depth, 1)
        hidden = lax.dynamic_slice_in_dim(hidden, info[0] * hidden_depth, hidden_depth, 1)
        kept = jnp.concatenate([latent, hidden], axis=1)
        order = info[1 : 1 + blocks]
        latent = latent.reshape(blocks, count, depth)[order].reshape(queries, depth)
        hidden = hidden.reshape(blocks, count, hidden_depth)[order].reshape(queries, hidden_depth)
        columns = whole
    *parts, kept_here = pl.pallas_call(
        functools.partial(project_kernel, aligned),
        grid_spec=pltpu.PrefetchScalarGridSpec(
            num_scalar_prefetch=1,
            grid=(1,),
            in_specs=[
                pl.BlockSpec((queries, depth), columns),
                pl.BlockSpec((depth, width), whole),
                pl.BlockSpec((queries, hidden_depth), columns),
                pl.BlockSpec(hidden_weight.shape, whole),
            ],
            out_specs=[pl.BlockSpec((count, width + lanes), whole)] * blocks
            + [pl.BlockSpec((queries, depth + hidden_depth), whole)],
        ),
        out_shape=[jax.ShapeDtypeStruct((count, width + lanes), f32)] * blocks
        + [jax.ShapeDtypeStruct((queries, depth + hidden_depth), bf16)],
        compiler_params=params(),
        cost_estimate=pl.CostEstimate(
            flops=2 * queries * weight.size, bytes_accessed=2 * weight.size, transcendentals=0
        ),
        name="project",
    )(info, latent, weight, hidden, hidden_weight)
    return parts, kept_here if aligned else kept


def score_kernel(
    t, base_at, info, positions, mine, other, keys, top_before, mass_before, weights, top, top_all, mass_all, mass
):
    count, heads, depth = mine.shape
    limits = [positions[info[0] * count + q] - info[base_at] for q in range(count)]
    span = keys.shape[1]
    key_at = lax.broadcasted_iota(jnp.int32, (1, span), 1)
    row_at = lax.broadcasted_iota(jnp.int32, (heads, lanes), 0)
    lane_at = lax.broadcasted_iota(jnp.int32, (heads, lanes), 1)
    group = min(8, count)
    for at in range(0, count, group):
        for source, offset in ((mine, 0), (other, heads)):
            rows = source[at : at + group].reshape(group * heads, depth)
            scores = times(rows, keys[...], 1, 0)
            diagonal = lane_at == row_at + offset
            blocks = [scores[k * heads : (k + 1) * heads] for k in range(group)]
            seen = [key_at <= limits[at + k] for k in range(group)]
            blocks = [jnp.where(seen[k], blocks[k], masked_floor) for k in range(group)]
            highs = [jnp.max(one, axis=1, keepdims=True) for one in blocks]
            totals = []
            for k in range(group):
                shifted = jnp.exp2((blocks[k] - highs[k]) * exponent_scale)
                weights[at + k, offset : offset + heads] = shifted.astype(bf16)
                totals.append(jnp.sum(shifted, axis=1, keepdims=True))
            for k in range(group):
                q = at + k
                high_row = jnp.sum(jnp.where(diagonal, highs[k], 0.0), axis=0, keepdims=True)
                total_row = jnp.sum(jnp.where(diagonal, totals[k], 0.0), axis=0, keepdims=True)
                if offset == 0:
                    top[q : q + 1, :] = high_row
                    mass[q : q + 1, :] = total_row
                else:
                    top[q : q + 1, :] += high_row
                    mass[q : q + 1, :] += total_row
    if t == 0:
        top_all[...] = top[...]
        mass_all[...] = mass[...]
    else:
        before, now = top_before[...], top[...]
        joint = jnp.maximum(before, now)
        top_all[...] = joint
        mass_all[...] = mass_before[...] * jnp.exp2((before - joint) * exponent_scale) + mass[
            ...
        ] * jnp.exp2((now - joint) * exponent_scale)


def score(t, n, info, positions, mine, other, keys, before):
    count, heads, depth = mine.shape
    span = keys.shape[1]
    stats = jax.ShapeDtypeStruct((count, lanes), f32)
    if before is None:
        before = (jnp.zeros((count, lanes), f32),) * 2
    return pl.pallas_call(
        functools.partial(score_kernel, t, 1 + n + t),
        out_shape=(jax.ShapeDtypeStruct((count, 2 * heads, span), bf16), stats, stats, stats),
        in_specs=[in_smem()] * 2 + [in_vmem()] * 5,
        out_specs=(in_vmem(),) * 4,
        scratch_shapes=[pltpu.VMEM((count, lanes), f32)],
        compiler_params=params(),
        cost_estimate=pl.CostEstimate(
            flops=4 * count * heads * depth * span,
            bytes_accessed=2 * (2 * mine.size + keys.size + 2 * count * heads * span),
            transcendentals=2 * count * heads * span,
        ),
        name="score",
    )(info, positions, mine, other, keys, *before)


def target_kernel(blocks, *refs):
    weights, tops = refs[:blocks], refs[blocks : 2 * blocks]
    top, mass, far, out, held = refs[2 * blocks :]
    count, heads, span = weights[0].shape
    far_top = pltpu.roll(far[0], heads // 2, 1)
    far_mass = pltpu.roll(far[1], heads // 2, 1)
    joint = jnp.maximum(top[...], far_top)
    total = mass[...] * jnp.exp2((top[...] - joint) * exponent_scale) + far_mass * jnp.exp2(
        (far_top - joint) * exponent_scale
    )
    row_at = lax.broadcasted_iota(jnp.int32, (heads, lanes), 0)
    lane_at = lax.broadcasted_iota(jnp.int32, (heads, lanes), 1)
    diagonal = row_at == lane_at
    inverse = 1.0 / (total * HM)
    for t in range(blocks):
        factor = jnp.exp2((tops[t][...] - joint) * exponent_scale) * inverse
        for q in range(count):
            column = jnp.sum(
                jnp.where(diagonal, factor[q : q + 1, :], 0.0), axis=1, keepdims=True
            )
            mixed = weights[t][q].astype(f32) * column
            held[q : q + 1, t * span : (t + 1) * span] = jnp.sum(mixed, axis=0, keepdims=True)
    out[...] = held[...].astype(bf16)


def make_target(weights, tops, top, mass, far):
    blocks = len(weights)
    count, heads, span = weights[0].shape
    return pl.pallas_call(
        functools.partial(target_kernel, blocks),
        out_shape=jax.ShapeDtypeStruct((count, blocks * span), bf16),
        in_specs=[in_vmem()] * (2 * blocks + 3),
        out_specs=in_vmem(),
        scratch_shapes=[pltpu.VMEM((count, blocks * span), f32)],
        compiler_params=params(),
        cost_estimate=pl.CostEstimate(
            flops=2 * blocks * count * heads * span,
            bytes_accessed=2 * blocks * count * heads * span,
            transcendentals=0,
        ),
        name="target",
    )(*weights, *tops, top, mass, far)


def query_rows(total, heads):
    return jnp.concatenate(
        [total[:, j * DI : (j + 1) * DI].astype(bf16) for j in range(heads)], axis=0
    )


def logits_kernel(heads, received, here, own, other, out):
    count = received.shape[0]
    total = received[...] + here[...]
    query = query_rows(total, heads)
    columns = [total[:, heads * DI + j : heads * DI + j + 1] for j in range(heads)]
    span = 512
    for part, keys in enumerate((own, other)):
        for at in range(0, keys.shape[0], span):
            affinity = times(query, keys[at : at + span, :], 1, 1)
            running = jnp.zeros((count, span), f32)
            for j in range(heads):
                reached = jnp.maximum(affinity[j * count : (j + 1) * count], 0.0)
                running = running + columns[j] * reached
            out[part, :, at : at + span] = running * index_scale


def make_logits(heads, received, here, own, other):
    count, length = received.shape[0], own.shape[0]
    return pl.pallas_call(
        functools.partial(logits_kernel, heads),
        out_shape=jax.ShapeDtypeStruct((2, count, length), f32),
        in_specs=[in_vmem()] * 4,
        out_specs=in_vmem(),
        compiler_params=params(),
        cost_estimate=pl.CostEstimate(
            flops=4 * count * heads * DI * length,
            bytes_accessed=4 * (2 * received.size + 2 * count * length) + 4 * length * DI,
            transcendentals=0,
        ),
        name="logits",
    )(received, here, own, other)


def gradient_kernel(
    heads, blocks, info, positions, received, here, own, other, part, far, target_own, target_other, out, logit, flow
):
    count = received.shape[0]
    total = received[...] + here[...]
    span = own.shape[0] // blocks
    query = query_rows(total, heads)
    row_at = lax.broadcasted_iota(jnp.int32, (count, lanes), 0)
    position = jnp.zeros((count, lanes), jnp.int32)
    for q in range(count):
        position = jnp.where(row_at == q, positions[info[0] * count + q], position)
    position = position[:, 0:1]
    key_at = lax.broadcasted_iota(jnp.int32, (count, span), 1)
    sides = ((own, target_own), (other, target_other))

    def seen(side, t):
        return key_at + info[1 + (1 + side) * blocks + t] <= position

    highs = []
    for side in range(2):
        high = jnp.full((count, span), masked_floor, f32)
        for t in range(blocks):
            at = slice(t * span, (t + 1) * span)
            value = part[side, :, at] + far[1 - side, :, at]
            logit[side, :, at] = value
            high = jnp.maximum(high, jnp.where(seen(side, t), value, masked_floor))
        highs.append(jnp.max(high, axis=1, keepdims=True))
    high = jnp.maximum(highs[0], highs[1])
    sums = []
    for side in range(2):
        running = jnp.zeros((count, span), f32)
        for t in range(blocks):
            at = slice(t * span, (t + 1) * span)
            grown = jnp.exp(logit[side, :, at] - high)
            running = running + jnp.where(seen(side, t), grown, 0.0)
        sums.append(jnp.sum(running, axis=1, keepdims=True))
    mass = sums[0] + sums[1]
    level = high + jnp.log(mass)
    inverse = 1.0 / mass
    columns = [
        total[:, heads * DI + j : heads * DI + j + 1] * index_scale for j in range(heads)
    ]
    losses = []
    query_sum = jnp.zeros((heads * count, DI), f32)
    flow[...] = jnp.zeros(flow.shape, f32)
    for side, (keys, target) in enumerate(sides):
        running = jnp.zeros((count, span), f32)
        for t in range(blocks):
            at = slice(t * span, (t + 1) * span)
            visible = seen(side, t)
            value = logit[side, :, at]
            wanted = target[:, at].astype(f32)
            running = running + jnp.where(visible, wanted * (value - level), 0.0)
            grown = jnp.exp(value - high) * inverse
            delta = jnp.where(visible, grown - wanted, 0.0)
            affinity = times(query, keys[at, :], 1, 1)
            grads = []
            for j in range(heads):
                rows = slice(j * count, (j + 1) * count)
                one = affinity[rows]
                reached = jnp.where(one > 0, delta, 0.0)
                grads.append((reached * columns[j]).astype(bf16))
                product = reached * one
                folded = product[:, :lanes]
                for k in range(lanes, span, lanes):
                    folded = folded + product[:, k : k + lanes]
                flow[rows, :] += folded
            query_sum = query_sum + times(jnp.concatenate(grads, axis=0), keys[at, :], 1, 0)
        losses.append(jnp.sum(running, axis=1, keepdims=True))
    loss = -(losses[0] + losses[1])
    lane_at = lax.broadcasted_iota(jnp.int32, (count, lanes), 1)
    tail = jnp.zeros((count, lanes), f32)
    for j in range(heads):
        rows = slice(j * count, (j + 1) * count)
        out[:, j * DI : (j + 1) * DI] = query_sum[rows].astype(bf16)
        column = jnp.sum(flow[rows, :], axis=1, keepdims=True) * index_scale
        tail = jnp.where(lane_at == j, column, tail)
    loss_high = loss.astype(bf16).astype(f32)
    tail = jnp.where(lane_at == heads, loss_high, tail)
    tail = jnp.where(lane_at == heads + 1, loss - loss_high, tail)
    out[:, heads * DI :] = tail.astype(bf16)


def gradients(heads, blocks, info, positions, received, here, own, other, part, far, target_own, target_other):
    count, length = received.shape[0], own.shape[0]
    return pl.pallas_call(
        functools.partial(gradient_kernel, heads, blocks),
        out_shape=jax.ShapeDtypeStruct((count, heads * DI + lanes), bf16),
        in_specs=[in_smem()] * 2 + [in_vmem()] * 8,
        out_specs=in_vmem(),
        scratch_shapes=[
            pltpu.VMEM((2, count, length), f32),
            pltpu.VMEM((heads * count, lanes), f32),
        ],
        compiler_params=params(),
        cost_estimate=pl.CostEstimate(
            flops=8 * count * heads * DI * length,
            bytes_accessed=4 * (2 * received.size + 6 * count * length) + 4 * length * DI,
            transcendentals=4 * count * length,
        ),
        name="gradient",
    )(info, positions, received, here, own, other, part, far, target_own, target_other)


def arrange_kernel(at, info, *refs):
    kept, (latents, hiddens, held) = refs[:-3], refs[-3:]
    queries, depth = kept[0].shape[0], latents.shape[0]
    for k, one in enumerate(kept):
        to = pl.ds(pl.multiple_of(info[at + k] * queries, queries), queries)
        held[to, :] = one[:, :depth].astype(f32)
        hiddens[to, :] = one[:, depth:]
    latents[...] = held[...].T.astype(bf16)


def arrange(at, info, depth, kept):
    queries, width = kept[0].shape
    total = queries * len(kept)
    return pl.pallas_call(
        functools.partial(arrange_kernel, at),
        out_shape=(
            jax.ShapeDtypeStruct((depth, total), bf16),
            jax.ShapeDtypeStruct((total, width - depth), bf16),
        ),
        in_specs=[in_smem()] + [in_vmem()] * len(kept),
        out_specs=(in_vmem(),) * 2,
        scratch_shapes=[pltpu.VMEM((total, depth), f32)],
        compiler_params=params(),
        cost_estimate=pl.CostEstimate(
            flops=0, bytes_accessed=4 * total * width, transcendentals=0
        ),
        name="arrange",
    )(info, *kept)


def outer_kernel(heads, order, dp_at, info, latents, hiddens, *refs):
    parts, (grad, grad_mixed, losses, rows) = refs[:-4], refs[-4:]
    count = parts[0].shape[-2]
    width = heads * DI
    span = grad.shape[1]
    step = pl.program_id(0)

    @pl.when(step == 0)
    def _():
        k = 0
        for part in parts:
            for t in range(part.shape[0]):
                to = 0 if order is None else pl.multiple_of(info[order[k]] * count, count)
                rows[pl.ds(to, count), :] = part[t]
                k += 1
        tails = rows[:, width:]
        grad_mixed[...] = times(tails, hiddens[...], 0, 0)[:heads]
        own = losses.shape[1]
        from_own = rows[pl.ds(pl.multiple_of(info[dp_at] * own, own), own), width:].astype(f32)
        column = from_own[:, heads : heads + 1] + from_own[:, heads + 1 : heads + 2]
        diagonal = lax.broadcasted_iota(jnp.int32, (own, own), 0) == lax.broadcasted_iota(
            jnp.int32, (own, own), 1
        )
        losses[...] = jnp.sum(jnp.where(diagonal, column, 0.0), axis=0, keepdims=True)

    at = pl.ds(pl.multiple_of(step * span, span), span)
    grad[...] = times(latents[...], rows[:, at], 1, 0)


def outer(heads, order, dp_at, queries, info, latents, hiddens, parts):
    row_count, total = latents.shape
    width = heads * DI
    span = 512
    hidden_count = hiddens.shape[1]
    return pl.pallas_call(
        functools.partial(outer_kernel, heads, order, dp_at),
        grid=(width // span,),
        out_shape=(
            jax.ShapeDtypeStruct((row_count, width), f32),
            jax.ShapeDtypeStruct((heads, hidden_count), f32),
            jax.ShapeDtypeStruct((1, queries), f32),
        ),
        in_specs=[in_smem()] + [in_vmem()] * (2 + len(parts)),
        out_specs=(
            pl.BlockSpec((row_count, span), lambda i: (0, i)),
            pl.BlockSpec((heads, hidden_count), lambda i: (0, 0)),
            pl.BlockSpec((1, queries), lambda i: (0, 0)),
        ),
        scratch_shapes=[pltpu.VMEM((total, width + lanes), bf16)],
        compiler_params=params(),
        cost_estimate=pl.CostEstimate(
            flops=2 * total * row_count * width,
            bytes_accessed=4 * row_count * width + 2 * total * width,
            transcendentals=0,
        ),
        name="outer",
    )(info, latents, hiddens, *parts)


def per_device(
    q_latent, hidden, main_queries, main_keys, index_keys, positions, w_query, w_weights
):
    n = lax.axis_size("ctx")
    z = lax.axis_index("ctx")
    head_size = lax.axis_size("head")
    y = lax.axis_index("head")
    dp_size = lax.axis_size("dp")
    dp = lax.axis_index("dp")
    ring = folded_ring(n)
    rows = main_keys.shape[1]
    half = rows // head_size
    rows_latent = w_query.shape[0]
    heads_here = w_weights.shape[1]
    queries_here = main_queries.shape[1]
    sequence_positions = positions[0]

    def onward(x, t=1):
        return lax.ppermute(x, "ctx", [(ring[k], ring[(k + t) % n]) for k in range(n)])

    def swap_head(x):
        return lax.ppermute(x, "head", [(0, 1), (1, 0)])

    def swap_dp(x, bit):
        return lax.ppermute(x, "dp", [(k, k ^ bit) for k in range(dp_size)])

    def over_dp(x):
        gathered, bit = [x], dp_size // 2
        while bit:
            gathered, bit = gathered + [swap_dp(one, bit) for one in gathered], bit // 2
        return gathered

    table = jnp.array(device_table(n, head_size, dp_size, rows))
    info = lax.dynamic_index_in_dim(table, (z * head_size + y) * dp_size + dp, 0, False)

    keys_mine = [lax.dynamic_slice_in_dim(main_keys[0].T, y * half, half, 1)]
    keys_mine.append(onward(keys_mine[0]))
    queries = main_queries[0]
    other_queries = swap_head(queries)
    index_part = lax.dynamic_slice_in_dim(index_keys[0], y * half, half)
    index_own = jnp.concatenate([index_part] + [onward(index_part, t) for t in range(1, n)])
    parts, kept = project(
        info, queries_here, q_latent[0], w_query, hidden[0], w_weights.T
    )
    received = onward(parts[0])
    weights, tops, before = [], [], None

    def score_next(keys):
        nonlocal before
        t = len(weights)
        numer, top, *before = score(
            t, n, info, sequence_positions, queries, other_queries, keys, before
        )
        weights.append(numer)
        tops.append(top)

    for t in range(1, n - 1):
        summed = received + parts[t]
        if t == 1:
            keys, summed, index_own = lax.optimization_barrier((keys_mine[t], summed, index_own))
            index_other = swap_head(index_own)
        else:
            keys, summed = lax.optimization_barrier((keys_mine[t], summed))
        keys_mine[t] = keys
        keys_mine.append(onward(keys))
        received = onward(summed)
    while len(weights) < n - 1:
        score_next(keys_mine[len(weights)])

    part = make_logits(heads_here, received, parts[n - 1], index_own, index_other)
    far = swap_head(part)
    order_at = 1 + 3 * n
    dp_at = order_at + n * dp_size
    latents, hiddens = arrange(dp_at, info, rows_latent, over_dp(kept))

    score_next(keys_mine[n - 1])
    target_own = make_target(weights, tops, *before, swap_head(jnp.stack(before)))
    target_other = swap_head(target_own)
    piece = gradients(
        heads_here,
        n,
        info,
        sequence_positions,
        received,
        parts[n - 1],
        index_own,
        index_other,
        part,
        far,
        target_own,
        target_other,
    )[None]

    brought = []
    for t in range(1, n):
        pairs = [(k, (k + t) % n) for k in range(n)]
        brought.append(lax.ppermute(piece, "ctx", pairs))
    own_pieces = over_dp(piece)
    brought = over_dp(jnp.concatenate(brought))
    if queries_here % 16:
        flat = jnp.concatenate([jnp.concatenate([a, b]) for a, b in zip(own_pieces, brought)])
        order = jnp.argsort(info[order_at : order_at + n * dp_size])
        parts_in, order = [flat[order].reshape(1, -1, flat.shape[2])], None
    else:
        parts_in, order = own_pieces + brought, []
        order += [order_at + k * n for k in range(dp_size)]
        order += [order_at + k * n + t for k in range(dp_size) for t in range(1, n)]
    grad_query, grad_weights, losses = outer(
        heads_here,
        order,
        dp_at,
        q_latent.shape[1],
        info,
        latents,
        hiddens,
        parts_in,
    )
    return (grad_query, grad_weights.T, losses)


def solution(mesh):
    return jax.shard_map(
        per_device,
        mesh=mesh,
        in_specs=(
            P("dp", None, None),
            P("dp", None, None),
            P("dp", "ctx", "head", None),
            P("dp", "ctx", None),
            P("dp", "ctx", None),
            P("dp", None),
            P("ctx", "head"),
            P("ctx", "head"),
        ),
        out_specs=(P("ctx", "head"), P("ctx", "head"), P("dp", None)),
        check_vma=False,
    )
```

```python
import functools
import math

import jax
import jax.numpy as jnp
import numpy as np
from jax import lax
from jax.experimental import pallas as pl
from jax.experimental.pallas import tpu as pltpu
from jax.sharding import PartitionSpec as P

HI = 64
DI = 128
HM = 128

index_scale = (HI * DI) ** (-0.5)
exponent_scale = 192.0 ** (-0.5) / math.log(2.0)
masked_floor = -1e30
lanes = 128
f32 = jnp.float32
bf16 = jnp.bfloat16
vmem_limit = 24 * 2**20
group_size = 4


def folded_ring(size):
    return [0] + list(range(1, size, 2)) + list(range(2, size, 2))[::-1]


def params():
    return pltpu.CompilerParams(vmem_limit_bytes=vmem_limit)


def in_smem():
    return pl.BlockSpec(memory_space=pltpu.SMEM)


def in_vmem():
    return pl.BlockSpec(memory_space=pltpu.VMEM)


def times(a, b, axis_a, axis_b):
    return lax.dot_general(a, b, (((axis_a,), (axis_b,)), ((), ())), preferred_element_type=f32)


def device_table(n, heads, dp_size, rows):
    ring = folded_ring(n)
    half = rows // heads
    flips = dp_flips(dp_size)
    table = []
    for z in range(n):
        place = ring.index(z)
        behind = [ring[(place - t) % n] for t in range(n)]
        for y in range(heads):
            for dp in range(dp_size):
                row = [z] + [ring[(place - 1 - t) % n] for t in range(n)]
                row += [k * rows + y * half for k in behind]
                row += [k * rows + (1 - y) * half for k in behind]
                row += [(dp ^ k) * n + (z - t) % n for k in flips for t in range(n)]
                row += [dp ^ k for k in flips]
                table.append(row)
    return np.array(table, np.int32)


def dp_flips(dp_size):
    flips, bit = [0], dp_size // 2
    while bit:
        flips, bit = flips + [k ^ bit for k in flips], bit // 2
    return flips


def project_kernel(aligned, info, latent, weight, hidden, hidden_weight, *outs):
    *parts, kept = outs
    width = weight.shape[1]
    heads = hidden_weight.shape[0]
    count = parts[0].shape[0]
    if aligned:
        starts = [pl.multiple_of(info[1 + k] * count, count) for k in range(len(parts))]
        rows = jnp.concatenate([latent[pl.ds(k, count), :] for k in starts], axis=0)
        mixed_rows = jnp.concatenate([hidden[pl.ds(k, count), :] for k in starts], axis=0)
    else:
        rows, mixed_rows = latent[...], hidden[...]
    for at in range(0, width, 512):
        product = times(rows, weight[:, at : at + 512], 1, 0)
        for k, out in enumerate(parts):
            out[:, at : at + 512] = product[k * count : (k + 1) * count]
    mixed = times(mixed_rows, hidden_weight[...], 1, 1)
    for k, out in enumerate(parts):
        out[:, width : width + heads] = mixed[k * count : (k + 1) * count]
        out[:, width + heads :] = jnp.zeros((count, lanes - heads), f32)
    kept[:, : latent.shape[1]] = latent[...]
    kept[:, latent.shape[1] :] = hidden[...]


def project(info, count, latent, weight, hidden, hidden_weight):
    queries, width = latent.shape[0], weight.shape[1]
    depth, hidden_depth = weight.shape[0], hidden_weight.shape[1]
    blocks = queries // count
    aligned = count % 16 == 0 and depth % lanes == 0 and hidden_depth % lanes == 0
    columns = lambda i, info: (0, info[0])
    whole = lambda i, info: (0, 0)
    kept = None
    if not aligned:
        latent = lax.dynamic_slice_in_dim(latent, info[0] * depth, depth, 1)
        hidden = lax.dynamic_slice_in_dim(hidden, info[0] * hidden_depth, hidden_depth, 1)
        kept = jnp.concatenate([latent, hidden], axis=1)
        order = info[1 : 1 + blocks]
        latent = latent.reshape(blocks, count, depth)[order].reshape(queries, depth)
        hidden = hidden.reshape(blocks, count, hidden_depth)[order].reshape(queries, hidden_depth)
        columns = whole
    *parts, kept_here = pl.pallas_call(
        functools.partial(project_kernel, aligned),
        grid_spec=pltpu.PrefetchScalarGridSpec(
            num_scalar_prefetch=1,
            grid=(1,),
            in_specs=[
                pl.BlockSpec((queries, depth), columns),
                pl.BlockSpec((depth, width), whole),
                pl.BlockSpec((queries, hidden_depth), columns),
                pl.BlockSpec(hidden_weight.shape, whole),
            ],
            out_specs=[pl.BlockSpec((count, width + lanes), whole)] * blocks
            + [pl.BlockSpec((queries, depth + hidden_depth), whole)],
        ),
        out_shape=[jax.ShapeDtypeStruct((count, width + lanes), f32)] * blocks
        + [jax.ShapeDtypeStruct((queries, depth + hidden_depth), bf16)],
        compiler_params=params(),
        cost_estimate=pl.CostEstimate(
            flops=2 * queries * weight.size, bytes_accessed=2 * weight.size, transcendentals=0
        ),
        name="project",
    )(info, latent, weight, hidden, hidden_weight)
    return parts, kept_here if aligned else kept


def score_kernel(
    t,
    base_at,
    info,
    positions,
    mine,
    other,
    keys,
    top_before,
    mass_before,
    weights,
    top,
    top_all,
    mass_all,
    mass,
    even,
    odd,
):
    count, heads, depth = mine.shape
    limits = [positions[info[0] * count + q] - info[base_at] for q in range(count)]
    span = keys.shape[1]
    key_at = lax.broadcasted_iota(jnp.int32, (1, span), 1)
    row_at = lax.broadcasted_iota(jnp.int32, (heads, lanes), 0)
    lane_at = lax.broadcasted_iota(jnp.int32, (heads, lanes), 1)
    group = min(group_size, count)
    work = [(at, k) for at in range(0, count, group) for k in range(2)]
    held = (even, odd)

    def multiply(step):
        at, k = work[step]
        rows = (mine, other)[k][at : at + group].reshape(group * heads, depth)
        held[step % 2][...] = times(rows, keys[...], 1, 0)

    multiply(0)
    for step, (at, k) in enumerate(work):
        if step + 1 < len(work):
            multiply(step + 1)
        scores = held[step % 2]
        offset = k * heads
        diagonal = lane_at == row_at + offset
        for i in range(group):
            q = at + i
            one = jnp.where(
                key_at <= limits[q], scores[i * heads : (i + 1) * heads, :], masked_floor
            )
            high = jnp.max(one, axis=1, keepdims=True)
            shifted = jnp.exp2((one - high) * exponent_scale)
            total = jnp.sum(shifted, axis=1, keepdims=True)
            weights[q, offset : offset + heads] = shifted.astype(bf16)
            high_row = jnp.sum(jnp.where(diagonal, high, 0.0), axis=0, keepdims=True)
            total_row = jnp.sum(jnp.where(diagonal, total, 0.0), axis=0, keepdims=True)
            if k == 0:
                top[q : q + 1, :] = high_row
                mass[q : q + 1, :] = total_row
            else:
                top[q : q + 1, :] += high_row
                mass[q : q + 1, :] += total_row
    if t == 0:
        top_all[...] = top[...]
        mass_all[...] = mass[...]
    else:
        before, now = top_before[...], top[...]
        joint = jnp.maximum(before, now)
        top_all[...] = joint
        mass_all[...] = mass_before[...] * jnp.exp2((before - joint) * exponent_scale) + mass[
            ...
        ] * jnp.exp2((now - joint) * exponent_scale)


def score(t, n, info, positions, mine, other, keys, before):
    count, heads, depth = mine.shape
    span = keys.shape[1]
    stats = jax.ShapeDtypeStruct((count, lanes), f32)
    if before is None:
        before = (jnp.zeros((count, lanes), f32),) * 2
    return pl.pallas_call(
        functools.partial(score_kernel, t, 1 + n + t),
        out_shape=(jax.ShapeDtypeStruct((count, 2 * heads, span), bf16), stats, stats, stats),
        in_specs=[in_smem()] * 2 + [in_vmem()] * 5,
        out_specs=(in_vmem(),) * 4,
        scratch_shapes=[pltpu.VMEM((count, lanes), f32)]
        + [pltpu.VMEM((min(group_size, count) * heads, span), f32)] * 2,
        compiler_params=params(),
        cost_estimate=pl.CostEstimate(
            flops=4 * count * heads * depth * span,
            bytes_accessed=2 * (2 * mine.size + keys.size + 2 * count * heads * span),
            transcendentals=2 * count * heads * span,
        ),
        name="score",
    )(info, positions, mine, other, keys, *before)


def delta_kernel(blocks, *refs):
    weights, tops = refs[:blocks], refs[blocks : 2 * blocks]
    top, mass, far, probs, out, sent, held = refs[2 * blocks :]
    count, heads, span = weights[0].shape
    far_top = pltpu.roll(far[0], heads // 2, 1)
    far_mass = pltpu.roll(far[1], heads // 2, 1)
    joint = jnp.maximum(top[...], far_top)
    total = mass[...] * jnp.exp2((top[...] - joint) * exponent_scale) + far_mass * jnp.exp2(
        (far_top - joint) * exponent_scale
    )
    row_at = lax.broadcasted_iota(jnp.int32, (heads, lanes), 0)
    lane_at = lax.broadcasted_iota(jnp.int32, (heads, lanes), 1)
    diagonal = row_at == lane_at
    inverse = 1.0 / (total * HM)
    for t in range(blocks):
        factor = jnp.exp2((tops[t][...] - joint) * exponent_scale) * inverse
        for q in range(count):
            column = jnp.sum(
                jnp.where(diagonal, factor[q : q + 1, :], 0.0), axis=1, keepdims=True
            )
            mixed = weights[t][q].astype(f32) * column
            held[q : q + 1, t * span : (t + 1) * span] = jnp.sum(mixed, axis=0, keepdims=True)
    delta = probs[0] - held[...]
    out[...] = delta
    sent[...] = delta.astype(bf16)


def make_delta(weights, tops, top, mass, far, probs):
    blocks = len(weights)
    count, heads, span = weights[0].shape
    return pl.pallas_call(
        functools.partial(delta_kernel, blocks),
        out_shape=(
            jax.ShapeDtypeStruct((count, blocks * span), f32),
            jax.ShapeDtypeStruct((count, blocks * span), bf16),
        ),
        in_specs=[in_vmem()] * (2 * blocks + 4),
        out_specs=(in_vmem(),) * 2,
        scratch_shapes=[pltpu.VMEM((count, blocks * span), f32)],
        compiler_params=params(),
        cost_estimate=pl.CostEstimate(
            flops=2 * blocks * count * heads * span,
            bytes_accessed=2 * blocks * count * heads * span,
            transcendentals=0,
        ),
        name="delta",
    )(*weights, *tops, top, mass, far, probs)


def query_rows(total, heads):
    return jnp.concatenate(
        [total[:, j * DI : (j + 1) * DI].astype(bf16) for j in range(heads)], axis=0
    )


def logits_kernel(heads, received, here, own, other, out):
    count = received.shape[0]
    total = received[...] + here[...]
    query = query_rows(total, heads)
    columns = [total[:, heads * DI + j : heads * DI + j + 1] for j in range(heads)]
    span = 512
    for part, keys in enumerate((own, other)):
        for at in range(0, keys.shape[0], span):
            affinity = times(query, keys[at : at + span, :], 1, 1)
            running = jnp.zeros((count, span), f32)
            for j in range(heads):
                reached = jnp.maximum(affinity[j * count : (j + 1) * count], 0.0)
                running = running + columns[j] * reached
            out[part, :, at : at + span] = running * index_scale


def make_logits(heads, received, here, own, other):
    count, length = received.shape[0], own.shape[0]
    return pl.pallas_call(
        functools.partial(logits_kernel, heads),
        out_shape=jax.ShapeDtypeStruct((2, count, length), f32),
        in_specs=[in_vmem()] * 4,
        out_specs=in_vmem(),
        compiler_params=params(),
        cost_estimate=pl.CostEstimate(
            flops=4 * count * heads * DI * length,
            bytes_accessed=4 * (2 * received.size + 2 * count * length) + 4 * length * DI,
            transcendentals=0,
        ),
        name="logits",
    )(received, here, own, other)


def softmax_kernel(blocks, info, positions, part, far, probs, log_probs):
    _, count, length = part.shape
    span = length // blocks
    row_at = lax.broadcasted_iota(jnp.int32, (count, lanes), 0)
    position = jnp.zeros((count, lanes), jnp.int32)
    for q in range(count):
        position = jnp.where(row_at == q, positions[info[0] * count + q], position)
    position = position[:, 0:1]
    key_at = lax.broadcasted_iota(jnp.int32, (count, span), 1)

    def seen(side, t):
        return key_at + info[1 + (1 + side) * blocks + t] <= position

    highs = []
    for side in range(2):
        high = jnp.full((count, span), masked_floor, f32)
        for t in range(blocks):
            at = slice(t * span, (t + 1) * span)
            value = part[side, :, at] + far[1 - side, :, at]
            log_probs[side, :, at] = value
            high = jnp.maximum(high, jnp.where(seen(side, t), value, masked_floor))
        highs.append(jnp.max(high, axis=1, keepdims=True))
    high = jnp.maximum(highs[0], highs[1])
    sums = []
    for side in range(2):
        running = jnp.zeros((count, span), f32)
        for t in range(blocks):
            at = slice(t * span, (t + 1) * span)
            grown = jnp.where(seen(side, t), jnp.exp(log_probs[side, :, at] - high), 0.0)
            probs[side, :, at] = grown
            running = running + grown
        sums.append(jnp.sum(running, axis=1, keepdims=True))
    mass = sums[0] + sums[1]
    level = high + jnp.log(mass)
    inverse = 1.0 / mass
    for side in range(2):
        for t in range(blocks):
            at = slice(t * span, (t + 1) * span)
            probs[side, :, at] = probs[side, :, at] * inverse
            log_probs[side, :, at] = jnp.where(seen(side, t), log_probs[side, :, at] - level, 0.0)


def make_softmax(blocks, info, positions, part, far):
    return pl.pallas_call(
        functools.partial(softmax_kernel, blocks),
        out_shape=(jax.ShapeDtypeStruct(part.shape, f32),) * 2,
        in_specs=[in_smem()] * 2 + [in_vmem()] * 2,
        out_specs=(in_vmem(),) * 2,
        compiler_params=params(),
        cost_estimate=pl.CostEstimate(
            flops=8 * part.size, bytes_accessed=16 * part.size, transcendentals=part.size
        ),
        name="softmax",
    )(info, positions, part, far)


def gradient_kernel(
    heads,
    blocks,
    received,
    here,
    own,
    other,
    probs,
    log_probs,
    delta_own,
    sent,
    brought,
    out,
    flow,
    query_sum,
    grads,
    even,
    odd,
):
    count = received.shape[0]
    total = received[...] + here[...]
    span = own.shape[0] // blocks
    query = query_rows(total, heads)
    columns = [
        total[:, heads * DI + j : heads * DI + j + 1] * index_scale for j in range(heads)
    ]
    work = [(side, t) for side in range(2) for t in range(blocks)]
    held = (even, odd)

    def multiply(step):
        side, t = work[step]
        keys = (own, other)[side][t * span : (t + 1) * span, :]
        held[step % 2][...] = times(query, keys, 1, 1)

    multiply(0)
    flow[...] = jnp.zeros(flow.shape, f32)
    running = [jnp.zeros((count, span), f32)] * 2
    for step, (side, t) in enumerate(work):
        if step + 1 < len(work):
            multiply(step + 1)
        at = slice(t * span, (t + 1) * span)
        affinity = held[step % 2]
        rounded = (sent, brought)[side][:, at].astype(f32)
        delta = delta_own[:, at] if side == 0 else rounded
        wanted = probs[side, :, at] - rounded
        running[side] = running[side] + wanted * log_probs[side, :, at]
        for j in range(heads):
            rows = slice(j * count, (j + 1) * count)
            one = affinity[rows, :]
            reached = jnp.where(one > 0, delta, 0.0)
            grads[rows, :] = (reached * columns[j]).astype(bf16)
            product = reached * one
            folded = product[:, :lanes]
            for k in range(lanes, span, lanes):
                folded = folded + product[:, k : k + lanes]
            flow[rows, :] += folded
        keys = (own, other)[side][at, :]
        product = times(grads[...], keys, 1, 0)
        if step == 0:
            query_sum[...] = product
        else:
            query_sum[...] += product
    losses = [jnp.sum(one, axis=1, keepdims=True) for one in running]
    loss = -(losses[0] + losses[1])
    lane_at = lax.broadcasted_iota(jnp.int32, (count, lanes), 1)
    tail = jnp.zeros((count, lanes), f32)
    for j in range(heads):
        rows = slice(j * count, (j + 1) * count)
        out[:, j * DI : (j + 1) * DI] = query_sum[rows, :].astype(bf16)
        column = jnp.sum(flow[rows, :], axis=1, keepdims=True) * index_scale
        tail = jnp.where(lane_at == j, column, tail)
    loss_high = loss.astype(bf16).astype(f32)
    tail = jnp.where(lane_at == heads, loss_high, tail)
    tail = jnp.where(lane_at == heads + 1, loss - loss_high, tail)
    out[:, heads * DI :] = tail.astype(bf16)


def gradients(heads, blocks, received, here, own, other, probs, log_probs, delta_own, sent, brought):
    count, length = received.shape[0], own.shape[0]
    span = length // blocks
    return pl.pallas_call(
        functools.partial(gradient_kernel, heads, blocks),
        out_shape=jax.ShapeDtypeStruct((count, heads * DI + lanes), bf16),
        in_specs=[in_vmem()] * 9,
        out_specs=in_vmem(),
        scratch_shapes=[
            pltpu.VMEM((heads * count, lanes), f32),
            pltpu.VMEM((heads * count, DI), f32),
            pltpu.VMEM((heads * count, span), bf16),
            pltpu.VMEM((heads * count, span), f32),
            pltpu.VMEM((heads * count, span), f32),
        ],
        compiler_params=params(),
        cost_estimate=pl.CostEstimate(
            flops=8 * count * heads * DI * length,
            bytes_accessed=4 * (2 * received.size + 6 * count * length) + 4 * length * DI,
            transcendentals=0,
        ),
        name="gradient",
    )(received, here, own, other, probs, log_probs, delta_own, sent, brought)


def arrange_kernel(at, info, *refs):
    kept, (latents, hiddens, held) = refs[:-3], refs[-3:]
    queries, depth = kept[0].shape[0], latents.shape[0]
    for k, one in enumerate(kept):
        to = pl.ds(pl.multiple_of(info[at + k] * queries, queries), queries)
        held[to, :] = one[:, :depth].astype(f32)
        hiddens[to, :] = one[:, depth:]
    latents[...] = held[...].T.astype(bf16)


def arrange(at, info, depth, kept):
    queries, width = kept[0].shape
    total = queries * len(kept)
    return pl.pallas_call(
        functools.partial(arrange_kernel, at),
        out_shape=(
            jax.ShapeDtypeStruct((depth, total), bf16),
            jax.ShapeDtypeStruct((total, width - depth), bf16),
        ),
        in_specs=[in_smem()] + [in_vmem()] * len(kept),
        out_specs=(in_vmem(),) * 2,
        scratch_shapes=[pltpu.VMEM((total, depth), f32)],
        compiler_params=params(),
        cost_estimate=pl.CostEstimate(
            flops=0, bytes_accessed=4 * total * width, transcendentals=0
        ),
        name="arrange",
    )(info, *kept)


def outer_kernel(heads, order, dp_at, info, latents, hiddens, *refs):
    parts, (grad, grad_mixed, losses, rows, blocks, sems) = refs[:-6], refs[-6:]
    count = parts[0].shape[-2]
    width = heads * DI
    steps, _, span = blocks.shape
    k = 0
    for part in parts:
        for t in range(part.shape[0]):
            to = 0 if order is None else pl.multiple_of(info[order[k]] * count, count)
            rows[pl.ds(to, count), :] = part[t]
            k += 1
    copies = []
    for i in range(steps):
        at = slice(i * span, (i + 1) * span)
        blocks[i] = times(latents[...], rows[:, at], 1, 0)
        copies.append(pltpu.make_async_copy(blocks.at[i], grad.at[:, at], sems.at[i]))
        copies[-1].start()
    tails = rows[:, width:]
    grad_mixed[...] = times(tails, hiddens[...], 0, 0)[:heads]
    own = losses.shape[1]
    from_own = rows[pl.ds(pl.multiple_of(info[dp_at] * own, own), own), width:].astype(f32)
    column = from_own[:, heads : heads + 1] + from_own[:, heads + 1 : heads + 2]
    diagonal = lax.broadcasted_iota(jnp.int32, (own, own), 0) == lax.broadcasted_iota(
        jnp.int32, (own, own), 1
    )
    losses[...] = jnp.sum(jnp.where(diagonal, column, 0.0), axis=0, keepdims=True)
    for copy in copies:
        copy.wait()


def outer(heads, order, dp_at, queries, info, latents, hiddens, parts):
    row_count, total = latents.shape
    width = heads * DI
    steps = 8
    hidden_count = hiddens.shape[1]
    return pl.pallas_call(
        functools.partial(outer_kernel, heads, order, dp_at),
        out_shape=(
            jax.ShapeDtypeStruct((row_count, width), f32),
            jax.ShapeDtypeStruct((heads, hidden_count), f32),
            jax.ShapeDtypeStruct((1, queries), f32),
        ),
        in_specs=[in_smem()] + [in_vmem()] * (2 + len(parts)),
        out_specs=(pl.BlockSpec(memory_space=pl.ANY), in_vmem(), in_vmem()),
        scratch_shapes=[
            pltpu.VMEM((total, width + lanes), bf16),
            pltpu.VMEM((steps, row_count, width // steps), f32),
            pltpu.SemaphoreType.DMA((steps,)),
        ],
        compiler_params=params(),
        cost_estimate=pl.CostEstimate(
            flops=2 * total * row_count * width,
            bytes_accessed=4 * row_count * width + 2 * total * width,
            transcendentals=0,
        ),
        name="outer",
    )(info, latents, hiddens, *parts)


def per_device(
    q_latent, hidden, main_queries, main_keys, index_keys, positions, w_query, w_weights
):
    n = lax.axis_size("ctx")
    z = lax.axis_index("ctx")
    head_size = lax.axis_size("head")
    y = lax.axis_index("head")
    dp_size = lax.axis_size("dp")
    dp = lax.axis_index("dp")
    ring = folded_ring(n)
    rows = main_keys.shape[1]
    half = rows // head_size
    rows_latent = w_query.shape[0]
    heads_here = w_weights.shape[1]
    queries_here = main_queries.shape[1]
    sequence_positions = positions[0]

    def onward(x, t=1):
        return lax.ppermute(x, "ctx", [(ring[k], ring[(k + t) % n]) for k in range(n)])

    def swap_head(x):
        return lax.ppermute(x, "head", [(0, 1), (1, 0)])

    def swap_dp(x, bit):
        return lax.ppermute(x, "dp", [(k, k ^ bit) for k in range(dp_size)])

    def over_dp(x):
        gathered, bit = [x], dp_size // 2
        while bit:
            gathered, bit = gathered + [swap_dp(one, bit) for one in gathered], bit // 2
        return gathered

    table = jnp.array(device_table(n, head_size, dp_size, rows))
    info = lax.dynamic_index_in_dim(table, (z * head_size + y) * dp_size + dp, 0, False)

    keys_mine = [lax.dynamic_slice_in_dim(main_keys[0].T, y * half, half, 1)]
    keys_mine.append(onward(keys_mine[0]))
    queries = main_queries[0]
    other_queries = swap_head(queries)
    index_parts = [lax.dynamic_slice_in_dim(index_keys[0], y * half, half)]
    index_parts += [onward(index_parts[0], t) for t in range(1, n - 1)]
    parts, kept = project(info, queries_here, q_latent[0], w_query, hidden[0], w_weights.T)
    received = onward(parts[0])
    order_at = 1 + 3 * n
    dp_at = order_at + n * dp_size
    weights, tops, before = [], [], None

    def score_next(keys):
        nonlocal before
        t = len(weights)
        numer, top, *before = score(
            t, n, info, sequence_positions, queries, other_queries, keys, before
        )
        weights.append(numer)
        tops.append(top)

    index_own = index_other = None
    for t in range(1, n - 1):
        summed = received + parts[t]
        if t == 1:
            keys, summed, index_parts = lax.optimization_barrier(
                (keys_mine[t], summed, index_parts)
            )
            index_parts.append(onward(index_parts[0], n - 1))
        elif t == 2:
            index_own = jnp.concatenate(index_parts)
            keys, summed, index_own = lax.optimization_barrier((keys_mine[t], summed, index_own))
            index_other = swap_head(index_own)
        else:
            keys, summed = lax.optimization_barrier((keys_mine[t], summed))
        keys_mine[t] = keys
        keys_mine.append(onward(keys))
        received = onward(summed)
    while len(weights) < n - 2:
        score_next(keys_mine[len(weights)])
    latents, hiddens = arrange(dp_at, info, rows_latent, over_dp(kept))
    before, latents, hiddens = lax.optimization_barrier((before, latents, hiddens))
    score_next(keys_mine[n - 2])

    part = make_logits(heads_here, received, parts[n - 1], index_own, index_other)
    probs, log_probs = make_softmax(n, info, sequence_positions, part, swap_head(part))

    score_next(keys_mine[n - 1])
    delta_own, sent = make_delta(weights, tops, *before, swap_head(jnp.stack(before)), probs)
    piece = gradients(
        heads_here,
        n,
        received,
        parts[n - 1],
        index_own,
        index_other,
        probs,
        log_probs,
        delta_own,
        sent,
        swap_head(sent),
    )[None]

    brought = []
    for t in range(1, n):
        pairs = [(k, (k + t) % n) for k in range(n)]
        brought.append(lax.ppermute(piece, "ctx", pairs))
    own_pieces = over_dp(piece)
    brought, own_pieces = lax.optimization_barrier((jnp.concatenate(brought), own_pieces))
    brought = over_dp(brought)
    if queries_here % 16:
        flat = jnp.concatenate([jnp.concatenate([a, b]) for a, b in zip(own_pieces, brought)])
        order = jnp.argsort(info[order_at : order_at + n * dp_size])
        parts_in, order = [flat[order].reshape(1, -1, flat.shape[2])], None
    else:
        parts_in, order = own_pieces + brought, []
        order += [order_at + k * n for k in range(dp_size)]
        order += [order_at + k * n + t for k in range(dp_size) for t in range(1, n)]
    grad_query, grad_weights, losses = outer(
        heads_here,
        order,
        dp_at,
        q_latent.shape[1],
        info,
        latents,
        hiddens,
        parts_in,
    )
    return (grad_query, grad_weights.T, losses)


def solution(mesh):
    return jax.shard_map(
        per_device,
        mesh=mesh,
        in_specs=(
            P("dp", None, None),
            P("dp", None, None),
            P("dp", "ctx", "head", None),
            P("dp", "ctx", None),
            P("dp", "ctx", None),
            P("dp", None),
            P("ctx", "head"),
            P("ctx", "head"),
        ),
        out_specs=(P("ctx", "head"), P("ctx", "head"), P("dp", None)),
        check_vma=False,
    )
```

```python
import functools
import math

import jax
import jax.numpy as jnp
import numpy as np
from jax import lax
from jax.experimental import pallas as pl
from jax.experimental.pallas import tpu as pltpu
from jax.sharding import PartitionSpec as P

HI = 64
DI = 128
HM = 128

index_scale = (HI * DI) ** (-0.5)
exponent_scale = 192.0 ** (-0.5) / math.log(2.0)
masked_floor = -1e30
lanes = 128
f32 = jnp.float32
bf16 = jnp.bfloat16
vmem_limit = 24 * 2**20
group_size = 4


def params():
    return pltpu.CompilerParams(vmem_limit_bytes=vmem_limit)


def in_smem():
    return pl.BlockSpec(memory_space=pltpu.SMEM)


def in_vmem():
    return pl.BlockSpec(memory_space=pltpu.VMEM)


def times(a, b, axis_a, axis_b):
    return lax.dot_general(a, b, (((axis_a,), (axis_b,)), ((), ())), preferred_element_type=f32)


at_ctx, at_head, at_dp = 0, 1, 2


class Route:
    def __init__(self, n):
        self.n = n

    def pairs(self, left, step):
        n = self.n
        if left:
            return [(k, k - 1) for k in range(1, n - step + 1)]
        return [(k, k + 1) for k in range(step - 1, n - 1)]

    def joined(self, step):
        return self.n - step < step - 1

    def choose(self, u, z):
        n = self.n
        if z < n // 2:
            return (True, u) if u <= n - 1 - z else (False, n - u)
        return (False, u) if u <= z else (True, n - u)

    def source(self, u, z):
        if u == 0:
            return z
        left, step = self.choose(u, z)
        return z + step if left else z - step

    def options(self, u):
        found = []
        for z in range(self.n):
            left, step = self.choose(u, z)
            one = (None if self.joined(step) else left, step)
            if one not in found:
                found.append(one)
        return found

    def option(self, u, z):
        left, step = self.choose(u, z)
        return self.options(u).index((None if self.joined(step) else left, step))


def device_table(n, heads, dp_size):
    route = Route(n)
    table = []
    for z in range(n):
        for y in range(heads):
            for dp in range(dp_size):
                row = [z, y, dp]
                row += [route.source(u, z) for u in range(n)]
                row += [0] + [route.option(u, z) for u in range(1, n)]
                row += [dp ^ k for k in dp_flips(dp_size)]
                row += [(z - t) % n for t in range(n)]
                table.append(row)
    return np.array(table, np.int32)


def at_source(n, u):
    return 3 + u


def at_option(n, u):
    return 3 + n + u


def at_partner(n, k):
    return 3 + 2 * n + k


def at_shift(n, dp_size, t):
    return 3 + 2 * n + dp_size + t


def dp_flips(dp_size):
    flips, bit = [0], dp_size // 2
    while bit:
        flips, bit = flips + [k ^ bit for k in flips], bit // 2
    return flips


def project_kernel(info, latent, weight, hidden, hidden_weight, out, kept):
    blocks, count, _ = out.shape
    width = weight.shape[1]
    heads = hidden_weight.shape[0]
    for at in range(0, width, 512):
        product = times(latent[...], weight[:, at : at + 512], 1, 0)
        for k in range(blocks):
            out[k, :, at : at + 512] = product[k * count : (k + 1) * count]
    mixed = times(hidden[...], hidden_weight[...], 1, 1)
    for k in range(blocks):
        out[k, :, width : width + heads] = mixed[k * count : (k + 1) * count]
        out[k, :, width + heads :] = jnp.zeros((count, lanes - heads), f32)
    kept[:, : latent.shape[1]] = latent[...]
    kept[:, latent.shape[1] :] = hidden[...]


def project(info, count, latent, weight, hidden, hidden_weight):
    queries, width = latent.shape[0], weight.shape[1]
    depth, hidden_depth = weight.shape[0], hidden_weight.shape[1]
    blocks = queries // count
    columns = lambda i, info: (0, info[at_ctx])
    whole = lambda i, info: (0, 0)
    if depth % lanes or hidden_depth % lanes:
        latent = lax.dynamic_slice_in_dim(latent, info[at_ctx] * depth, depth, 1)
        hidden = lax.dynamic_slice_in_dim(hidden, info[at_ctx] * hidden_depth, hidden_depth, 1)
        columns = whole
    return pl.pallas_call(
        project_kernel,
        grid_spec=pltpu.PrefetchScalarGridSpec(
            num_scalar_prefetch=1,
            grid=(1,),
            in_specs=[
                pl.BlockSpec((queries, depth), columns),
                pl.BlockSpec((depth, width), whole),
                pl.BlockSpec((queries, hidden_depth), columns),
                pl.BlockSpec(hidden_weight.shape, whole),
            ],
            out_specs=[
                pl.BlockSpec((blocks, count, width + lanes), lambda i, info: (0, 0, 0)),
                pl.BlockSpec((queries, depth + hidden_depth), whole),
            ],
        ),
        out_shape=[
            jax.ShapeDtypeStruct((blocks, count, width + lanes), f32),
            jax.ShapeDtypeStruct((queries, depth + hidden_depth), bf16),
        ],
        compiler_params=params(),
        cost_estimate=pl.CostEstimate(
            flops=2 * queries * weight.size, bytes_accessed=2 * weight.size, transcendentals=0
        ),
        name="project",
    )(info, latent, weight, hidden, hidden_weight)


def score_kernel(t, n, rows_here, info, positions, mine, other, *refs):
    options, refs = refs[:-10], refs[-10:]
    top_before, mass_before, weights, top, top_all, mass_all, mass, even, odd, chosen = refs
    count, heads, depth = mine.shape
    keys = options[0]
    if len(options) > 1:
        keys = chosen
        for k, option in enumerate(options):

            @pl.when(info[at_option(n, t)] == k)
            def _():
                chosen[...] = option[...]

    base = info[at_source(n, t)] * rows_here + info[at_head] * keys.shape[1]
    limits = [positions[info[at_ctx] * count + q] - base for q in range(count)]
    span = keys.shape[1]
    key_at = lax.broadcasted_iota(jnp.int32, (1, span), 1)
    row_at = lax.broadcasted_iota(jnp.int32, (heads, lanes), 0)
    lane_at = lax.broadcasted_iota(jnp.int32, (heads, lanes), 1)
    group = min(group_size, count)
    work = [(at, k) for at in range(0, count, group) for k in range(2)]
    held = (even, odd)

    def multiply(step):
        at, k = work[step]
        rows = (mine, other)[k][at : at + group].reshape(group * heads, depth)
        held[step % 2][...] = times(rows, keys[...], 1, 0)

    multiply(0)
    for step, (at, k) in enumerate(work):
        if step + 1 < len(work):
            multiply(step + 1)
        scores = held[step % 2]
        offset = k * heads
        diagonal = lane_at == row_at + offset
        for i in range(group):
            q = at + i
            one = jnp.where(
                key_at <= limits[q], scores[i * heads : (i + 1) * heads, :], masked_floor
            )
            high = jnp.max(one, axis=1, keepdims=True)
            shifted = jnp.exp2((one - high) * exponent_scale)
            total = jnp.sum(shifted, axis=1, keepdims=True)
            weights[q, offset : offset + heads] = shifted.astype(bf16)
            high_row = jnp.sum(jnp.where(diagonal, high, 0.0), axis=0, keepdims=True)
            total_row = jnp.sum(jnp.where(diagonal, total, 0.0), axis=0, keepdims=True)
            if k == 0:
                top[q : q + 1, :] = high_row
                mass[q : q + 1, :] = total_row
            else:
                top[q : q + 1, :] += high_row
                mass[q : q + 1, :] += total_row
    if t == 0:
        top_all[...] = top[...]
        mass_all[...] = mass[...]
    else:
        before, now = top_before[...], top[...]
        joint = jnp.maximum(before, now)
        top_all[...] = joint
        mass_all[...] = mass_before[...] * jnp.exp2((before - joint) * exponent_scale) + mass[
            ...
        ] * jnp.exp2((now - joint) * exponent_scale)


def score(t, n, rows_here, info, positions, mine, other, options, before):
    count, heads, depth = mine.shape
    span = options[0].shape[1]
    stats = jax.ShapeDtypeStruct((count, lanes), f32)
    if before is None:
        before = (jnp.zeros((count, lanes), f32),) * 2
    return pl.pallas_call(
        functools.partial(score_kernel, t, n, rows_here),
        out_shape=(jax.ShapeDtypeStruct((count, 2 * heads, span), bf16), stats, stats, stats),
        in_specs=[in_smem()] * 2 + [in_vmem()] * (4 + len(options)),
        out_specs=(in_vmem(),) * 4,
        scratch_shapes=[pltpu.VMEM((count, lanes), f32)]
        + [pltpu.VMEM((min(group_size, count) * heads, span), f32)] * 2
        + [pltpu.VMEM((depth, span), bf16)],
        compiler_params=params(),
        cost_estimate=pl.CostEstimate(
            flops=4 * count * heads * depth * span,
            bytes_accessed=2 * (2 * mine.size + depth * span + 2 * count * heads * span),
            transcendentals=2 * count * heads * span,
        ),
        name="score",
    )(info, positions, mine, other, *options, *before)


def delta_kernel(blocks, info, *refs):
    weights, tops = refs[:blocks], refs[blocks : 2 * blocks]
    top, mass, far, probs, out, sent, held = refs[2 * blocks :]
    count, heads, span = weights[0].shape
    far_top = pltpu.roll(far[0], heads // 2, 1)
    far_mass = pltpu.roll(far[1], heads // 2, 1)
    joint = jnp.maximum(top[...], far_top)
    total = mass[...] * jnp.exp2((top[...] - joint) * exponent_scale) + far_mass * jnp.exp2(
        (far_top - joint) * exponent_scale
    )
    row_at = lax.broadcasted_iota(jnp.int32, (heads, lanes), 0)
    lane_at = lax.broadcasted_iota(jnp.int32, (heads, lanes), 1)
    diagonal = row_at == lane_at
    inverse = 1.0 / (total * HM)
    for t in range(blocks):
        factor = jnp.exp2((tops[t][...] - joint) * exponent_scale) * inverse
        to = pl.ds(pl.multiple_of(info[at_source(blocks, t)] * span, span), span)
        for q in range(count):
            column = jnp.sum(
                jnp.where(diagonal, factor[q : q + 1, :], 0.0), axis=1, keepdims=True
            )
            mixed = weights[t][q].astype(f32) * column
            held[q : q + 1, to] = jnp.sum(mixed, axis=0, keepdims=True)
    delta = probs[0] - held[...]
    out[...] = delta
    sent[...] = delta.astype(bf16)


def make_delta(info, weights, tops, top, mass, far, probs):
    blocks = len(weights)
    count, heads, span = weights[0].shape
    return pl.pallas_call(
        functools.partial(delta_kernel, blocks),
        out_shape=(
            jax.ShapeDtypeStruct((count, blocks * span), f32),
            jax.ShapeDtypeStruct((count, blocks * span), bf16),
        ),
        in_specs=[in_smem()] + [in_vmem()] * (2 * blocks + 4),
        out_specs=(in_vmem(),) * 2,
        scratch_shapes=[pltpu.VMEM((count, blocks * span), f32)],
        compiler_params=params(),
        cost_estimate=pl.CostEstimate(
            flops=2 * blocks * count * heads * span,
            bytes_accessed=2 * blocks * count * heads * span,
            transcendentals=0,
        ),
        name="delta",
    )(info, *weights, *tops, top, mass, far, probs)


def query_rows(total, heads):
    return jnp.concatenate(
        [total[:, j * DI : (j + 1) * DI].astype(bf16) for j in range(heads)], axis=0
    )


def summed(received):
    total = received[0]
    for k in range(1, received.shape[0]):
        total = total + received[k]
    return total


def logits_kernel(heads, received, own, other, out):
    count = received.shape[1]
    total = summed(received)
    query = query_rows(total, heads)
    columns = [total[:, heads * DI + j : heads * DI + j + 1] for j in range(heads)]
    span = 512
    for part, keys in enumerate((own, other)):
        for at in range(0, keys.shape[0], span):
            affinity = times(query, keys[at : at + span, :], 1, 1)
            running = jnp.zeros((count, span), f32)
            for j in range(heads):
                reached = jnp.maximum(affinity[j * count : (j + 1) * count], 0.0)
                running = running + columns[j] * reached
            out[part, :, at : at + span] = running * index_scale


def make_logits(heads, received, own, other):
    count, length = received.shape[1], own.shape[0]
    return pl.pallas_call(
        functools.partial(logits_kernel, heads),
        out_shape=jax.ShapeDtypeStruct((2, count, length), f32),
        in_specs=[in_vmem()] * 3,
        out_specs=in_vmem(),
        compiler_params=params(),
        cost_estimate=pl.CostEstimate(
            flops=4 * count * heads * DI * length,
            bytes_accessed=4 * (received.size + 2 * count * length) + 4 * length * DI,
            transcendentals=0,
        ),
        name="logits",
    )(received, own, other)


def softmax_kernel(blocks, rows_here, info, positions, part, far, probs, log_probs):
    _, count, length = part.shape
    span = length // blocks
    row_at = lax.broadcasted_iota(jnp.int32, (count, lanes), 0)
    position = jnp.zeros((count, lanes), jnp.int32)
    for q in range(count):
        position = jnp.where(row_at == q, positions[info[at_ctx] * count + q], position)
    position = position[:, 0:1]
    key_at = lax.broadcasted_iota(jnp.int32, (count, span), 1)

    def seen(side, t):
        half = info[at_head] if side == 0 else 1 - info[at_head]
        return key_at + (t * rows_here + half * span) <= position

    highs = []
    for side in range(2):
        high = jnp.full((count, span), masked_floor, f32)
        for t in range(blocks):
            at = slice(t * span, (t + 1) * span)
            value = part[side, :, at] + far[1 - side, :, at]
            log_probs[side, :, at] = value
            high = jnp.maximum(high, jnp.where(seen(side, t), value, masked_floor))
        highs.append(jnp.max(high, axis=1, keepdims=True))
    high = jnp.maximum(highs[0], highs[1])
    sums = []
    for side in range(2):
        running = jnp.zeros((count, span), f32)
        for t in range(blocks):
            at = slice(t * span, (t + 1) * span)
            grown = jnp.where(seen(side, t), jnp.exp(log_probs[side, :, at] - high), 0.0)
            probs[side, :, at] = grown
            running = running + grown
        sums.append(jnp.sum(running, axis=1, keepdims=True))
    mass = sums[0] + sums[1]
    level = high + jnp.log(mass)
    inverse = 1.0 / mass
    for side in range(2):
        for t in range(blocks):
            at = slice(t * span, (t + 1) * span)
            probs[side, :, at] = probs[side, :, at] * inverse
            log_probs[side, :, at] = jnp.where(seen(side, t), log_probs[side, :, at] - level, 0.0)


def make_softmax(blocks, rows_here, info, positions, part, far):
    return pl.pallas_call(
        functools.partial(softmax_kernel, blocks, rows_here),
        out_shape=(jax.ShapeDtypeStruct(part.shape, f32),) * 2,
        in_specs=[in_smem()] * 2 + [in_vmem()] * 2,
        out_specs=(in_vmem(),) * 2,
        compiler_params=params(),
        cost_estimate=pl.CostEstimate(
            flops=8 * part.size, bytes_accessed=16 * part.size, transcendentals=part.size
        ),
        name="softmax",
    )(info, positions, part, far)


def gradient_kernel(
    heads,
    blocks,
    received,
    own,
    other,
    probs,
    log_probs,
    delta_own,
    sent,
    brought,
    out,
    flow,
    query_sum,
    grads,
    even,
    odd,
):
    count = received.shape[1]
    total = summed(received)
    span = own.shape[0] // blocks
    query = query_rows(total, heads)
    columns = [
        total[:, heads * DI + j : heads * DI + j + 1] * index_scale for j in range(heads)
    ]
    work = [(side, t) for side in range(2) for t in range(blocks)]
    held = (even, odd)

    def multiply(step):
        side, t = work[step]
        keys = (own, other)[side][t * span : (t + 1) * span, :]
        held[step % 2][...] = times(query, keys, 1, 1)

    multiply(0)
    flow[...] = jnp.zeros(flow.shape, f32)
    running = [jnp.zeros((count, span), f32)] * 2
    for step, (side, t) in enumerate(work):
        if step + 1 < len(work):
            multiply(step + 1)
        at = slice(t * span, (t + 1) * span)
        affinity = held[step % 2]
        rounded = (sent, brought)[side][:, at].astype(f32)
        delta = delta_own[:, at] if side == 0 else rounded
        wanted = probs[side, :, at] - rounded
        running[side] = running[side] + wanted * log_probs[side, :, at]
        for j in range(heads):
            rows = slice(j * count, (j + 1) * count)
            one = affinity[rows, :]
            reached = jnp.where(one > 0, delta, 0.0)
            grads[rows, :] = (reached * columns[j]).astype(bf16)
            product = reached * one
            folded = product[:, :lanes]
            for k in range(lanes, span, lanes):
                folded = folded + product[:, k : k + lanes]
            flow[rows, :] += folded
        keys = (own, other)[side][at, :]
        product = times(grads[...], keys, 1, 0)
        if step == 0:
            query_sum[...] = product
        else:
            query_sum[...] += product
    losses = [jnp.sum(one, axis=1, keepdims=True) for one in running]
    loss = -(losses[0] + losses[1])
    lane_at = lax.broadcasted_iota(jnp.int32, (count, lanes), 1)
    tail = jnp.zeros((count, lanes), f32)
    for j in range(heads):
        rows = slice(j * count, (j + 1) * count)
        out[:, j * DI : (j + 1) * DI] = query_sum[rows, :].astype(bf16)
        column = jnp.sum(flow[rows, :], axis=1, keepdims=True) * index_scale
        tail = jnp.where(lane_at == j, column, tail)
    loss_high = loss.astype(bf16).astype(f32)
    tail = jnp.where(lane_at == heads, loss_high, tail)
    tail = jnp.where(lane_at == heads + 1, loss - loss_high, tail)
    out[:, heads * DI :] = tail.astype(bf16)


def gradients(heads, blocks, received, own, other, probs, log_probs, delta_own, sent, brought):
    count, length = received.shape[1], own.shape[0]
    span = length // blocks
    return pl.pallas_call(
        functools.partial(gradient_kernel, heads, blocks),
        out_shape=jax.ShapeDtypeStruct((count, heads * DI + lanes), bf16),
        in_specs=[in_vmem()] * 8,
        out_specs=in_vmem(),
        scratch_shapes=[
            pltpu.VMEM((heads * count, lanes), f32),
            pltpu.VMEM((heads * count, DI), f32),
            pltpu.VMEM((heads * count, span), bf16),
            pltpu.VMEM((heads * count, span), f32),
            pltpu.VMEM((heads * count, span), f32),
        ],
        compiler_params=params(),
        cost_estimate=pl.CostEstimate(
            flops=8 * count * heads * DI * length,
            bytes_accessed=4 * (received.size + 6 * count * length) + 4 * length * DI,
            transcendentals=0,
        ),
        name="gradient",
    )(received, own, other, probs, log_probs, delta_own, sent, brought)


def arrange_kernel(n, info, *refs):
    kept, (latents, hiddens, held) = refs[:-3], refs[-3:]
    queries, depth = kept[0].shape[0], latents.shape[0]
    for k, one in enumerate(kept):
        to = pl.ds(pl.multiple_of(info[at_partner(n, k)] * queries, queries), queries)
        held[to, :] = one[:, :depth].astype(f32)
        hiddens[to, :] = one[:, depth:]
    latents[...] = held[...].T.astype(bf16)


def arrange(n, info, depth, kept):
    queries, width = kept[0].shape
    total = queries * len(kept)
    return pl.pallas_call(
        functools.partial(arrange_kernel, n),
        out_shape=(
            jax.ShapeDtypeStruct((depth, total), bf16),
            jax.ShapeDtypeStruct((total, width - depth), bf16),
        ),
        in_specs=[in_smem()] + [in_vmem()] * len(kept),
        out_specs=(in_vmem(),) * 2,
        scratch_shapes=[pltpu.VMEM((total, depth), f32)],
        compiler_params=params(),
        cost_estimate=pl.CostEstimate(
            flops=0, bytes_accessed=4 * total * width, transcendentals=0
        ),
        name="arrange",
    )(info, *kept)


def outer_kernel(heads, n, order, info, latents, hiddens, *refs):
    parts, (grad, grad_mixed, losses, rows, blocks, sems) = refs[:-6], refs[-6:]
    count = parts[0].shape[-2]
    width = heads * DI
    steps, _, span = blocks.shape
    k = 0
    for part in parts:
        for t in range(part.shape[0]):
            to = 0
            if order is not None:
                to = pl.multiple_of((info[order[k][0]] * n + info[order[k][1]]) * count, count)
            rows[pl.ds(to, count), :] = part[t]
            k += 1
    copies = []
    for i in range(steps):
        at = slice(i * span, (i + 1) * span)
        blocks[i] = times(latents[...], rows[:, at], 1, 0)
        copies.append(pltpu.make_async_copy(blocks.at[i], grad.at[:, at], sems.at[i]))
        copies[-1].start()
    tails = rows[:, width:]
    grad_mixed[...] = times(tails, hiddens[...], 0, 0)[:heads]
    own = losses.shape[1]
    from_own = rows[pl.ds(pl.multiple_of(info[at_dp] * own, own), own), width:].astype(f32)
    column = from_own[:, heads : heads + 1] + from_own[:, heads + 1 : heads + 2]
    diagonal = lax.broadcasted_iota(jnp.int32, (own, own), 0) == lax.broadcasted_iota(
        jnp.int32, (own, own), 1
    )
    losses[...] = jnp.sum(jnp.where(diagonal, column, 0.0), axis=0, keepdims=True)
    for copy in copies:
        copy.wait()


def outer(heads, n, order, queries, info, latents, hiddens, parts):
    row_count, total = latents.shape
    width = heads * DI
    steps = 8
    hidden_count = hiddens.shape[1]
    return pl.pallas_call(
        functools.partial(outer_kernel, heads, n, order),
        out_shape=(
            jax.ShapeDtypeStruct((row_count, width), f32),
            jax.ShapeDtypeStruct((heads, hidden_count), f32),
            jax.ShapeDtypeStruct((1, queries), f32),
        ),
        in_specs=[in_smem()] + [in_vmem()] * (2 + len(parts)),
        out_specs=(pl.BlockSpec(memory_space=pl.ANY), in_vmem(), in_vmem()),
        scratch_shapes=[
            pltpu.VMEM((total, width + lanes), bf16),
            pltpu.VMEM((steps, row_count, width // steps), f32),
            pltpu.SemaphoreType.DMA((steps,)),
        ],
        compiler_params=params(),
        cost_estimate=pl.CostEstimate(
            flops=2 * total * row_count * width,
            bytes_accessed=4 * row_count * width + 2 * total * width,
            transcendentals=0,
        ),
        name="outer",
    )(info, latents, hiddens, *parts)


def per_device(
    q_latent, hidden, main_queries, main_keys, index_keys, positions, w_query, w_weights
):
    n = lax.axis_size("ctx")
    z = lax.axis_index("ctx")
    head_size = lax.axis_size("head")
    y = lax.axis_index("head")
    dp_size = lax.axis_size("dp")
    dp = lax.axis_index("dp")
    route = Route(n)
    rows = main_keys.shape[1]
    half = rows // head_size
    rows_latent = w_query.shape[0]
    heads_here = w_weights.shape[1]
    queries_here = main_queries.shape[1]
    sequence_positions = positions[0]

    def to_each(x):
        return lax.all_to_all(x, "ctx", 0, 0)

    def swap_head(x):
        return lax.ppermute(x, "head", [(0, 1), (1, 0)])

    def swap_dp(x, bit):
        return lax.ppermute(x, "dp", [(k, k ^ bit) for k in range(dp_size)])

    def over_dp(x):
        gathered, bit = [x], dp_size // 2
        while bit:
            gathered, bit = gathered + [swap_dp(one, bit) for one in gathered], bit // 2
        return gathered

    table = jnp.array(device_table(n, head_size, dp_size))
    info = lax.dynamic_index_in_dim(table, (z * head_size + y) * dp_size + dp, 0, False)

    own_keys = lax.dynamic_slice_in_dim(main_keys[0].T, y * half, half, 1)
    carried = {}
    last = {True: own_keys, False: own_keys}
    for step in range(1, n):
        if route.joined(step):
            x = jnp.where(z <= n - step, last[True], last[False])
            x = lax.ppermute(x, "ctx", route.pairs(True, step) + route.pairs(False, step))
            carried[None, step] = last[True] = last[False] = x
        else:
            for left in (True, False):
                last[left] = lax.ppermute(last[left], "ctx", route.pairs(left, step))
                carried[left, step] = last[left]
    queries = main_queries[0]
    other_queries = swap_head(queries)

    partial, kept = project(info, queries_here, q_latent[0], w_query, hidden[0], w_weights.T)
    received = to_each(partial)
    index_part = lax.dynamic_slice_in_dim(index_keys[0], y * half, half)
    index_own = to_each(jnp.broadcast_to(index_part[None], (n, *index_part.shape)))
    index_own = index_own.reshape(n * half, DI)
    index_other = swap_head(index_own)
    part = make_logits(heads_here, received, index_own, index_other)
    probs, log_probs = make_softmax(n, rows, info, sequence_positions, part, swap_head(part))
    latents, hiddens = arrange(n, info, rows_latent, over_dp(kept))

    weights, tops, before = [], [], None
    for t in range(n):
        options = [own_keys] if t == 0 else [carried[one] for one in route.options(t)]
        if t == n - 2:
            before, latents, hiddens, part = lax.optimization_barrier(
                (before, latents, hiddens, part)
            )
        if t == n - 1:
            before, probs, log_probs = lax.optimization_barrier((before, probs, log_probs))
        numer, top, *before = score(
            t, n, rows, info, sequence_positions, queries, other_queries, options, before
        )
        weights.append(numer)
        tops.append(top)
    delta_own, sent = make_delta(info, weights, tops, *before, swap_head(jnp.stack(before)), probs)
    piece = gradients(
        heads_here,
        n,
        received,
        index_own,
        index_other,
        probs,
        log_probs,
        delta_own,
        sent,
        swap_head(sent),
    )[None]

    brought = []
    for t in range(1, n):
        pairs = [(k, (k + t) % n) for k in range(n)]
        brought.append(lax.ppermute(piece, "ctx", pairs))
    own_pieces = over_dp(piece)
    brought, own_pieces = lax.optimization_barrier((jnp.concatenate(brought), own_pieces))
    brought = over_dp(brought)
    parts_in = own_pieces + brought
    order = [(at_partner(n, k), at_shift(n, dp_size, 0)) for k in range(dp_size)]
    order += [
        (at_partner(n, k), at_shift(n, dp_size, t)) for k in range(dp_size) for t in range(1, n)
    ]
    if queries_here % 16:
        places = jnp.stack([info[a] * n + info[b] for a, b in order])
        flat = jnp.concatenate(parts_in)[jnp.argsort(places)]
        parts_in, order = [flat.reshape(1, -1, flat.shape[2])], None
    grad_query, grad_weights, losses = outer(
        heads_here, n, order, q_latent.shape[1], info, latents, hiddens, parts_in
    )
    return (grad_query, grad_weights.T, losses)


def solution(mesh):
    return jax.shard_map(
        per_device,
        mesh=mesh,
        in_specs=(
            P("dp", None, None),
            P("dp", None, None),
            P("dp", "ctx", "head", None),
            P("dp", "ctx", None),
            P("dp", "ctx", None),
            P("dp", None),
            P("ctx", "head"),
            P("ctx", "head"),
        ),
        out_specs=(P("ctx", "head"), P("ctx", "head"), P("dp", None)),
        check_vma=False,
    )
```

```python
import functools
import math

import jax
import jax.numpy as jnp
import numpy as np
from jax import lax
from jax.experimental import pallas as pl
from jax.experimental.pallas import tpu as pltpu
from jax.sharding import PartitionSpec as P

HI = 64
DI = 128
HM = 128

index_scale = (HI * DI) ** (-0.5)
exponent_scale = 192.0 ** (-0.5) / math.log(2.0)
masked_floor = -1e30
lanes = 128
f32 = jnp.float32
bf16 = jnp.bfloat16
vmem_limit = 24 * 2**20
group_size = 4


def folded_ring(size):
    return [0] + list(range(1, size, 2)) + list(range(2, size, 2))[::-1]


def params():
    return pltpu.CompilerParams(vmem_limit_bytes=vmem_limit)


def in_smem():
    return pl.BlockSpec(memory_space=pltpu.SMEM)


def in_vmem():
    return pl.BlockSpec(memory_space=pltpu.VMEM)


def times(a, b, axis_a, axis_b):
    return lax.dot_general(a, b, (((axis_a,), (axis_b,)), ((), ())), preferred_element_type=f32)


def device_table(n, heads, dp_size, rows):
    ring = folded_ring(n)
    half = rows // heads
    flips = dp_flips(dp_size)
    table = []
    for z in range(n):
        place = ring.index(z)
        behind = [ring[(place - t) % n] for t in range(n)]
        for y in range(heads):
            for dp in range(dp_size):
                row = [z] + [ring[(place - 1 - t) % n] for t in range(n)]
                row += [k * rows + y * half for k in behind]
                row += [k * rows + (1 - y) * half for k in behind]
                row += [(dp ^ k) * n + (z - t) % n for k in flips for t in range(n)]
                row += [dp ^ k for k in flips]
                table.append(row)
    return np.array(table, np.int32)


def dp_flips(dp_size):
    flips, bit = [0], dp_size // 2
    while bit:
        flips, bit = flips + [k ^ bit for k in flips], bit // 2
    return flips


def project_kernel(aligned, info, latent, weight, hidden, hidden_weight, *outs):
    *parts, kept = outs
    width = weight.shape[1]
    heads = hidden_weight.shape[0]
    count = parts[0].shape[0]
    if aligned:
        starts = [pl.multiple_of(info[1 + k] * count, count) for k in range(len(parts))]
        rows = jnp.concatenate([latent[pl.ds(k, count), :] for k in starts], axis=0)
        mixed_rows = jnp.concatenate([hidden[pl.ds(k, count), :] for k in starts], axis=0)
    else:
        rows, mixed_rows = latent[...], hidden[...]
    for at in range(0, width, 512):
        product = times(rows, weight[:, at : at + 512], 1, 0)
        for k, out in enumerate(parts):
            out[:, at : at + 512] = product[k * count : (k + 1) * count]
    mixed = times(mixed_rows, hidden_weight[...], 1, 1)
    for k, out in enumerate(parts):
        out[:, width : width + heads] = mixed[k * count : (k + 1) * count]
        out[:, width + heads :] = jnp.zeros((count, lanes - heads), f32)
    kept[:, : latent.shape[1]] = latent[...]
    kept[:, latent.shape[1] :] = hidden[...]


def project(info, count, latent, weight, hidden, hidden_weight):
    queries, width = latent.shape[0], weight.shape[1]
    depth, hidden_depth = weight.shape[0], hidden_weight.shape[1]
    blocks = queries // count
    aligned = count % 16 == 0 and depth % lanes == 0 and hidden_depth % lanes == 0
    columns = lambda i, info: (0, info[0])
    whole = lambda i, info: (0, 0)
    kept = None
    if not aligned:
        latent = lax.dynamic_slice_in_dim(latent, info[0] * depth, depth, 1)
        hidden = lax.dynamic_slice_in_dim(hidden, info[0] * hidden_depth, hidden_depth, 1)
        kept = jnp.concatenate([latent, hidden], axis=1)
        order = info[1 : 1 + blocks]
        latent = latent.reshape(blocks, count, depth)[order].reshape(queries, depth)
        hidden = hidden.reshape(blocks, count, hidden_depth)[order].reshape(queries, hidden_depth)
        columns = whole
    *parts, kept_here = pl.pallas_call(
        functools.partial(project_kernel, aligned),
        grid_spec=pltpu.PrefetchScalarGridSpec(
            num_scalar_prefetch=1,
            grid=(1,),
            in_specs=[
                pl.BlockSpec((queries, depth), columns),
                pl.BlockSpec((depth, width), whole),
                pl.BlockSpec((queries, hidden_depth), columns),
                pl.BlockSpec(hidden_weight.shape, whole),
            ],
            out_specs=[pl.BlockSpec((count, width + lanes), whole)] * blocks
            + [pl.BlockSpec((queries, depth + hidden_depth), whole)],
        ),
        out_shape=[jax.ShapeDtypeStruct((count, width + lanes), f32)] * blocks
        + [jax.ShapeDtypeStruct((queries, depth + hidden_depth), bf16)],
        compiler_params=params(),
        cost_estimate=pl.CostEstimate(
            flops=2 * queries * weight.size, bytes_accessed=2 * weight.size, transcendentals=0
        ),
        name="project",
    )(info, latent, weight, hidden, hidden_weight)
    return parts, kept_here if aligned else kept


def score_kernel(
    t,
    base_at,
    info,
    positions,
    mine,
    other,
    *refs,
):
    chains, refs = refs[:-9], refs[-9:]
    top_before, mass_before, weights, top, top_all, mass_all, mass, even, odd = refs
    count, heads, depth = mine.shape
    limits = [positions[info[0] * count + q] - info[base_at] for q in range(count)]
    part = chains[0].shape[1]
    span = part * len(chains)
    key_at = lax.broadcasted_iota(jnp.int32, (1, span), 1)
    row_at = lax.broadcasted_iota(jnp.int32, (heads, lanes), 0)
    lane_at = lax.broadcasted_iota(jnp.int32, (heads, lanes), 1)
    group = min(group_size, count)
    work = [(at, k) for at in range(0, count, group) for k in range(2)]
    held = (even, odd)

    def multiply(step):
        at, k = work[step]
        rows = (mine, other)[k][at : at + group].reshape(group * heads, depth)
        for c, keys in enumerate(chains):
            held[step % 2][:, c * part : (c + 1) * part] = times(rows, keys[...], 1, 0)

    multiply(0)
    for step, (at, k) in enumerate(work):
        if step + 1 < len(work):
            multiply(step + 1)
        scores = held[step % 2]
        offset = k * heads
        diagonal = lane_at == row_at + offset
        for i in range(group):
            q = at + i
            one = jnp.where(
                key_at <= limits[q], scores[i * heads : (i + 1) * heads, :], masked_floor
            )
            high = jnp.max(one, axis=1, keepdims=True)
            shifted = jnp.exp2((one - high) * exponent_scale)
            total = jnp.sum(shifted, axis=1, keepdims=True)
            weights[q, offset : offset + heads] = shifted.astype(bf16)
            high_row = jnp.sum(jnp.where(diagonal, high, 0.0), axis=0, keepdims=True)
            total_row = jnp.sum(jnp.where(diagonal, total, 0.0), axis=0, keepdims=True)
            if k == 0:
                top[q : q + 1, :] = high_row
                mass[q : q + 1, :] = total_row
            else:
                top[q : q + 1, :] += high_row
                mass[q : q + 1, :] += total_row
    if t == 0:
        top_all[...] = top[...]
        mass_all[...] = mass[...]
    else:
        before, now = top_before[...], top[...]
        joint = jnp.maximum(before, now)
        top_all[...] = joint
        mass_all[...] = mass_before[...] * jnp.exp2((before - joint) * exponent_scale) + mass[
            ...
        ] * jnp.exp2((now - joint) * exponent_scale)


def score(t, n, info, positions, mine, other, chains, before):
    count, heads, depth = mine.shape
    span = chains[0].shape[1] * len(chains)
    stats = jax.ShapeDtypeStruct((count, lanes), f32)
    if before is None:
        before = (jnp.zeros((count, lanes), f32),) * 2
    return pl.pallas_call(
        functools.partial(score_kernel, t, 1 + n + t),
        out_shape=(jax.ShapeDtypeStruct((count, 2 * heads, span), bf16), stats, stats, stats),
        in_specs=[in_smem()] * 2 + [in_vmem()] * (4 + len(chains)),
        out_specs=(in_vmem(),) * 4,
        scratch_shapes=[pltpu.VMEM((count, lanes), f32)]
        + [pltpu.VMEM((min(group_size, count) * heads, span), f32)] * 2,
        compiler_params=params(),
        cost_estimate=pl.CostEstimate(
            flops=4 * count * heads * depth * span,
            bytes_accessed=2 * (2 * mine.size + depth * span + 2 * count * heads * span),
            transcendentals=2 * count * heads * span,
        ),
        name="score",
    )(info, positions, mine, other, *chains, *before)


def delta_kernel(blocks, *refs):
    weights, tops = refs[:blocks], refs[blocks : 2 * blocks]
    top, mass, far, probs, out, sent, held = refs[2 * blocks :]
    count, heads, span = weights[0].shape
    far_top = pltpu.roll(far[0], heads // 2, 1)
    far_mass = pltpu.roll(far[1], heads // 2, 1)
    joint = jnp.maximum(top[...], far_top)
    total = mass[...] * jnp.exp2((top[...] - joint) * exponent_scale) + far_mass * jnp.exp2(
        (far_top - joint) * exponent_scale
    )
    row_at = lax.broadcasted_iota(jnp.int32, (heads, lanes), 0)
    lane_at = lax.broadcasted_iota(jnp.int32, (heads, lanes), 1)
    diagonal = row_at == lane_at
    inverse = 1.0 / (total * HM)
    for t in range(blocks):
        factor = jnp.exp2((tops[t][...] - joint) * exponent_scale) * inverse
        for q in range(count):
            column = jnp.sum(
                jnp.where(diagonal, factor[q : q + 1, :], 0.0), axis=1, keepdims=True
            )
            mixed = weights[t][q].astype(f32) * column
            held[q : q + 1, t * span : (t + 1) * span] = jnp.sum(mixed, axis=0, keepdims=True)
    delta = probs[0] - held[...]
    out[...] = delta
    sent[...] = delta.astype(bf16)


def make_delta(weights, tops, top, mass, far, probs):
    blocks = len(weights)
    count, heads, span = weights[0].shape
    return pl.pallas_call(
        functools.partial(delta_kernel, blocks),
        out_shape=(
            jax.ShapeDtypeStruct((count, blocks * span), f32),
            jax.ShapeDtypeStruct((count, blocks * span), bf16),
        ),
        in_specs=[in_vmem()] * (2 * blocks + 4),
        out_specs=(in_vmem(),) * 2,
        scratch_shapes=[pltpu.VMEM((count, blocks * span), f32)],
        compiler_params=params(),
        cost_estimate=pl.CostEstimate(
            flops=2 * blocks * count * heads * span,
            bytes_accessed=2 * blocks * count * heads * span,
            transcendentals=0,
        ),
        name="delta",
    )(*weights, *tops, top, mass, far, probs)


def query_rows(total, heads):
    return jnp.concatenate(
        [total[:, j * DI : (j + 1) * DI].astype(bf16) for j in range(heads)], axis=0
    )


def logits_kernel(heads, received, here, own, other, out):
    count = received.shape[0]
    total = received[...] + here[...]
    query = query_rows(total, heads)
    columns = [total[:, heads * DI + j : heads * DI + j + 1] for j in range(heads)]
    span = 512
    for part, keys in enumerate((own, other)):
        for at in range(0, keys.shape[0], span):
            affinity = times(query, keys[at : at + span, :], 1, 1)
            running = jnp.zeros((count, span), f32)
            for j in range(heads):
                reached = jnp.maximum(affinity[j * count : (j + 1) * count], 0.0)
                running = running + columns[j] * reached
            out[part, :, at : at + span] = running * index_scale


def make_logits(heads, received, here, own, other):
    count, length = received.shape[0], own.shape[0]
    return pl.pallas_call(
        functools.partial(logits_kernel, heads),
        out_shape=jax.ShapeDtypeStruct((2, count, length), f32),
        in_specs=[in_vmem()] * 4,
        out_specs=in_vmem(),
        compiler_params=params(),
        cost_estimate=pl.CostEstimate(
            flops=4 * count * heads * DI * length,
            bytes_accessed=4 * (2 * received.size + 2 * count * length) + 4 * length * DI,
            transcendentals=0,
        ),
        name="logits",
    )(received, here, own, other)


def softmax_kernel(blocks, info, positions, part, far, probs, log_probs):
    _, count, length = part.shape
    span = length // blocks
    row_at = lax.broadcasted_iota(jnp.int32, (count, lanes), 0)
    position = jnp.zeros((count, lanes), jnp.int32)
    for q in range(count):
        position = jnp.where(row_at == q, positions[info[0] * count + q], position)
    position = position[:, 0:1]
    key_at = lax.broadcasted_iota(jnp.int32, (count, span), 1)

    def seen(side, t):
        return key_at + info[1 + (1 + side) * blocks + t] <= position

    highs = []
    for side in range(2):
        high = jnp.full((count, span), masked_floor, f32)
        for t in range(blocks):
            at = slice(t * span, (t + 1) * span)
            value = part[side, :, at] + far[1 - side, :, at]
            log_probs[side, :, at] = value
            high = jnp.maximum(high, jnp.where(seen(side, t), value, masked_floor))
        highs.append(jnp.max(high, axis=1, keepdims=True))
    high = jnp.maximum(highs[0], highs[1])
    sums = []
    for side in range(2):
        running = jnp.zeros((count, span), f32)
        for t in range(blocks):
            at = slice(t * span, (t + 1) * span)
            grown = jnp.where(seen(side, t), jnp.exp(log_probs[side, :, at] - high), 0.0)
            probs[side, :, at] = grown
            running = running + grown
        sums.append(jnp.sum(running, axis=1, keepdims=True))
    mass = sums[0] + sums[1]
    level = high + jnp.log(mass)
    inverse = 1.0 / mass
    for side in range(2):
        for t in range(blocks):
            at = slice(t * span, (t + 1) * span)
            probs[side, :, at] = probs[side, :, at] * inverse
            log_probs[side, :, at] = jnp.where(seen(side, t), log_probs[side, :, at] - level, 0.0)


def make_softmax(blocks, info, positions, part, far):
    return pl.pallas_call(
        functools.partial(softmax_kernel, blocks),
        out_shape=(jax.ShapeDtypeStruct(part.shape, f32),) * 2,
        in_specs=[in_smem()] * 2 + [in_vmem()] * 2,
        out_specs=(in_vmem(),) * 2,
        compiler_params=params(),
        cost_estimate=pl.CostEstimate(
            flops=8 * part.size, bytes_accessed=16 * part.size, transcendentals=part.size
        ),
        name="softmax",
    )(info, positions, part, far)


def gradient_kernel(
    heads,
    blocks,
    received,
    here,
    own,
    other,
    probs,
    log_probs,
    delta_own,
    sent,
    brought,
    out,
    flow,
    query_sum,
    grads,
    even,
    odd,
):
    count = received.shape[0]
    total = received[...] + here[...]
    span = own.shape[0] // blocks
    query = query_rows(total, heads)
    columns = [
        total[:, heads * DI + j : heads * DI + j + 1] * index_scale for j in range(heads)
    ]
    work = [(side, t) for side in range(2) for t in range(blocks)]
    held = (even, odd)

    def multiply(step):
        side, t = work[step]
        keys = (own, other)[side][t * span : (t + 1) * span, :]
        held[step % 2][...] = times(query, keys, 1, 1)

    multiply(0)
    flow[...] = jnp.zeros(flow.shape, f32)
    running = [jnp.zeros((count, span), f32)] * 2
    for step, (side, t) in enumerate(work):
        if step + 1 < len(work):
            multiply(step + 1)
        at = slice(t * span, (t + 1) * span)
        affinity = held[step % 2]
        rounded = (sent, brought)[side][:, at].astype(f32)
        delta = delta_own[:, at] if side == 0 else rounded
        wanted = probs[side, :, at] - rounded
        running[side] = running[side] + wanted * log_probs[side, :, at]
        for j in range(heads):
            rows = slice(j * count, (j + 1) * count)
            one = affinity[rows, :]
            reached = jnp.where(one > 0, delta, 0.0)
            grads[rows, :] = (reached * columns[j]).astype(bf16)
            product = reached * one
            folded = product[:, :lanes]
            for k in range(lanes, span, lanes):
                folded = folded + product[:, k : k + lanes]
            flow[rows, :] += folded
        keys = (own, other)[side][at, :]
        product = times(grads[...], keys, 1, 0)
        if step == 0:
            query_sum[...] = product
        else:
            query_sum[...] += product
    losses = [jnp.sum(one, axis=1, keepdims=True) for one in running]
    loss = -(losses[0] + losses[1])
    lane_at = lax.broadcasted_iota(jnp.int32, (count, lanes), 1)
    tail = jnp.zeros((count, lanes), f32)
    for j in range(heads):
        rows = slice(j * count, (j + 1) * count)
        out[:, j * DI : (j + 1) * DI] = query_sum[rows, :].astype(bf16)
        column = jnp.sum(flow[rows, :], axis=1, keepdims=True) * index_scale
        tail = jnp.where(lane_at == j, column, tail)
    loss_high = loss.astype(bf16).astype(f32)
    tail = jnp.where(lane_at == heads, loss_high, tail)
    tail = jnp.where(lane_at == heads + 1, loss - loss_high, tail)
    out[:, heads * DI :] = tail.astype(bf16)


def gradients(heads, blocks, received, here, own, other, probs, log_probs, delta_own, sent, brought):
    count, length = received.shape[0], own.shape[0]
    span = length // blocks
    return pl.pallas_call(
        functools.partial(gradient_kernel, heads, blocks),
        out_shape=jax.ShapeDtypeStruct((count, heads * DI + lanes), bf16),
        in_specs=[in_vmem()] * 9,
        out_specs=in_vmem(),
        scratch_shapes=[
            pltpu.VMEM((heads * count, lanes), f32),
            pltpu.VMEM((heads * count, DI), f32),
            pltpu.VMEM((heads * count, span), bf16),
            pltpu.VMEM((heads * count, span), f32),
            pltpu.VMEM((heads * count, span), f32),
        ],
        compiler_params=params(),
        cost_estimate=pl.CostEstimate(
            flops=8 * count * heads * DI * length,
            bytes_accessed=4 * (2 * received.size + 6 * count * length) + 4 * length * DI,
            transcendentals=0,
        ),
        name="gradient",
    )(received, here, own, other, probs, log_probs, delta_own, sent, brought)


def arrange_kernel(at, info, *refs):
    kept, (latents, hiddens, held) = refs[:-3], refs[-3:]
    queries, depth = kept[0].shape[0], latents.shape[0]
    for k, one in enumerate(kept):
        to = pl.ds(pl.multiple_of(info[at + k] * queries, queries), queries)
        held[to, :] = one[:, :depth].astype(f32)
        hiddens[to, :] = one[:, depth:]
    latents[...] = held[...].T.astype(bf16)


def arrange(at, info, depth, kept):
    queries, width = kept[0].shape
    total = queries * len(kept)
    return pl.pallas_call(
        functools.partial(arrange_kernel, at),
        out_shape=(
            jax.ShapeDtypeStruct((depth, total), bf16),
            jax.ShapeDtypeStruct((total, width - depth), bf16),
        ),
        in_specs=[in_smem()] + [in_vmem()] * len(kept),
        out_specs=(in_vmem(),) * 2,
        scratch_shapes=[pltpu.VMEM((total, depth), f32)],
        compiler_params=params(),
        cost_estimate=pl.CostEstimate(
            flops=0, bytes_accessed=4 * total * width, transcendentals=0
        ),
        name="arrange",
    )(info, *kept)


def outer_kernel(heads, order, dp_at, info, latents, hiddens, *refs):
    parts, (grad, grad_mixed, losses, rows, blocks, sems) = refs[:-6], refs[-6:]
    count = parts[0].shape[-2]
    width = heads * DI
    steps, _, span = blocks.shape
    k = 0
    for part in parts:
        for t in range(part.shape[0]):
            to = 0 if order is None else pl.multiple_of(info[order[k]] * count, count)
            rows[pl.ds(to, count), :] = part[t]
            k += 1
    copies = []
    for i in range(steps):
        at = slice(i * span, (i + 1) * span)
        blocks[i] = times(latents[...], rows[:, at], 1, 0)
        copies.append(pltpu.make_async_copy(blocks.at[i], grad.at[:, at], sems.at[i]))
        copies[-1].start()
    tails = rows[:, width:]
    grad_mixed[...] = times(tails, hiddens[...], 0, 0)[:heads]
    own = losses.shape[1]
    from_own = rows[pl.ds(pl.multiple_of(info[dp_at] * own, own), own), width:].astype(f32)
    column = from_own[:, heads : heads + 1] + from_own[:, heads + 1 : heads + 2]
    diagonal = lax.broadcasted_iota(jnp.int32, (own, own), 0) == lax.broadcasted_iota(
        jnp.int32, (own, own), 1
    )
    losses[...] = jnp.sum(jnp.where(diagonal, column, 0.0), axis=0, keepdims=True)
    for copy in copies:
        copy.wait()


def outer(heads, order, dp_at, queries, info, latents, hiddens, parts):
    row_count, total = latents.shape
    width = heads * DI
    steps = 8
    hidden_count = hiddens.shape[1]
    return pl.pallas_call(
        functools.partial(outer_kernel, heads, order, dp_at),
        out_shape=(
            jax.ShapeDtypeStruct((row_count, width), f32),
            jax.ShapeDtypeStruct((heads, hidden_count), f32),
            jax.ShapeDtypeStruct((1, queries), f32),
        ),
        in_specs=[in_smem()] + [in_vmem()] * (2 + len(parts)),
        out_specs=(pl.BlockSpec(memory_space=pl.ANY), in_vmem(), in_vmem()),
        scratch_shapes=[
            pltpu.VMEM((total, width + lanes), bf16),
            pltpu.VMEM((steps, row_count, width // steps), f32),
            pltpu.SemaphoreType.DMA((steps,)),
        ],
        compiler_params=params(),
        cost_estimate=pl.CostEstimate(
            flops=2 * total * row_count * width,
            bytes_accessed=4 * row_count * width + 2 * total * width,
            transcendentals=0,
        ),
        name="outer",
    )(info, latents, hiddens, *parts)


def per_device(
    q_latent, hidden, main_queries, main_keys, index_keys, positions, w_query, w_weights
):
    n = lax.axis_size("ctx")
    z = lax.axis_index("ctx")
    head_size = lax.axis_size("head")
    y = lax.axis_index("head")
    dp_size = lax.axis_size("dp")
    dp = lax.axis_index("dp")
    ring = folded_ring(n)
    rows = main_keys.shape[1]
    half = rows // head_size
    rows_latent = w_query.shape[0]
    heads_here = w_weights.shape[1]
    queries_here = main_queries.shape[1]
    sequence_positions = positions[0]

    def onward(x, t=1):
        return lax.ppermute(x, "ctx", [(ring[k], ring[(k + t) % n]) for k in range(n)])

    def swap_head(x):
        return lax.ppermute(x, "head", [(0, 1), (1, 0)])

    def swap_dp(x, bit):
        return lax.ppermute(x, "dp", [(k, k ^ bit) for k in range(dp_size)])

    def over_dp(x):
        gathered, bit = [x], dp_size // 2
        while bit:
            gathered, bit = gathered + [swap_dp(one, bit) for one in gathered], bit // 2
        return gathered

    table = jnp.array(device_table(n, head_size, dp_size, rows))
    info = lax.dynamic_index_in_dim(table, (z * head_size + y) * dp_size + dp, 0, False)

    key_half = lax.dynamic_slice_in_dim(main_keys[0].T, y * half, half, 1)
    chains = [[key_half[:, : half // 2], key_half[:, half // 2 :]]]
    chains.append([onward(one) for one in chains[0]])
    queries = main_queries[0]
    other_queries = swap_head(queries)
    index_parts = [lax.dynamic_slice_in_dim(index_keys[0], y * half, half)] + [None] * (n - 1)
    index_parts[1] = onward(index_parts[0])
    index_parts[1], back = lax.optimization_barrier((index_parts[1], index_parts[0]))
    index_parts[n - 1] = onward(back, n - 1)
    parts, kept = project(info, queries_here, q_latent[0], w_query, hidden[0], w_weights.T)

    def advance(step, running):
        running = onward(running)
        return running + parts[step] if step < n - 1 else running

    summed = advance(1, parts[0])
    order_at = 1 + 3 * n
    dp_at = order_at + n * dp_size
    weights, tops, before = [], [], None

    def score_next():
        nonlocal before
        t = len(weights)
        numer, top, *before = score(
            t, n, info, sequence_positions, queries, other_queries, chains[t], before
        )
        weights.append(numer)
        tops.append(top)

    index_own = index_other = None
    for t in range(1, n - 1):
        summed = advance(t + 1, summed)
        if t == 1:
            sent_on, summed, index_parts = lax.optimization_barrier(
                (chains[t], summed, index_parts)
            )
            for k in range(2, n - 1):
                index_parts[k] = onward(index_parts[1]) if k == 2 else onward(index_parts[0], k)
        elif t == 2:
            index_own = jnp.concatenate(index_parts)
            sent_on, summed, index_own = lax.optimization_barrier((chains[t], summed, index_own))
            index_other = swap_head(index_own)
        else:
            sent_on, summed = lax.optimization_barrier((chains[t], summed))
        chains[t] = sent_on
        chains.append([onward(one) for one in sent_on])
    received = summed
    while len(weights) < n - 2:
        score_next()
    latents, hiddens = arrange(dp_at, info, rows_latent, over_dp(kept))
    before, latents, hiddens = lax.optimization_barrier((before, latents, hiddens))
    score_next()

    part = make_logits(heads_here, received, parts[n - 1], index_own, index_other)
    probs, log_probs = make_softmax(n, info, sequence_positions, part, swap_head(part))

    before, probs, log_probs = lax.optimization_barrier((before, probs, log_probs))
    score_next()
    delta_own, sent = make_delta(weights, tops, *before, swap_head(jnp.stack(before)), probs)
    piece = gradients(
        heads_here,
        n,
        received,
        parts[n - 1],
        index_own,
        index_other,
        probs,
        log_probs,
        delta_own,
        sent,
        swap_head(sent),
    )[None]

    brought = []
    for t in range(1, n):
        pairs = [(k, (k + t) % n) for k in range(n)]
        brought.append(lax.ppermute(piece, "ctx", pairs))
    own_pieces = over_dp(piece)
    brought, own_pieces = lax.optimization_barrier((jnp.concatenate(brought), own_pieces))
    brought = over_dp(brought)
    if queries_here % 16:
        flat = jnp.concatenate([jnp.concatenate([a, b]) for a, b in zip(own_pieces, brought)])
        order = jnp.argsort(info[order_at : order_at + n * dp_size])
        parts_in, order = [flat[order].reshape(1, -1, flat.shape[2])], None
    else:
        parts_in, order = own_pieces + brought, []
        order += [order_at + k * n for k in range(dp_size)]
        order += [order_at + k * n + t for k in range(dp_size) for t in range(1, n)]
    grad_query, grad_weights, losses = outer(
        heads_here,
        order,
        dp_at,
        q_latent.shape[1],
        info,
        latents,
        hiddens,
        parts_in,
    )
    return (grad_query, grad_weights.T, losses)


def solution(mesh):
    return jax.shard_map(
        per_device,
        mesh=mesh,
        in_specs=(
            P("dp", None, None),
            P("dp", None, None),
            P("dp", "ctx", "head", None),
            P("dp", "ctx", None),
            P("dp", "ctx", None),
            P("dp", None),
            P("ctx", "head"),
            P("ctx", "head"),
        ),
        out_specs=(P("ctx", "head"), P("ctx", "head"), P("dp", None)),
        check_vma=False,
    )
```

```python
import functools
import math

import jax
import jax.numpy as jnp
import numpy as np
from jax import lax
from jax.experimental import pallas as pl
from jax.experimental.pallas import tpu as pltpu
from jax.sharding import PartitionSpec as P

HI = 64
DI = 128
HM = 128

index_scale = (HI * DI) ** (-0.5)
exponent_scale = 192.0 ** (-0.5) / math.log(2.0)
masked_floor = -1e30
lanes = 128
f32 = jnp.float32
bf16 = jnp.bfloat16
vmem_limit = 24 * 2**20
group_size = 4


def folded_ring(size):
    return [0] + list(range(1, size, 2)) + list(range(2, size, 2))[::-1]


def params():
    return pltpu.CompilerParams(vmem_limit_bytes=vmem_limit)


def in_smem():
    return pl.BlockSpec(memory_space=pltpu.SMEM)


def in_vmem():
    return pl.BlockSpec(memory_space=pltpu.VMEM)


def times(a, b, axis_a, axis_b):
    return lax.dot_general(a, b, (((axis_a,), (axis_b,)), ((), ())), preferred_element_type=f32)


def device_table(n, heads, dp_size, rows):
    ring = folded_ring(n)
    half = rows // heads
    flips = dp_flips(dp_size)
    table = []
    for z in range(n):
        place = ring.index(z)
        behind = [ring[(place - t) % n] for t in range(n)]
        for y in range(heads):
            for dp in range(dp_size):
                row = [z] + [ring[(place - 1 - t) % n] for t in range(n)]
                row += [k * rows + y * half for k in behind]
                row += [k * rows + (1 - y) * half for k in behind]
                row += [(dp ^ k) * n + (z - t) % n for k in flips for t in range(n)]
                row += [dp ^ k for k in flips]
                table.append(row)
    return np.array(table, np.int32)


def dp_flips(dp_size):
    flips, bit = [0], dp_size // 2
    while bit:
        flips, bit = flips + [k ^ bit for k in flips], bit // 2
    return flips


def project_kernel(aligned, info, latent, weight, hidden, hidden_weight, *outs):
    *parts, kept = outs
    width = weight.shape[1]
    heads = hidden_weight.shape[0]
    count = parts[0].shape[0]
    if aligned:
        starts = [pl.multiple_of(info[1 + k] * count, count) for k in range(len(parts))]
        rows = jnp.concatenate([latent[pl.ds(k, count), :] for k in starts], axis=0)
        mixed_rows = jnp.concatenate([hidden[pl.ds(k, count), :] for k in starts], axis=0)
    else:
        rows, mixed_rows = latent[...], hidden[...]
    for at in range(0, width, 512):
        product = times(rows, weight[:, at : at + 512], 1, 0)
        for k, out in enumerate(parts):
            out[:, at : at + 512] = product[k * count : (k + 1) * count]
    mixed = times(mixed_rows, hidden_weight[...], 1, 1)
    for k, out in enumerate(parts):
        out[:, width : width + heads] = mixed[k * count : (k + 1) * count]
        out[:, width + heads :] = jnp.zeros((count, lanes - heads), f32)
    kept[:, : latent.shape[1]] = latent[...]
    kept[:, latent.shape[1] :] = hidden[...]


def project(info, count, latent, weight, hidden, hidden_weight):
    queries, width = latent.shape[0], weight.shape[1]
    depth, hidden_depth = weight.shape[0], hidden_weight.shape[1]
    blocks = queries // count
    aligned = count % 16 == 0 and depth % lanes == 0 and hidden_depth % lanes == 0
    columns = lambda i, info: (0, info[0])
    whole = lambda i, info: (0, 0)
    kept = None
    if not aligned:
        latent = lax.dynamic_slice_in_dim(latent, info[0] * depth, depth, 1)
        hidden = lax.dynamic_slice_in_dim(hidden, info[0] * hidden_depth, hidden_depth, 1)
        kept = jnp.concatenate([latent, hidden], axis=1)
        order = info[1 : 1 + blocks]
        latent = latent.reshape(blocks, count, depth)[order].reshape(queries, depth)
        hidden = hidden.reshape(blocks, count, hidden_depth)[order].reshape(queries, hidden_depth)
        columns = whole
    *parts, kept_here = pl.pallas_call(
        functools.partial(project_kernel, aligned),
        grid_spec=pltpu.PrefetchScalarGridSpec(
            num_scalar_prefetch=1,
            grid=(1,),
            in_specs=[
                pl.BlockSpec((queries, depth), columns),
                pl.BlockSpec((depth, width), whole),
                pl.BlockSpec((queries, hidden_depth), columns),
                pl.BlockSpec(hidden_weight.shape, whole),
            ],
            out_specs=[pl.BlockSpec((count, width + lanes), whole)] * blocks
            + [pl.BlockSpec((queries, depth + hidden_depth), whole)],
        ),
        out_shape=[jax.ShapeDtypeStruct((count, width + lanes), f32)] * blocks
        + [jax.ShapeDtypeStruct((queries, depth + hidden_depth), bf16)],
        compiler_params=params(),
        cost_estimate=pl.CostEstimate(
            flops=2 * queries * weight.size, bytes_accessed=2 * weight.size, transcendentals=0
        ),
        name="project",
    )(info, latent, weight, hidden, hidden_weight)
    return parts, kept_here if aligned else kept


def score_kernel(
    t,
    base_at,
    info,
    positions,
    mine,
    other,
    keys,
    top_before,
    mass_before,
    weights,
    top,
    top_all,
    mass_all,
    mass,
    even,
    odd,
):
    count, heads, depth = mine.shape
    limits = [positions[info[0] * count + q] - info[base_at] for q in range(count)]
    span = keys.shape[1]
    key_at = lax.broadcasted_iota(jnp.int32, (1, span), 1)
    row_at = lax.broadcasted_iota(jnp.int32, (heads, lanes), 0)
    lane_at = lax.broadcasted_iota(jnp.int32, (heads, lanes), 1)
    group = min(group_size, count)
    work = [(at, k) for at in range(0, count, group) for k in range(2)]
    held = (even, odd)

    def multiply(step):
        at, k = work[step]
        rows = (mine, other)[k][at : at + group].reshape(group * heads, depth)
        held[step % 2][...] = times(rows, keys[...], 1, 0)

    multiply(0)
    for step, (at, k) in enumerate(work):
        if step + 1 < len(work):
            multiply(step + 1)
        scores = held[step % 2]
        offset = k * heads
        diagonal = lane_at == row_at + offset
        for i in range(group):
            q = at + i
            one = jnp.where(
                key_at <= limits[q], scores[i * heads : (i + 1) * heads, :], masked_floor
            )
            high = jnp.max(one, axis=1, keepdims=True)
            shifted = jnp.exp2((one - high) * exponent_scale)
            total = jnp.sum(shifted, axis=1, keepdims=True)
            weights[q, offset : offset + heads] = shifted.astype(bf16)
            high_row = jnp.sum(jnp.where(diagonal, high, 0.0), axis=0, keepdims=True)
            total_row = jnp.sum(jnp.where(diagonal, total, 0.0), axis=0, keepdims=True)
            if k == 0:
                top[q : q + 1, :] = high_row
                mass[q : q + 1, :] = total_row
            else:
                top[q : q + 1, :] += high_row
                mass[q : q + 1, :] += total_row
    if t == 0:
        top_all[...] = top[...]
        mass_all[...] = mass[...]
    else:
        before, now = top_before[...], top[...]
        joint = jnp.maximum(before, now)
        top_all[...] = joint
        mass_all[...] = mass_before[...] * jnp.exp2((before - joint) * exponent_scale) + mass[
            ...
        ] * jnp.exp2((now - joint) * exponent_scale)


def score(t, n, info, positions, mine, other, keys, before):
    count, heads, depth = mine.shape
    span = keys.shape[1]
    stats = jax.ShapeDtypeStruct((count, lanes), f32)
    if before is None:
        before = (jnp.zeros((count, lanes), f32),) * 2
    return pl.pallas_call(
        functools.partial(score_kernel, t, 1 + n + t),
        out_shape=(jax.ShapeDtypeStruct((count, 2 * heads, span), bf16), stats, stats, stats),
        in_specs=[in_smem()] * 2 + [in_vmem()] * 5,
        out_specs=(in_vmem(),) * 4,
        scratch_shapes=[pltpu.VMEM((count, lanes), f32)]
        + [pltpu.VMEM((min(group_size, count) * heads, span), f32)] * 2,
        compiler_params=params(),
        cost_estimate=pl.CostEstimate(
            flops=4 * count * heads * depth * span,
            bytes_accessed=2 * (2 * mine.size + keys.size + 2 * count * heads * span),
            transcendentals=2 * count * heads * span,
        ),
        name="score",
    )(info, positions, mine, other, keys, *before)


def delta_kernel(blocks, *refs):
    weights, tops = refs[:blocks], refs[blocks : 2 * blocks]
    top, mass, far, probs, out, sent, held = refs[2 * blocks :]
    count, heads, span = weights[0].shape
    far_top = pltpu.roll(far[0], heads // 2, 1)
    far_mass = pltpu.roll(far[1], heads // 2, 1)
    joint = jnp.maximum(top[...], far_top)
    total = mass[...] * jnp.exp2((top[...] - joint) * exponent_scale) + far_mass * jnp.exp2(
        (far_top - joint) * exponent_scale
    )
    row_at = lax.broadcasted_iota(jnp.int32, (heads, lanes), 0)
    lane_at = lax.broadcasted_iota(jnp.int32, (heads, lanes), 1)
    diagonal = row_at == lane_at
    inverse = 1.0 / (total * HM)
    for t in range(blocks):
        factor = jnp.exp2((tops[t][...] - joint) * exponent_scale) * inverse
        for q in range(count):
            column = jnp.sum(
                jnp.where(diagonal, factor[q : q + 1, :], 0.0), axis=1, keepdims=True
            )
            mixed = weights[t][q].astype(f32) * column
            held[q : q + 1, t * span : (t + 1) * span] = jnp.sum(mixed, axis=0, keepdims=True)
    delta = probs[0] - held[...]
    out[...] = delta
    sent[...] = delta.astype(bf16)


def make_delta(weights, tops, top, mass, far, probs):
    blocks = len(weights)
    count, heads, span = weights[0].shape
    return pl.pallas_call(
        functools.partial(delta_kernel, blocks),
        out_shape=(
            jax.ShapeDtypeStruct((count, blocks * span), f32),
            jax.ShapeDtypeStruct((count, blocks * span), bf16),
        ),
        in_specs=[in_vmem()] * (2 * blocks + 4),
        out_specs=(in_vmem(),) * 2,
        scratch_shapes=[pltpu.VMEM((count, blocks * span), f32)],
        compiler_params=params(),
        cost_estimate=pl.CostEstimate(
            flops=2 * blocks * count * heads * span,
            bytes_accessed=2 * blocks * count * heads * span,
            transcendentals=0,
        ),
        name="delta",
    )(*weights, *tops, top, mass, far, probs)


def query_rows(total, heads):
    return jnp.concatenate(
        [total[:, j * DI : (j + 1) * DI].astype(bf16) for j in range(heads)], axis=0
    )


def logits_kernel(heads, received, here, own, other, out):
    count = received.shape[0]
    total = received[...] + here[...]
    query = query_rows(total, heads)
    columns = [total[:, heads * DI + j : heads * DI + j + 1] for j in range(heads)]
    span = 512
    for part, keys in enumerate((own, other)):
        for at in range(0, keys.shape[0], span):
            affinity = times(query, keys[at : at + span, :], 1, 1)
            running = jnp.zeros((count, span), f32)
            for j in range(heads):
                reached = jnp.maximum(affinity[j * count : (j + 1) * count], 0.0)
                running = running + columns[j] * reached
            out[part, :, at : at + span] = running * index_scale


def make_logits(heads, received, here, own, other):
    count, length = received.shape[0], own.shape[0]
    return pl.pallas_call(
        functools.partial(logits_kernel, heads),
        out_shape=jax.ShapeDtypeStruct((2, count, length), f32),
        in_specs=[in_vmem()] * 4,
        out_specs=in_vmem(),
        compiler_params=params(),
        cost_estimate=pl.CostEstimate(
            flops=4 * count * heads * DI * length,
            bytes_accessed=4 * (2 * received.size + 2 * count * length) + 4 * length * DI,
            transcendentals=0,
        ),
        name="logits",
    )(received, here, own, other)


def softmax_kernel(blocks, info, positions, part, far, probs, log_probs):
    _, count, length = part.shape
    span = length // blocks
    row_at = lax.broadcasted_iota(jnp.int32, (count, lanes), 0)
    position = jnp.zeros((count, lanes), jnp.int32)
    for q in range(count):
        position = jnp.where(row_at == q, positions[info[0] * count + q], position)
    position = position[:, 0:1]
    key_at = lax.broadcasted_iota(jnp.int32, (count, span), 1)

    def seen(side, t):
        return key_at + info[1 + (1 + side) * blocks + t] <= position

    highs = []
    for side in range(2):
        high = jnp.full((count, span), masked_floor, f32)
        for t in range(blocks):
            at = slice(t * span, (t + 1) * span)
            value = part[side, :, at] + far[1 - side, :, at]
            log_probs[side, :, at] = value
            high = jnp.maximum(high, jnp.where(seen(side, t), value, masked_floor))
        highs.append(jnp.max(high, axis=1, keepdims=True))
    high = jnp.maximum(highs[0], highs[1])
    sums = []
    for side in range(2):
        running = jnp.zeros((count, span), f32)
        for t in range(blocks):
            at = slice(t * span, (t + 1) * span)
            grown = jnp.where(seen(side, t), jnp.exp(log_probs[side, :, at] - high), 0.0)
            probs[side, :, at] = grown
            running = running + grown
        sums.append(jnp.sum(running, axis=1, keepdims=True))
    mass = sums[0] + sums[1]
    level = high + jnp.log(mass)
    inverse = 1.0 / mass
    for side in range(2):
        for t in range(blocks):
            at = slice(t * span, (t + 1) * span)
            probs[side, :, at] = probs[side, :, at] * inverse
            log_probs[side, :, at] = jnp.where(seen(side, t), log_probs[side, :, at] - level, 0.0)


def make_softmax(blocks, info, positions, part, far):
    return pl.pallas_call(
        functools.partial(softmax_kernel, blocks),
        out_shape=(jax.ShapeDtypeStruct(part.shape, f32),) * 2,
        in_specs=[in_smem()] * 2 + [in_vmem()] * 2,
        out_specs=(in_vmem(),) * 2,
        compiler_params=params(),
        cost_estimate=pl.CostEstimate(
            flops=8 * part.size, bytes_accessed=16 * part.size, transcendentals=part.size
        ),
        name="softmax",
    )(info, positions, part, far)


def gradient_kernel(
    heads,
    blocks,
    received,
    here,
    own,
    other,
    probs,
    log_probs,
    delta_own,
    sent,
    brought,
    out,
    flow,
    query_sum,
    grads,
    even,
    odd,
):
    count = received.shape[0]
    total = received[...] + here[...]
    span = own.shape[0] // blocks
    query = query_rows(total, heads)
    columns = [
        total[:, heads * DI + j : heads * DI + j + 1] * index_scale for j in range(heads)
    ]
    work = [(side, t) for side in range(2) for t in range(blocks)]
    held = (even, odd)

    def multiply(step):
        side, t = work[step]
        keys = (own, other)[side][t * span : (t + 1) * span, :]
        held[step % 2][...] = times(query, keys, 1, 1)

    multiply(0)
    flow[...] = jnp.zeros(flow.shape, f32)
    running = [jnp.zeros((count, span), f32)] * 2
    for step, (side, t) in enumerate(work):
        if step + 1 < len(work):
            multiply(step + 1)
        at = slice(t * span, (t + 1) * span)
        affinity = held[step % 2]
        rounded = (sent, brought)[side][:, at].astype(f32)
        delta = delta_own[:, at] if side == 0 else rounded
        wanted = probs[side, :, at] - rounded
        running[side] = running[side] + wanted * log_probs[side, :, at]
        for j in range(heads):
            rows = slice(j * count, (j + 1) * count)
            one = affinity[rows, :]
            reached = jnp.where(one > 0, delta, 0.0)
            grads[rows, :] = (reached * columns[j]).astype(bf16)
            product = reached * one
            folded = product[:, :lanes]
            for k in range(lanes, span, lanes):
                folded = folded + product[:, k : k + lanes]
            flow[rows, :] += folded
        keys = (own, other)[side][at, :]
        product = times(grads[...], keys, 1, 0)
        if step == 0:
            query_sum[...] = product
        else:
            query_sum[...] += product
    losses = [jnp.sum(one, axis=1, keepdims=True) for one in running]
    loss = -(losses[0] + losses[1])
    lane_at = lax.broadcasted_iota(jnp.int32, (count, lanes), 1)
    tail = jnp.zeros((count, lanes), f32)
    for j in range(heads):
        rows = slice(j * count, (j + 1) * count)
        out[:, j * DI : (j + 1) * DI] = query_sum[rows, :].astype(bf16)
        column = jnp.sum(flow[rows, :], axis=1, keepdims=True) * index_scale
        tail = jnp.where(lane_at == j, column, tail)
    loss_high = loss.astype(bf16).astype(f32)
    tail = jnp.where(lane_at == heads, loss_high, tail)
    tail = jnp.where(lane_at == heads + 1, loss - loss_high, tail)
    out[:, heads * DI :] = tail.astype(bf16)


def gradients(heads, blocks, received, here, own, other, probs, log_probs, delta_own, sent, brought):
    count, length = received.shape[0], own.shape[0]
    span = length // blocks
    return pl.pallas_call(
        functools.partial(gradient_kernel, heads, blocks),
        out_shape=jax.ShapeDtypeStruct((count, heads * DI + lanes), bf16),
        in_specs=[in_vmem()] * 9,
        out_specs=in_vmem(),
        scratch_shapes=[
            pltpu.VMEM((heads * count, lanes), f32),
            pltpu.VMEM((heads * count, DI), f32),
            pltpu.VMEM((heads * count, span), bf16),
            pltpu.VMEM((heads * count, span), f32),
            pltpu.VMEM((heads * count, span), f32),
        ],
        compiler_params=params(),
        cost_estimate=pl.CostEstimate(
            flops=8 * count * heads * DI * length,
            bytes_accessed=4 * (2 * received.size + 6 * count * length) + 4 * length * DI,
            transcendentals=0,
        ),
        name="gradient",
    )(received, here, own, other, probs, log_probs, delta_own, sent, brought)


def arrange_kernel(at, info, *refs):
    kept, (latents, hiddens, held) = refs[:-3], refs[-3:]
    queries, depth = kept[0].shape[0], latents.shape[0]
    for k, one in enumerate(kept):
        to = pl.ds(pl.multiple_of(info[at + k] * queries, queries), queries)
        held[to, :] = one[:, :depth].astype(f32)
        hiddens[to, :] = one[:, depth:]
    latents[...] = held[...].T.astype(bf16)


def arrange(at, info, depth, kept):
    queries, width = kept[0].shape
    total = queries * len(kept)
    return pl.pallas_call(
        functools.partial(arrange_kernel, at),
        out_shape=(
            jax.ShapeDtypeStruct((depth, total), bf16),
            jax.ShapeDtypeStruct((total, width - depth), bf16),
        ),
        in_specs=[in_smem()] + [in_vmem()] * len(kept),
        out_specs=(in_vmem(),) * 2,
        scratch_shapes=[pltpu.VMEM((total, depth), f32)],
        compiler_params=params(),
        cost_estimate=pl.CostEstimate(
            flops=0, bytes_accessed=4 * total * width, transcendentals=0
        ),
        name="arrange",
    )(info, *kept)


def outer_kernel(heads, order, dp_at, info, latents, hiddens, *refs):
    parts, (grad, grad_mixed, losses, rows, blocks, sems) = refs[:-6], refs[-6:]
    count = parts[0].shape[-2]
    width = heads * DI
    steps, _, span = blocks.shape
    k = 0
    for part in parts:
        for t in range(part.shape[0]):
            to = 0 if order is None else pl.multiple_of(info[order[k]] * count, count)
            rows[pl.ds(to, count), :] = part[t]
            k += 1
    copies = []
    for i in range(steps):
        at = slice(i * span, (i + 1) * span)
        blocks[i] = times(latents[...], rows[:, at], 1, 0)
        copies.append(pltpu.make_async_copy(blocks.at[i], grad.at[:, at], sems.at[i]))
        copies[-1].start()
    tails = rows[:, width:]
    grad_mixed[...] = times(tails, hiddens[...], 0, 0)[:heads]
    own = losses.shape[1]
    from_own = rows[pl.ds(pl.multiple_of(info[dp_at] * own, own), own), width:].astype(f32)
    column = from_own[:, heads : heads + 1] + from_own[:, heads + 1 : heads + 2]
    diagonal = lax.broadcasted_iota(jnp.int32, (own, own), 0) == lax.broadcasted_iota(
        jnp.int32, (own, own), 1
    )
    losses[...] = jnp.sum(jnp.where(diagonal, column, 0.0), axis=0, keepdims=True)
    for copy in copies:
        copy.wait()


def outer(heads, order, dp_at, queries, info, latents, hiddens, parts):
    row_count, total = latents.shape
    width = heads * DI
    steps = 8
    hidden_count = hiddens.shape[1]
    return pl.pallas_call(
        functools.partial(outer_kernel, heads, order, dp_at),
        out_shape=(
            jax.ShapeDtypeStruct((row_count, width), f32),
            jax.ShapeDtypeStruct((heads, hidden_count), f32),
            jax.ShapeDtypeStruct((1, queries), f32),
        ),
        in_specs=[in_smem()] + [in_vmem()] * (2 + len(parts)),
        out_specs=(pl.BlockSpec(memory_space=pl.ANY), in_vmem(), in_vmem()),
        scratch_shapes=[
            pltpu.VMEM((total, width + lanes), bf16),
            pltpu.VMEM((steps, row_count, width // steps), f32),
            pltpu.SemaphoreType.DMA((steps,)),
        ],
        compiler_params=params(),
        cost_estimate=pl.CostEstimate(
            flops=2 * total * row_count * width,
            bytes_accessed=4 * row_count * width + 2 * total * width,
            transcendentals=0,
        ),
        name="outer",
    )(info, latents, hiddens, *parts)


def per_device(
    q_latent, hidden, main_queries, main_keys, index_keys, positions, w_query, w_weights
):
    n = lax.axis_size("ctx")
    z = lax.axis_index("ctx")
    head_size = lax.axis_size("head")
    y = lax.axis_index("head")
    dp_size = lax.axis_size("dp")
    dp = lax.axis_index("dp")
    ring = folded_ring(n)
    rows = main_keys.shape[1]
    half = rows // head_size
    rows_latent = w_query.shape[0]
    heads_here = w_weights.shape[1]
    queries_here = main_queries.shape[1]
    sequence_positions = positions[0]

    def onward(x, t=1):
        return lax.ppermute(x, "ctx", [(ring[k], ring[(k + t) % n]) for k in range(n)])

    def swap_head(x):
        return lax.ppermute(x, "head", [(0, 1), (1, 0)])

    def swap_dp(x, bit):
        return lax.ppermute(x, "dp", [(k, k ^ bit) for k in range(dp_size)])

    def over_dp(x):
        gathered, bit = [x], dp_size // 2
        while bit:
            gathered, bit = gathered + [swap_dp(one, bit) for one in gathered], bit // 2
        return gathered

    table = jnp.array(device_table(n, head_size, dp_size, rows))
    info = lax.dynamic_index_in_dim(table, (z * head_size + y) * dp_size + dp, 0, False)

    keys_mine = [lax.dynamic_slice_in_dim(main_keys[0].T, y * half, half, 1)]
    keys_mine.append(onward(keys_mine[0]))
    queries = main_queries[0]
    other_queries = swap_head(queries)
    index_parts = [lax.dynamic_slice_in_dim(index_keys[0], y * half, half)] + [None] * (n - 1)
    index_parts[1] = onward(index_parts[0])
    index_parts[n - 1] = onward(index_parts[0], n - 1)
    parts, kept = project(info, queries_here, q_latent[0], w_query, hidden[0], w_weights.T)
    first_part, index_parts = lax.optimization_barrier((parts[0], index_parts))
    summed = onward(first_part) + parts[1]
    order_at = 1 + 3 * n
    dp_at = order_at + n * dp_size
    weights, tops, before = [], [], None

    def score_next(keys):
        nonlocal before
        t = len(weights)
        numer, top, *before = score(
            t, n, info, sequence_positions, queries, other_queries, keys, before
        )
        weights.append(numer)
        tops.append(top)

    index_own = index_other = None
    for t in range(1, n - 1):
        if t == 1:
            sent_on, summed, index_parts, kept = lax.optimization_barrier(
                (keys_mine[t], summed, index_parts, kept)
            )
            for k in range(2, n - 1):
                index_parts[k] = onward(index_parts[1]) if k == 2 else onward(index_parts[0], k)
            index_own = jnp.concatenate(index_parts)
            index_other = swap_head(index_own)
            over_half = swap_dp(kept, dp_size // 2)
            kept = [kept, over_half, swap_dp(kept, dp_size // 4)]
        elif t == 2:
            sent_on, summed, index_other, kept, other_queries = lax.optimization_barrier(
                (keys_mine[t], summed, index_other, kept, other_queries)
            )
            kept = kept + [swap_dp(kept[1], dp_size // 4)]
        else:
            sent_on, summed = lax.optimization_barrier((keys_mine[t], summed))
        keys_mine[t] = sent_on
        keys_mine.append(onward(sent_on))
        summed = onward(summed)
        if t + 1 < n - 1:
            summed = summed + parts[t + 1]
    received = summed
    latents, hiddens = arrange(dp_at, info, rows_latent, kept)
    other_queries, latents, hiddens = lax.optimization_barrier((other_queries, latents, hiddens))
    while len(weights) < n - 1:
        score_next(keys_mine[len(weights)])
    before, received = lax.optimization_barrier((before, received))

    part = make_logits(heads_here, received, parts[n - 1], index_own, index_other)
    probs, log_probs = make_softmax(n, info, sequence_positions, part, swap_head(part))

    before, probs, log_probs = lax.optimization_barrier((before, probs, log_probs))
    score_next(keys_mine[n - 1])
    delta_own, sent = make_delta(weights, tops, *before, swap_head(jnp.stack(before)), probs)
    piece = gradients(
        heads_here,
        n,
        received,
        parts[n - 1],
        index_own,
        index_other,
        probs,
        log_probs,
        delta_own,
        sent,
        swap_head(sent),
    )[None]

    brought = []
    for t in range(1, n):
        pairs = [(k, (k + t) % n) for k in range(n)]
        brought.append(lax.ppermute(piece, "ctx", pairs))
    own_pieces = over_dp(piece)
    brought, own_pieces = lax.optimization_barrier((jnp.concatenate(brought), own_pieces))
    brought = over_dp(brought)
    if queries_here % 16:
        flat = jnp.concatenate([jnp.concatenate([a, b]) for a, b in zip(own_pieces, brought)])
        order = jnp.argsort(info[order_at : order_at + n * dp_size])
        parts_in, order = [flat[order].reshape(1, -1, flat.shape[2])], None
    else:
        parts_in, order = own_pieces + brought, []
        order += [order_at + k * n for k in range(dp_size)]
        order += [order_at + k * n + t for k in range(dp_size) for t in range(1, n)]
    grad_query, grad_weights, losses = outer(
        heads_here,
        order,
        dp_at,
        q_latent.shape[1],
        info,
        latents,
        hiddens,
        parts_in,
    )
    return (grad_query, grad_weights.T, losses)


def solution(mesh):
    return jax.shard_map(
        per_device,
        mesh=mesh,
        in_specs=(
            P("dp", None, None),
            P("dp", None, None),
            P("dp", "ctx", "head", None),
            P("dp", "ctx", None),
            P("dp", "ctx", None),
            P("dp", None),
            P("ctx", "head"),
            P("ctx", "head"),
        ),
        out_specs=(P("ctx", "head"), P("ctx", "head"), P("dp", None)),
        check_vma=False,
    )
```

```python
import functools
import math

import jax
import jax.numpy as jnp
import numpy as np
from jax import lax
from jax.experimental import pallas as pl
from jax.experimental.pallas import tpu as pltpu
from jax.sharding import PartitionSpec as P

HI = 64
DI = 128
HM = 128

index_scale = (HI * DI) ** (-0.5)
exponent_scale = 192.0 ** (-0.5) / math.log(2.0)
masked_floor = -1e30
lanes = 128
f32 = jnp.float32
bf16 = jnp.bfloat16
vmem_limit = 24 * 2**20
group_size = 4


def params():
    return pltpu.CompilerParams(vmem_limit_bytes=vmem_limit)


def in_smem():
    return pl.BlockSpec(memory_space=pltpu.SMEM)


def in_vmem():
    return pl.BlockSpec(memory_space=pltpu.VMEM)


def times(a, b, axis_a, axis_b):
    return lax.dot_general(a, b, (((axis_a,), (axis_b,)), ((), ())), preferred_element_type=f32)


at_ctx, at_head, at_dp, at_end = 0, 1, 2, 3


def folded_ring(size):
    return [0] + list(range(1, size, 2)) + list(range(2, size, 2))[::-1]


def on_line(n):
    return n == 4


def key_source(n, z, u):
    if on_line(n):
        return ([0, 1, 2, 3], [1, 2, 0, 3], [2, 1, 3, 0], [3, 2, 1, 0])[z][u]
    ring = folded_ring(n)
    return ring[(ring.index(z) - u) % n]


def device_table(n, heads, dp_size):
    table = []
    for z in range(n):
        for y in range(heads):
            for dp in range(dp_size):
                row = [z, y, dp, int(z in (0, n - 1))]
                row += [key_source(n, z, u) for u in range(n)]
                row += [(z - key_source(n, z, u)) % n for u in range(n)]
                row += [dp ^ k for k in dp_flips(dp_size)]
                row += [(z - t) % n for t in range(n)]
                row += [k if z < n // 2 or not on_line(n) else n - 1 - k for k in range(n)]
                table.append(row)
    return np.array(table, np.int32)


def at_source(n, u):
    return 4 + u


def at_place(n, u):
    return 4 + n + u


def at_partner(n, k):
    return 4 + 2 * n + k


def at_shift(n, dp_size, t):
    return 4 + 2 * n + dp_size + t


def at_part(n, dp_size, k):
    return 4 + 3 * n + dp_size + k


def dp_flips(dp_size):
    flips, bit = [0], dp_size // 2
    while bit:
        flips, bit = flips + [k ^ bit for k in flips], bit // 2
    return flips


def project_kernel(order_at, info, latent, weight, hidden, hidden_weight, out, own, kept):
    blocks, count, _ = out.shape
    width = weight.shape[1]
    heads = hidden_weight.shape[0]
    rows, mixed_rows = latent[...], hidden[...]
    if order_at is not None:
        starts = [pl.multiple_of(info[order_at + k] * count, count) for k in range(blocks)]
        rows = jnp.concatenate([latent[pl.ds(k, count), :] for k in starts], axis=0)
        mixed_rows = jnp.concatenate([hidden[pl.ds(k, count), :] for k in starts], axis=0)
    for at in range(0, width, 512):
        product = times(rows, weight[:, at : at + 512], 1, 0)
        for k in range(blocks):
            out[k, :, at : at + 512] = product[k * count : (k + 1) * count]
    mixed = times(mixed_rows, hidden_weight[...], 1, 1)
    for k in range(blocks):
        out[k, :, width : width + heads] = mixed[k * count : (k + 1) * count]
        out[k, :, width + heads :] = jnp.zeros((count, lanes - heads), f32)
    if order_at is None:
        own[...] = jnp.zeros(own.shape, f32)
    else:
        own[...] = out[1 - info[at_end]]
    kept[:, : latent.shape[1]] = latent[...]
    kept[:, latent.shape[1] :] = hidden[...]


def project(info, order_at, count, latent, weight, hidden, hidden_weight):
    queries, width = latent.shape[0], weight.shape[1]
    depth, hidden_depth = weight.shape[0], hidden_weight.shape[1]
    blocks = queries // count
    columns = lambda i, info: (0, info[at_ctx])
    whole = lambda i, info: (0, 0)
    if depth % lanes or hidden_depth % lanes:
        latent = lax.dynamic_slice_in_dim(latent, info[at_ctx] * depth, depth, 1)
        hidden = lax.dynamic_slice_in_dim(hidden, info[at_ctx] * hidden_depth, hidden_depth, 1)
        columns = whole
    return pl.pallas_call(
        functools.partial(project_kernel, order_at),
        grid_spec=pltpu.PrefetchScalarGridSpec(
            num_scalar_prefetch=1,
            grid=(1,),
            in_specs=[
                pl.BlockSpec((queries, depth), columns),
                pl.BlockSpec((depth, width), whole),
                pl.BlockSpec((queries, hidden_depth), columns),
                pl.BlockSpec(hidden_weight.shape, whole),
            ],
            out_specs=[
                pl.BlockSpec((blocks, count, width + lanes), lambda i, info: (0, 0, 0)),
                pl.BlockSpec((count, width + lanes), whole),
                pl.BlockSpec((queries, depth + hidden_depth), whole),
            ],
        ),
        out_shape=[
            jax.ShapeDtypeStruct((blocks, count, width + lanes), f32),
            jax.ShapeDtypeStruct((count, width + lanes), f32),
            jax.ShapeDtypeStruct((queries, depth + hidden_depth), bf16),
        ],
        compiler_params=params(),
        cost_estimate=pl.CostEstimate(
            flops=2 * queries * weight.size, bytes_accessed=2 * weight.size, transcendentals=0
        ),
        name="project",
    )(info, latent, weight, hidden, hidden_weight)


def score_kernel(t, n, rows_here, info, positions, mine, other, *refs):
    options, refs = refs[:-10], refs[-10:]
    top_before, mass_before, weights, top, top_all, mass_all, mass, even, odd, chosen = refs
    count, heads, depth = mine.shape
    keys = options[0]
    if len(options) > 1:
        keys = chosen
        for k, option in enumerate(options):

            @pl.when(info[at_end] == 1 - k)
            def _():
                chosen[...] = option[...]

    base = info[at_source(n, t)] * rows_here + info[at_head] * keys.shape[1]
    limits = [positions[info[at_ctx] * count + q] - base for q in range(count)]
    span = keys.shape[1]
    key_at = lax.broadcasted_iota(jnp.int32, (1, span), 1)
    row_at = lax.broadcasted_iota(jnp.int32, (heads, lanes), 0)
    lane_at = lax.broadcasted_iota(jnp.int32, (heads, lanes), 1)
    group = min(group_size, count)
    work = [(at, k) for at in range(0, count, group) for k in range(2)]
    held = (even, odd)

    def multiply(step):
        at, k = work[step]
        rows = (mine, other)[k][at : at + group].reshape(group * heads, depth)
        held[step % 2][...] = times(rows, keys[...], 1, 0)

    multiply(0)
    for step, (at, k) in enumerate(work):
        if step + 1 < len(work):
            multiply(step + 1)
        scores = held[step % 2]
        offset = k * heads
        diagonal = lane_at == row_at + offset
        for i in range(group):
            q = at + i
            one = jnp.where(
                key_at <= limits[q], scores[i * heads : (i + 1) * heads, :], masked_floor
            )
            high = jnp.max(one, axis=1, keepdims=True)
            shifted = jnp.exp2((one - high) * exponent_scale)
            total = jnp.sum(shifted, axis=1, keepdims=True)
            weights[q, offset : offset + heads] = shifted.astype(bf16)
            high_row = jnp.sum(jnp.where(diagonal, high, 0.0), axis=0, keepdims=True)
            total_row = jnp.sum(jnp.where(diagonal, total, 0.0), axis=0, keepdims=True)
            if k == 0:
                top[q : q + 1, :] = high_row
                mass[q : q + 1, :] = total_row
            else:
                top[q : q + 1, :] += high_row
                mass[q : q + 1, :] += total_row
    if t == 0:
        top_all[...] = top[...]
        mass_all[...] = mass[...]
    else:
        before, now = top_before[...], top[...]
        joint = jnp.maximum(before, now)
        top_all[...] = joint
        mass_all[...] = mass_before[...] * jnp.exp2((before - joint) * exponent_scale) + mass[
            ...
        ] * jnp.exp2((now - joint) * exponent_scale)


def score(t, n, rows_here, info, positions, mine, other, options, before):
    count, heads, depth = mine.shape
    span = options[0].shape[1]
    stats = jax.ShapeDtypeStruct((count, lanes), f32)
    if before is None:
        before = (jnp.zeros((count, lanes), f32),) * 2
    return pl.pallas_call(
        functools.partial(score_kernel, t, n, rows_here),
        out_shape=(jax.ShapeDtypeStruct((count, 2 * heads, span), bf16), stats, stats, stats),
        in_specs=[in_smem()] * 2 + [in_vmem()] * (4 + len(options)),
        out_specs=(in_vmem(),) * 4,
        scratch_shapes=[pltpu.VMEM((count, lanes), f32)]
        + [pltpu.VMEM((min(group_size, count) * heads, span), f32)] * 2
        + [pltpu.VMEM((depth, span), bf16)],
        compiler_params=params(),
        cost_estimate=pl.CostEstimate(flops=0, bytes_accessed=0, transcendentals=0),
        name="score",
    )(info, positions, mine, other, *options, *before)


def delta_kernel(blocks, info, *refs):
    weights, tops = refs[:blocks], refs[blocks : 2 * blocks]
    top, mass, far, probs, out, sent, held = refs[2 * blocks :]
    count, heads, span = weights[0].shape
    far_top = pltpu.roll(far[0], heads // 2, 1)
    far_mass = pltpu.roll(far[1], heads // 2, 1)
    joint = jnp.maximum(top[...], far_top)
    total = mass[...] * jnp.exp2((top[...] - joint) * exponent_scale) + far_mass * jnp.exp2(
        (far_top - joint) * exponent_scale
    )
    row_at = lax.broadcasted_iota(jnp.int32, (heads, lanes), 0)
    lane_at = lax.broadcasted_iota(jnp.int32, (heads, lanes), 1)
    diagonal = row_at == lane_at
    inverse = 1.0 / (total * HM)
    for t in range(blocks):
        factor = jnp.exp2((tops[t][...] - joint) * exponent_scale) * inverse
        to = pl.ds(pl.multiple_of(info[at_place(blocks, t)] * span, span), span)
        for q in range(count):
            column = jnp.sum(
                jnp.where(diagonal, factor[q : q + 1, :], 0.0), axis=1, keepdims=True
            )
            mixed = weights[t][q].astype(f32) * column
            held[q : q + 1, to] = jnp.sum(mixed, axis=0, keepdims=True)
    delta = probs[0] - held[...]
    out[...] = delta
    sent[...] = delta.astype(bf16)


def make_delta(info, weights, tops, top, mass, far, probs):
    blocks = len(weights)
    count, heads, span = weights[0].shape
    return pl.pallas_call(
        functools.partial(delta_kernel, blocks),
        out_shape=(
            jax.ShapeDtypeStruct((count, blocks * span), f32),
            jax.ShapeDtypeStruct((count, blocks * span), bf16),
        ),
        in_specs=[in_smem()] + [in_vmem()] * (2 * blocks + 4),
        out_specs=(in_vmem(),) * 2,
        scratch_shapes=[pltpu.VMEM((count, blocks * span), f32)],
        compiler_params=params(),
        cost_estimate=pl.CostEstimate(
            flops=2 * blocks * count * heads * span,
            bytes_accessed=2 * blocks * count * heads * span,
            transcendentals=0,
        ),
        name="delta",
    )(info, *weights, *tops, top, mass, far, probs)


def query_rows(total, heads):
    return jnp.concatenate(
        [total[:, j * DI : (j + 1) * DI].astype(bf16) for j in range(heads)], axis=0
    )


def summed(terms):
    total = terms[0][...]
    for one in terms[1:]:
        total = total + one[...]
    return total


def logits_kernel(heads, *refs):
    terms, (own, other, out) = refs[:-3], refs[-3:]
    total = summed(terms)
    count = total.shape[0]
    query = query_rows(total, heads)
    columns = [total[:, heads * DI + j : heads * DI + j + 1] for j in range(heads)]
    span = 512
    for part, keys in enumerate((own, other)):
        for at in range(0, keys.shape[0], span):
            affinity = times(query, keys[at : at + span, :], 1, 1)
            running = jnp.zeros((count, span), f32)
            for j in range(heads):
                reached = jnp.maximum(affinity[j * count : (j + 1) * count], 0.0)
                running = running + columns[j] * reached
            out[part, :, at : at + span] = running * index_scale


def make_logits(heads, terms, own, other):
    count, length = terms[0].shape[0], own.shape[0]
    return pl.pallas_call(
        functools.partial(logits_kernel, heads),
        out_shape=jax.ShapeDtypeStruct((2, count, length), f32),
        in_specs=[in_vmem()] * (2 + len(terms)),
        out_specs=in_vmem(),
        compiler_params=params(),
        cost_estimate=pl.CostEstimate(flops=0, bytes_accessed=0, transcendentals=0),
        name="logits",
    )(*terms, own, other)


def softmax_kernel(blocks, rows_here, shift_at, info, positions, part, far, probs, log_probs):
    _, count, length = part.shape
    span = length // blocks
    row_at = lax.broadcasted_iota(jnp.int32, (count, lanes), 0)
    position = jnp.zeros((count, lanes), jnp.int32)
    for q in range(count):
        position = jnp.where(row_at == q, positions[info[at_ctx] * count + q], position)
    position = position[:, 0:1]
    key_at = lax.broadcasted_iota(jnp.int32, (count, span), 1)

    def seen(side, t):
        half = info[at_head] if side == 0 else 1 - info[at_head]
        return key_at + (info[shift_at + t] * rows_here + half * span) <= position

    highs = []
    for side in range(2):
        high = jnp.full((count, span), masked_floor, f32)
        for t in range(blocks):
            at = slice(t * span, (t + 1) * span)
            value = part[side, :, at] + far[1 - side, :, at]
            log_probs[side, :, at] = value
            high = jnp.maximum(high, jnp.where(seen(side, t), value, masked_floor))
        highs.append(jnp.max(high, axis=1, keepdims=True))
    high = jnp.maximum(highs[0], highs[1])
    sums = []
    for side in range(2):
        running = jnp.zeros((count, span), f32)
        for t in range(blocks):
            at = slice(t * span, (t + 1) * span)
            grown = jnp.where(seen(side, t), jnp.exp(log_probs[side, :, at] - high), 0.0)
            probs[side, :, at] = grown
            running = running + grown
        sums.append(jnp.sum(running, axis=1, keepdims=True))
    mass = sums[0] + sums[1]
    level = high + jnp.log(mass)
    inverse = 1.0 / mass
    for side in range(2):
        for t in range(blocks):
            at = slice(t * span, (t + 1) * span)
            probs[side, :, at] = probs[side, :, at] * inverse
            log_probs[side, :, at] = jnp.where(seen(side, t), log_probs[side, :, at] - level, 0.0)


def make_softmax(blocks, rows_here, shift_at, info, positions, part, far):
    return pl.pallas_call(
        functools.partial(softmax_kernel, blocks, rows_here, shift_at),
        out_shape=(jax.ShapeDtypeStruct(part.shape, f32),) * 2,
        in_specs=[in_smem()] * 2 + [in_vmem()] * 2,
        out_specs=(in_vmem(),) * 2,
        compiler_params=params(),
        cost_estimate=pl.CostEstimate(flops=0, bytes_accessed=0, transcendentals=0),
        name="softmax",
    )(info, positions, part, far)


def gradient_kernel(
    heads,
    blocks,
    *refs,
):
    terms, refs = refs[:-13], refs[-13:]
    own, other, probs, log_probs, delta_own, sent, brought, out = refs[:8]
    flow, query_sum, grads, even, odd = refs[8:]
    total = summed(terms)
    count = total.shape[0]
    span = own.shape[0] // blocks
    query = query_rows(total, heads)
    columns = [
        total[:, heads * DI + j : heads * DI + j + 1] * index_scale for j in range(heads)
    ]
    work = [(side, t) for side in range(2) for t in range(blocks)]
    held = (even, odd)

    def multiply(step):
        side, t = work[step]
        keys = (own, other)[side][t * span : (t + 1) * span, :]
        held[step % 2][...] = times(query, keys, 1, 1)

    multiply(0)
    flow[...] = jnp.zeros(flow.shape, f32)
    running = [jnp.zeros((count, span), f32)] * 2
    for step, (side, t) in enumerate(work):
        if step + 1 < len(work):
            multiply(step + 1)
        at = slice(t * span, (t + 1) * span)
        affinity = held[step % 2]
        rounded = (sent, brought)[side][:, at].astype(f32)
        delta = delta_own[:, at] if side == 0 else rounded
        wanted = probs[side, :, at] - rounded
        running[side] = running[side] + wanted * log_probs[side, :, at]
        for j in range(heads):
            rows = slice(j * count, (j + 1) * count)
            one = affinity[rows, :]
            reached = jnp.where(one > 0, delta, 0.0)
            grads[rows, :] = (reached * columns[j]).astype(bf16)
            product = reached * one
            folded = product[:, :lanes]
            for k in range(lanes, span, lanes):
                folded = folded + product[:, k : k + lanes]
            flow[rows, :] += folded
        keys = (own, other)[side][at, :]
        product = times(grads[...], keys, 1, 0)
        if step == 0:
            query_sum[...] = product
        else:
            query_sum[...] += product
    losses = [jnp.sum(one, axis=1, keepdims=True) for one in running]
    loss = -(losses[0] + losses[1])
    lane_at = lax.broadcasted_iota(jnp.int32, (count, lanes), 1)
    tail = jnp.zeros((count, lanes), f32)
    for j in range(heads):
        rows = slice(j * count, (j + 1) * count)
        out[:, j * DI : (j + 1) * DI] = query_sum[rows, :].astype(bf16)
        column = jnp.sum(flow[rows, :], axis=1, keepdims=True) * index_scale
        tail = jnp.where(lane_at == j, column, tail)
    loss_high = loss.astype(bf16).astype(f32)
    tail = jnp.where(lane_at == heads, loss_high, tail)
    tail = jnp.where(lane_at == heads + 1, loss - loss_high, tail)
    out[:, heads * DI :] = tail.astype(bf16)


def gradients(heads, blocks, terms, own, other, probs, log_probs, delta_own, sent, brought):
    count, length = terms[0].shape[0], own.shape[0]
    span = length // blocks
    return pl.pallas_call(
        functools.partial(gradient_kernel, heads, blocks),
        out_shape=jax.ShapeDtypeStruct((count, heads * DI + lanes), bf16),
        in_specs=[in_vmem()] * (7 + len(terms)),
        out_specs=in_vmem(),
        scratch_shapes=[
            pltpu.VMEM((heads * count, lanes), f32),
            pltpu.VMEM((heads * count, DI), f32),
            pltpu.VMEM((heads * count, span), bf16),
            pltpu.VMEM((heads * count, span), f32),
            pltpu.VMEM((heads * count, span), f32),
        ],
        compiler_params=params(),
        cost_estimate=pl.CostEstimate(
            flops=8 * count * heads * DI * length,
            bytes_accessed=4 * (terms[0].size + 6 * count * length) + 4 * length * DI,
            transcendentals=0,
        ),
        name="gradient",
    )(*terms, own, other, probs, log_probs, delta_own, sent, brought)


def arrange_kernel(n, info, *refs):
    kept, (latents, hiddens, held) = refs[:-3], refs[-3:]
    queries, depth = kept[0].shape[0], latents.shape[0]
    for k, one in enumerate(kept):
        to = pl.ds(pl.multiple_of(info[at_partner(n, k)] * queries, queries), queries)
        held[to, :] = one[:, :depth].astype(f32)
        hiddens[to, :] = one[:, depth:]
    latents[...] = held[...].T.astype(bf16)


def arrange(n, info, depth, kept):
    queries, width = kept[0].shape
    total = queries * len(kept)
    return pl.pallas_call(
        functools.partial(arrange_kernel, n),
        out_shape=(
            jax.ShapeDtypeStruct((depth, total), bf16),
            jax.ShapeDtypeStruct((total, width - depth), bf16),
        ),
        in_specs=[in_smem()] + [in_vmem()] * len(kept),
        out_specs=(in_vmem(),) * 2,
        scratch_shapes=[pltpu.VMEM((total, depth), f32)],
        compiler_params=params(),
        cost_estimate=pl.CostEstimate(
            flops=0, bytes_accessed=4 * total * width, transcendentals=0
        ),
        name="arrange",
    )(info, *kept)


def outer_kernel(heads, n, order, info, latents, hiddens, *refs):
    parts, (grad, grad_mixed, losses, rows, blocks, sems) = refs[:-6], refs[-6:]
    count = parts[0].shape[-2]
    width = heads * DI
    steps, _, span = blocks.shape
    k = 0
    for part in parts:
        for t in range(part.shape[0]):
            to = 0
            if order is not None:
                to = pl.multiple_of((info[order[k][0]] * n + info[order[k][1]]) * count, count)
            rows[pl.ds(to, count), :] = part[t]
            k += 1
    copies = []
    for i in range(steps):
        at = slice(i * span, (i + 1) * span)
        blocks[i] = times(latents[...], rows[:, at], 1, 0)
        copies.append(pltpu.make_async_copy(blocks.at[i], grad.at[:, at], sems.at[i]))
        copies[-1].start()
    tails = rows[:, width:]
    grad_mixed[...] = times(tails, hiddens[...], 0, 0)[:heads]
    own = losses.shape[1]
    from_own = rows[pl.ds(pl.multiple_of(info[at_dp] * own, own), own), width:].astype(f32)
    column = from_own[:, heads : heads + 1] + from_own[:, heads + 1 : heads + 2]
    diagonal = lax.broadcasted_iota(jnp.int32, (own, own), 0) == lax.broadcasted_iota(
        jnp.int32, (own, own), 1
    )
    losses[...] = jnp.sum(jnp.where(diagonal, column, 0.0), axis=0, keepdims=True)
    for copy in copies:
        copy.wait()


def outer(heads, n, order, queries, info, latents, hiddens, parts):
    row_count, total = latents.shape
    width = heads * DI
    steps = 8
    hidden_count = hiddens.shape[1]
    return pl.pallas_call(
        functools.partial(outer_kernel, heads, n, order),
        out_shape=(
            jax.ShapeDtypeStruct((row_count, width), f32),
            jax.ShapeDtypeStruct((heads, hidden_count), f32),
            jax.ShapeDtypeStruct((1, queries), f32),
        ),
        in_specs=[in_smem()] + [in_vmem()] * (2 + len(parts)),
        out_specs=(pl.BlockSpec(memory_space=pl.ANY), in_vmem(), in_vmem()),
        scratch_shapes=[
            pltpu.VMEM((total, width + lanes), bf16),
            pltpu.VMEM((steps, row_count, width // steps), f32),
            pltpu.SemaphoreType.DMA((steps,)),
        ],
        compiler_params=params(),
        cost_estimate=pl.CostEstimate(
            flops=2 * total * row_count * width,
            bytes_accessed=4 * row_count * width + 2 * total * width,
            transcendentals=0,
        ),
        name="outer",
    )(info, latents, hiddens, *parts)


def per_device(
    q_latent, hidden, main_queries, main_keys, index_keys, positions, w_query, w_weights
):
    n = lax.axis_size("ctx")
    z = lax.axis_index("ctx")
    head_size = lax.axis_size("head")
    y = lax.axis_index("head")
    dp_size = lax.axis_size("dp")
    dp = lax.axis_index("dp")
    rows = main_keys.shape[1]
    half = rows // head_size
    rows_latent = w_query.shape[0]
    heads_here = w_weights.shape[1]
    queries_here = main_queries.shape[1]

    def shifted(x, t):
        return lax.ppermute(x, "ctx", [(k, (k + t) % n) for k in range(n)])

    def outward(x):
        return lax.ppermute(x, "ctx", [(1, 0), (2, 3)])

    def centre(x):
        return lax.ppermute(x, "ctx", [(1, 2), (2, 1)])

    def inward(x):
        return lax.ppermute(x, "ctx", [(0, 1), (3, 2)])

    def after(waited, *held):
        nonlocal token
        token, waited, held = lax.optimization_barrier((token, waited, held))
        return waited, *held

    def swap_head(x):
        return lax.ppermute(x, "head", [(0, 1), (1, 0)])

    def swap_dp(x, bit):
        return lax.ppermute(x, "dp", [(k, k ^ bit) for k in range(dp_size)])

    def over_dp(x):
        gathered, bit = [x], dp_size // 2
        while bit:
            gathered, bit = gathered + [swap_dp(one, bit) for one in gathered], bit // 2
        return gathered

    table = jnp.array(device_table(n, head_size, dp_size))
    info = lax.dynamic_index_in_dim(table, (z * head_size + y) * dp_size + dp, 0, False)

    token = positions[0]
    queries = main_queries[0]
    own_keys = lax.dynamic_slice_in_dim(main_keys[0].T, y * half, half, 1)
    index_part = lax.dynamic_slice_in_dim(index_keys[0], y * half, half)
    line = on_line(n)
    order_at = at_part(n, dp_size, 0) if line else None
    weights, tops, before = [], [], None

    def score_next(*options):
        nonlocal before
        t = len(weights)
        numer, top, *before = score(
            t, n, rows, info, token, queries, other_queries, options, before
        )
        weights.append(numer)
        tops.append(top)

    if line:
        index_1, index_3 = shifted(index_part, 1), shifted(index_part, 3)
        keys_out, keys_over, keys_in = outward(own_keys), centre(own_keys), inward(own_keys)
        partial, own_part, kept = project(
            info, order_at, queries_here, q_latent[0], w_query, hidden[0], w_weights.T
        )
        (index_1, index_3), sent_queries = after((index_1, index_3), queries)
        other_queries = swap_head(sent_queries)
        _, far_part = after((), partial[3])
        far_in = inward(far_part)
        (keys_out, keys_over, keys_in), index_again = after(
            (keys_out, keys_over, keys_in), index_part
        )
        keys_out2, keys_over2 = outward(keys_over), centre(keys_in)
        index_2 = shifted(index_again, 2)
        (far_in,) = after(far_in)
        far_over = centre(far_part + far_in)
        index_2, near_parts = after(index_2, partial[1:3])
        near_in = inward(near_parts)
        (far_over, other_queries), kept = after((far_over, other_queries), kept)
        sum_out = outward(partial[0] + far_over)
        half_dp, near_dp = swap_dp(kept, dp_size // 2), swap_dp(kept, dp_size // 4)
        index_own = jnp.concatenate([index_part, index_1, index_2, index_3])
        (keys_out2, keys_over2, sum_out, near_in, half_dp, near_dp), index_own = after(
            (keys_out2, keys_over2, sum_out, near_in, half_dp, near_dp), index_own
        )
        keys_out3 = outward(keys_over2)
        sum_over = centre(partial[2] + near_in[1])
        index_other = swap_head(index_own)
        kept = [kept, half_dp, near_dp, swap_dp(half_dp, dp_size // 4)]
        score_next(own_keys)
        score_next(keys_out, keys_over)
        latents, hiddens = arrange(n, info, rows_latent, kept)
        before, latents, hiddens = lax.optimization_barrier((before, latents, hiddens))
        score_next(keys_out2, keys_in)
        before, sum_out, sum_over, near_in = lax.optimization_barrier(
            (before, sum_out, sum_over, near_in)
        )
        terms = [own_part, sum_out, sum_over, near_in[0]]
        last_keys = (keys_out3, keys_over2)
    else:
        ring = folded_ring(n)
        partial, _, kept = project(
            info, order_at, queries_here, q_latent[0], w_query, hidden[0], w_weights.T
        )
        terms = [jnp.sum(lax.all_to_all(partial, "ctx", 0, 0), axis=0)]
        other_queries = swap_head(queries)
        index_own = jnp.concatenate([index_part] + [shifted(index_part, t) for t in range(1, n)])
        index_other = swap_head(index_own)
        latents, hiddens = arrange(n, info, rows_latent, over_dp(kept))
        keys = own_keys
        for _ in range(n - 1):
            score_next(keys)
            keys = lax.ppermute(keys, "ctx", [(ring[k], ring[(k + 1) % n]) for k in range(n)])
        last_keys = (keys,)

    part = make_logits(heads_here, terms, index_own, index_other)
    probs, log_probs = make_softmax(
        n, rows, at_shift(n, dp_size, 0), info, token, part, swap_head(part)
    )
    before, probs, log_probs = lax.optimization_barrier((before, probs, log_probs))
    score_next(*last_keys)
    delta_own, sent = make_delta(info, weights, tops, *before, swap_head(jnp.stack(before)), probs)
    piece = gradients(
        heads_here,
        n,
        terms,
        index_own,
        index_other,
        probs,
        log_probs,
        delta_own,
        sent,
        swap_head(sent),
    )[None]

    brought = []
    for t in range(1, n):
        pairs = [(k, (k + t) % n) for k in range(n)]
        brought.append(lax.ppermute(piece, "ctx", pairs))
    own_pieces = over_dp(piece)
    brought, own_pieces = lax.optimization_barrier((jnp.concatenate(brought), own_pieces))
    brought = over_dp(brought)
    parts_in = own_pieces + brought
    order = [(at_partner(n, k), at_shift(n, dp_size, 0)) for k in range(dp_size)]
    order += [
        (at_partner(n, k), at_shift(n, dp_size, t)) for k in range(dp_size) for t in range(1, n)
    ]
    if queries_here % 16:
        places = jnp.stack([info[a] * n + info[b] for a, b in order])
        flat = jnp.concatenate(parts_in)[jnp.argsort(places)]
        parts_in, order = [flat.reshape(1, -1, flat.shape[2])], None
    grad_query, grad_weights, losses = outer(
        heads_here, n, order, q_latent.shape[1], info, latents, hiddens, parts_in
    )
    return (grad_query, grad_weights.T, losses)


def solution(mesh):
    return jax.shard_map(
        per_device,
        mesh=mesh,
        in_specs=(
            P("dp", None, None),
            P("dp", None, None),
            P("dp", "ctx", "head", None),
            P("dp", "ctx", None),
            P("dp", "ctx", None),
            P("dp", None),
            P("ctx", "head"),
            P("ctx", "head"),
        ),
        out_specs=(P("ctx", "head"), P("ctx", "head"), P("dp", None)),
        check_vma=False,
    )
```

```python
import functools
import math

import jax
import jax.numpy as jnp
import numpy as np
from jax import lax
from jax.experimental import pallas as pl
from jax.experimental.pallas import tpu as pltpu
from jax.sharding import PartitionSpec as P

HI = 64
DI = 128
HM = 128

index_scale = (HI * DI) ** (-0.5)
exponent_scale = 192.0 ** (-0.5) / math.log(2.0)
masked_floor = -1e30
lanes = 128
f32 = jnp.float32
bf16 = jnp.bfloat16
vmem_limit = 24 * 2**20
group_size = 4


def params():
    return pltpu.CompilerParams(vmem_limit_bytes=vmem_limit)


def in_smem():
    return pl.BlockSpec(memory_space=pltpu.SMEM)


def in_vmem():
    return pl.BlockSpec(memory_space=pltpu.VMEM)


def times(a, b, axis_a, axis_b):
    return lax.dot_general(a, b, (((axis_a,), (axis_b,)), ((), ())), preferred_element_type=f32)


at_ctx, at_head, at_dp, at_end = 0, 1, 2, 3


def folded_ring(size):
    return [0] + list(range(1, size, 2)) + list(range(2, size, 2))[::-1]


def on_line(n):
    return n == 4


left_1, right_1, left_2, right_2, last = range(5)
line_sources = ((0, 1, 2, 3), (1, 2, 3, 0), (2, 1, 0, 3), (3, 2, 1, 0))
line_options = ((left_1, right_1), (left_2, right_2), (last, right_1, left_1))
line_brought = ((left_1, left_2, last), (left_1, left_2, right_1), (right_1, right_2, left_1), (right_1, right_2, last))


def key_source(n, z, u):
    if on_line(n):
        return line_sources[z][u]
    ring = folded_ring(n)
    return ring[(ring.index(z) - u) % n]


def key_option(n, z, u):
    if u == 0 or not on_line(n):
        return 0
    return line_options[u - 1].index(line_brought[z][u - 1])


def device_table(n, heads, dp_size):
    table = []
    for z in range(n):
        for y in range(heads):
            for dp in range(dp_size):
                row = [z, y, dp, int(z in (0, n - 1))]
                row += [key_source(n, z, u) for u in range(n)]
                row += [(z - key_source(n, z, u)) % n for u in range(n)]
                row += [dp ^ k for k in dp_flips(dp_size)]
                row += [(z - t) % n for t in range(n)]
                row += [k if z < n // 2 or not on_line(n) else n - 1 - k for k in range(n)]
                row += [key_option(n, z, u) for u in range(n)]
                table.append(row)
    return np.array(table, np.int32)


def at_source(n, u):
    return 4 + u


def at_place(n, u):
    return 4 + n + u


def at_partner(n, k):
    return 4 + 2 * n + k


def at_shift(n, dp_size, t):
    return 4 + 2 * n + dp_size + t


def at_part(n, dp_size, k):
    return 4 + 3 * n + dp_size + k


def at_option(n, dp_size, u):
    return 4 + 4 * n + dp_size + u


def dp_flips(dp_size):
    flips, bit = [0], dp_size // 2
    while bit:
        flips, bit = flips + [k ^ bit for k in flips], bit // 2
    return flips


def project_kernel(order_at, info, latent, weight, hidden, hidden_weight, out, own, kept):
    blocks, count, _ = out.shape
    width = weight.shape[1]
    heads = hidden_weight.shape[0]
    rows, mixed_rows = latent[...], hidden[...]
    if order_at is not None:
        starts = [pl.multiple_of(info[order_at + k] * count, count) for k in range(blocks)]
        rows = jnp.concatenate([latent[pl.ds(k, count), :] for k in starts], axis=0)
        mixed_rows = jnp.concatenate([hidden[pl.ds(k, count), :] for k in starts], axis=0)
    for at in range(0, width, 512):
        product = times(rows, weight[:, at : at + 512], 1, 0)
        for k in range(blocks):
            out[k, :, at : at + 512] = product[k * count : (k + 1) * count]
    mixed = times(mixed_rows, hidden_weight[...], 1, 1)
    for k in range(blocks):
        out[k, :, width : width + heads] = mixed[k * count : (k + 1) * count]
        out[k, :, width + heads :] = jnp.zeros((count, lanes - heads), f32)
    if order_at is None:
        own[...] = jnp.zeros(own.shape, f32)
    else:
        own[...] = out[1 - info[at_end]]
    kept[:, : latent.shape[1]] = latent[...]
    kept[:, latent.shape[1] :] = hidden[...]


def project(info, order_at, count, latent, weight, hidden, hidden_weight):
    queries, width = latent.shape[0], weight.shape[1]
    depth, hidden_depth = weight.shape[0], hidden_weight.shape[1]
    blocks = queries // count
    columns = lambda i, info: (0, info[at_ctx])
    whole = lambda i, info: (0, 0)
    if depth % lanes or hidden_depth % lanes:
        latent = lax.dynamic_slice_in_dim(latent, info[at_ctx] * depth, depth, 1)
        hidden = lax.dynamic_slice_in_dim(hidden, info[at_ctx] * hidden_depth, hidden_depth, 1)
        columns = whole
    return pl.pallas_call(
        functools.partial(project_kernel, order_at),
        grid_spec=pltpu.PrefetchScalarGridSpec(
            num_scalar_prefetch=1,
            grid=(1,),
            in_specs=[
                pl.BlockSpec((queries, depth), columns),
                pl.BlockSpec((depth, width), whole),
                pl.BlockSpec((queries, hidden_depth), columns),
                pl.BlockSpec(hidden_weight.shape, whole),
            ],
            out_specs=[
                pl.BlockSpec((blocks, count, width + lanes), lambda i, info: (0, 0, 0)),
                pl.BlockSpec((count, width + lanes), whole),
                pl.BlockSpec((queries, depth + hidden_depth), whole),
            ],
        ),
        out_shape=[
            jax.ShapeDtypeStruct((blocks, count, width + lanes), f32),
            jax.ShapeDtypeStruct((count, width + lanes), f32),
            jax.ShapeDtypeStruct((queries, depth + hidden_depth), bf16),
        ],
        compiler_params=params(),
        cost_estimate=pl.CostEstimate(
            flops=2 * queries * weight.size, bytes_accessed=2 * weight.size, transcendentals=0
        ),
        name="project",
    )(info, latent, weight, hidden, hidden_weight)


def score_kernel(t, n, rows_here, option_at, info, positions, mine, other, *refs):
    options, refs = refs[:-10], refs[-10:]
    top_before, mass_before, weights, top, top_all, mass_all, mass, even, odd, chosen = refs
    count, heads, depth = mine.shape
    keys = options[0]
    if len(options) > 1:
        keys = chosen
        for k, option in enumerate(options):

            @pl.when(info[option_at] == k)
            def _():
                chosen[...] = option[...]

    base = info[at_source(n, t)] * rows_here + info[at_head] * keys.shape[1]
    limits = [positions[info[at_ctx] * count + q] - base for q in range(count)]
    span = keys.shape[1]
    key_at = lax.broadcasted_iota(jnp.int32, (1, span), 1)
    row_at = lax.broadcasted_iota(jnp.int32, (heads, lanes), 0)
    lane_at = lax.broadcasted_iota(jnp.int32, (heads, lanes), 1)
    group = min(group_size, count)
    work = [(at, k) for at in range(0, count, group) for k in range(2)]
    held = (even, odd)

    def multiply(step):
        at, k = work[step]
        rows = (mine, other)[k][at : at + group].reshape(group * heads, depth)
        held[step % 2][...] = times(rows, keys[...], 1, 0)

    multiply(0)
    for step, (at, k) in enumerate(work):
        if step + 1 < len(work):
            multiply(step + 1)
        scores = held[step % 2]
        offset = k * heads
        diagonal = lane_at == row_at + offset
        for i in range(group):
            q = at + i
            one = jnp.where(
                key_at <= limits[q], scores[i * heads : (i + 1) * heads, :], masked_floor
            )
            high = jnp.max(one, axis=1, keepdims=True)
            shifted = jnp.exp2((one - high) * exponent_scale)
            total = jnp.sum(shifted, axis=1, keepdims=True)
            weights[q, offset : offset + heads] = shifted.astype(bf16)
            high_row = jnp.sum(jnp.where(diagonal, high, 0.0), axis=0, keepdims=True)
            total_row = jnp.sum(jnp.where(diagonal, total, 0.0), axis=0, keepdims=True)
            if k == 0:
                top[q : q + 1, :] = high_row
                mass[q : q + 1, :] = total_row
            else:
                top[q : q + 1, :] += high_row
                mass[q : q + 1, :] += total_row
    if t == 0:
        top_all[...] = top[...]
        mass_all[...] = mass[...]
    else:
        before, now = top_before[...], top[...]
        joint = jnp.maximum(before, now)
        top_all[...] = joint
        mass_all[...] = mass_before[...] * jnp.exp2((before - joint) * exponent_scale) + mass[
            ...
        ] * jnp.exp2((now - joint) * exponent_scale)


def score(t, n, rows_here, option_at, info, positions, mine, other, options, before):
    count, heads, depth = mine.shape
    span = options[0].shape[1]
    stats = jax.ShapeDtypeStruct((count, lanes), f32)
    if before is None:
        before = (jnp.zeros((count, lanes), f32),) * 2
    return pl.pallas_call(
        functools.partial(score_kernel, t, n, rows_here, option_at),
        out_shape=(jax.ShapeDtypeStruct((count, 2 * heads, span), bf16), stats, stats, stats),
        in_specs=[in_smem()] * 2 + [in_vmem()] * (4 + len(options)),
        out_specs=(in_vmem(),) * 4,
        scratch_shapes=[pltpu.VMEM((count, lanes), f32)]
        + [pltpu.VMEM((min(group_size, count) * heads, span), f32)] * 2
        + [pltpu.VMEM((depth, span), bf16)],
        compiler_params=params(),
        cost_estimate=pl.CostEstimate(flops=0, bytes_accessed=0, transcendentals=0),
        name="score",
    )(info, positions, mine, other, *options, *before)


def delta_kernel(blocks, info, *refs):
    weights, tops = refs[:blocks], refs[blocks : 2 * blocks]
    top, mass, far, probs, out, sent, held = refs[2 * blocks :]
    count, heads, span = weights[0].shape
    far_top = pltpu.roll(far[0], heads // 2, 1)
    far_mass = pltpu.roll(far[1], heads // 2, 1)
    joint = jnp.maximum(top[...], far_top)
    total = mass[...] * jnp.exp2((top[...] - joint) * exponent_scale) + far_mass * jnp.exp2(
        (far_top - joint) * exponent_scale
    )
    row_at = lax.broadcasted_iota(jnp.int32, (heads, lanes), 0)
    lane_at = lax.broadcasted_iota(jnp.int32, (heads, lanes), 1)
    diagonal = row_at == lane_at
    inverse = 1.0 / (total * HM)
    for t in range(blocks):
        factor = jnp.exp2((tops[t][...] - joint) * exponent_scale) * inverse
        to = pl.ds(pl.multiple_of(info[at_place(blocks, t)] * span, span), span)
        for q in range(count):
            column = jnp.sum(
                jnp.where(diagonal, factor[q : q + 1, :], 0.0), axis=1, keepdims=True
            )
            mixed = weights[t][q].astype(f32) * column
            held[q : q + 1, to] = jnp.sum(mixed, axis=0, keepdims=True)
    delta = probs[0] - held[...]
    out[...] = delta
    sent[...] = delta.astype(bf16)


def make_delta(info, weights, tops, top, mass, far, probs):
    blocks = len(weights)
    count, heads, span = weights[0].shape
    return pl.pallas_call(
        functools.partial(delta_kernel, blocks),
        out_shape=(
            jax.ShapeDtypeStruct((count, blocks * span), f32),
            jax.ShapeDtypeStruct((count, blocks * span), bf16),
        ),
        in_specs=[in_smem()] + [in_vmem()] * (2 * blocks + 4),
        out_specs=(in_vmem(),) * 2,
        scratch_shapes=[pltpu.VMEM((count, blocks * span), f32)],
        compiler_params=params(),
        cost_estimate=pl.CostEstimate(
            flops=2 * blocks * count * heads * span,
            bytes_accessed=2 * blocks * count * heads * span,
            transcendentals=0,
        ),
        name="delta",
    )(info, *weights, *tops, top, mass, far, probs)


def query_rows(total, heads):
    return jnp.concatenate(
        [total[:, j * DI : (j + 1) * DI].astype(bf16) for j in range(heads)], axis=0
    )


def summed(terms):
    total = terms[0][...]
    for one in terms[1:]:
        total = total + one[...]
    return total


def logits_kernel(heads, *refs):
    terms, (own, other, out) = refs[:-3], refs[-3:]
    total = summed(terms)
    count = total.shape[0]
    query = query_rows(total, heads)
    columns = [total[:, heads * DI + j : heads * DI + j + 1] for j in range(heads)]
    span = 512
    for part, keys in enumerate((own, other)):
        for at in range(0, keys.shape[0], span):
            affinity = times(query, keys[at : at + span, :], 1, 1)
            running = jnp.zeros((count, span), f32)
            for j in range(heads):
                reached = jnp.maximum(affinity[j * count : (j + 1) * count], 0.0)
                running = running + columns[j] * reached
            out[part, :, at : at + span] = running * index_scale


def make_logits(heads, terms, own, other):
    count, length = terms[0].shape[0], own.shape[0]
    return pl.pallas_call(
        functools.partial(logits_kernel, heads),
        out_shape=jax.ShapeDtypeStruct((2, count, length), f32),
        in_specs=[in_vmem()] * (2 + len(terms)),
        out_specs=in_vmem(),
        compiler_params=params(),
        cost_estimate=pl.CostEstimate(flops=0, bytes_accessed=0, transcendentals=0),
        name="logits",
    )(*terms, own, other)


def softmax_kernel(blocks, rows_here, shift_at, info, positions, part, far, probs, log_probs):
    _, count, length = part.shape
    span = length // blocks
    row_at = lax.broadcasted_iota(jnp.int32, (count, lanes), 0)
    position = jnp.zeros((count, lanes), jnp.int32)
    for q in range(count):
        position = jnp.where(row_at == q, positions[info[at_ctx] * count + q], position)
    position = position[:, 0:1]
    key_at = lax.broadcasted_iota(jnp.int32, (count, span), 1)

    def seen(side, t):
        half = info[at_head] if side == 0 else 1 - info[at_head]
        return key_at + (info[shift_at + t] * rows_here + half * span) <= position

    highs = []
    for side in range(2):
        high = jnp.full((count, span), masked_floor, f32)
        for t in range(blocks):
            at = slice(t * span, (t + 1) * span)
            value = part[side, :, at] + far[1 - side, :, at]
            log_probs[side, :, at] = value
            high = jnp.maximum(high, jnp.where(seen(side, t), value, masked_floor))
        highs.append(jnp.max(high, axis=1, keepdims=True))
    high = jnp.maximum(highs[0], highs[1])
    sums = []
    for side in range(2):
        running = jnp.zeros((count, span), f32)
        for t in range(blocks):
            at = slice(t * span, (t + 1) * span)
            grown = jnp.where(seen(side, t), jnp.exp(log_probs[side, :, at] - high), 0.0)
            probs[side, :, at] = grown
            running = running + grown
        sums.append(jnp.sum(running, axis=1, keepdims=True))
    mass = sums[0] + sums[1]
    level = high + jnp.log(mass)
    inverse = 1.0 / mass
    for side in range(2):
        for t in range(blocks):
            at = slice(t * span, (t + 1) * span)
            probs[side, :, at] = probs[side, :, at] * inverse
            log_probs[side, :, at] = jnp.where(seen(side, t), log_probs[side, :, at] - level, 0.0)


def make_softmax(blocks, rows_here, shift_at, info, positions, part, far):
    return pl.pallas_call(
        functools.partial(softmax_kernel, blocks, rows_here, shift_at),
        out_shape=(jax.ShapeDtypeStruct(part.shape, f32),) * 2,
        in_specs=[in_smem()] * 2 + [in_vmem()] * 2,
        out_specs=(in_vmem(),) * 2,
        compiler_params=params(),
        cost_estimate=pl.CostEstimate(flops=0, bytes_accessed=0, transcendentals=0),
        name="softmax",
    )(info, positions, part, far)


def gradient_kernel(
    heads,
    blocks,
    *refs,
):
    terms, refs = refs[:-13], refs[-13:]
    own, other, probs, log_probs, delta_own, sent, brought, out = refs[:8]
    flow, query_sum, grads, even, odd = refs[8:]
    total = summed(terms)
    count = total.shape[0]
    span = own.shape[0] // blocks
    query = query_rows(total, heads)
    columns = [
        total[:, heads * DI + j : heads * DI + j + 1] * index_scale for j in range(heads)
    ]
    work = [(side, t) for side in range(2) for t in range(blocks)]
    held = (even, odd)

    def multiply(step):
        side, t = work[step]
        keys = (own, other)[side][t * span : (t + 1) * span, :]
        held[step % 2][...] = times(query, keys, 1, 1)

    multiply(0)
    flow[...] = jnp.zeros(flow.shape, f32)
    running = [jnp.zeros((count, span), f32)] * 2
    for step, (side, t) in enumerate(work):
        if step + 1 < len(work):
            multiply(step + 1)
        at = slice(t * span, (t + 1) * span)
        affinity = held[step % 2]
        rounded = (sent, brought)[side][:, at].astype(f32)
        delta = delta_own[:, at] if side == 0 else rounded
        wanted = probs[side, :, at] - rounded
        running[side] = running[side] + wanted * log_probs[side, :, at]
        for j in range(heads):
            rows = slice(j * count, (j + 1) * count)
            one = affinity[rows, :]
            reached = jnp.where(one > 0, delta, 0.0)
            grads[rows, :] = (reached * columns[j]).astype(bf16)
            product = reached * one
            folded = product[:, :lanes]
            for k in range(lanes, span, lanes):
                folded = folded + product[:, k : k + lanes]
            flow[rows, :] += folded
        keys = (own, other)[side][at, :]
        product = times(grads[...], keys, 1, 0)
        if step == 0:
            query_sum[...] = product
        else:
            query_sum[...] += product
    losses = [jnp.sum(one, axis=1, keepdims=True) for one in running]
    loss = -(losses[0] + losses[1])
    lane_at = lax.broadcasted_iota(jnp.int32, (count, lanes), 1)
    tail = jnp.zeros((count, lanes), f32)
    for j in range(heads):
        rows = slice(j * count, (j + 1) * count)
        out[:, j * DI : (j + 1) * DI] = query_sum[rows, :].astype(bf16)
        column = jnp.sum(flow[rows, :], axis=1, keepdims=True) * index_scale
        tail = jnp.where(lane_at == j, column, tail)
    loss_high = loss.astype(bf16).astype(f32)
    tail = jnp.where(lane_at == heads, loss_high, tail)
    tail = jnp.where(lane_at == heads + 1, loss - loss_high, tail)
    out[:, heads * DI :] = tail.astype(bf16)


def gradients(heads, blocks, terms, own, other, probs, log_probs, delta_own, sent, brought):
    count, length = terms[0].shape[0], own.shape[0]
    span = length // blocks
    return pl.pallas_call(
        functools.partial(gradient_kernel, heads, blocks),
        out_shape=jax.ShapeDtypeStruct((count, heads * DI + lanes), bf16),
        in_specs=[in_vmem()] * (7 + len(terms)),
        out_specs=in_vmem(),
        scratch_shapes=[
            pltpu.VMEM((heads * count, lanes), f32),
            pltpu.VMEM((heads * count, DI), f32),
            pltpu.VMEM((heads * count, span), bf16),
            pltpu.VMEM((heads * count, span), f32),
            pltpu.VMEM((heads * count, span), f32),
        ],
        compiler_params=params(),
        cost_estimate=pl.CostEstimate(
            flops=8 * count * heads * DI * length,
            bytes_accessed=4 * (terms[0].size + 6 * count * length) + 4 * length * DI,
            transcendentals=0,
        ),
        name="gradient",
    )(*terms, own, other, probs, log_probs, delta_own, sent, brought)


def arrange_kernel(n, info, *refs):
    kept, (latents, hiddens, held) = refs[:-3], refs[-3:]
    queries, depth = kept[0].shape[0], latents.shape[0]
    for k, one in enumerate(kept):
        to = pl.ds(pl.multiple_of(info[at_partner(n, k)] * queries, queries), queries)
        held[to, :] = one[:, :depth].astype(f32)
        hiddens[to, :] = one[:, depth:]
    latents[...] = held[...].T.astype(bf16)


def arrange(n, info, depth, kept):
    queries, width = kept[0].shape
    total = queries * len(kept)
    return pl.pallas_call(
        functools.partial(arrange_kernel, n),
        out_shape=(
            jax.ShapeDtypeStruct((depth, total), bf16),
            jax.ShapeDtypeStruct((total, width - depth), bf16),
        ),
        in_specs=[in_smem()] + [in_vmem()] * len(kept),
        out_specs=(in_vmem(),) * 2,
        scratch_shapes=[pltpu.VMEM((total, depth), f32)],
        compiler_params=params(),
        cost_estimate=pl.CostEstimate(
            flops=0, bytes_accessed=4 * total * width, transcendentals=0
        ),
        name="arrange",
    )(info, *kept)


def outer_kernel(heads, n, order, info, latents, hiddens, *refs):
    parts, (grad, grad_mixed, losses, rows, blocks, sems) = refs[:-6], refs[-6:]
    count = parts[0].shape[-2]
    width = heads * DI
    steps, _, span = blocks.shape
    k = 0
    for part in parts:
        for t in range(part.shape[0]):
            to = 0
            if order is not None:
                to = pl.multiple_of((info[order[k][0]] * n + info[order[k][1]]) * count, count)
            rows[pl.ds(to, count), :] = part[t]
            k += 1
    copies = []
    for i in range(steps):
        at = slice(i * span, (i + 1) * span)
        blocks[i] = times(latents[...], rows[:, at], 1, 0)
        copies.append(pltpu.make_async_copy(blocks.at[i], grad.at[:, at], sems.at[i]))
        copies[-1].start()
    tails = rows[:, width:]
    grad_mixed[...] = times(tails, hiddens[...], 0, 0)[:heads]
    own = losses.shape[1]
    from_own = rows[pl.ds(pl.multiple_of(info[at_dp] * own, own), own), width:].astype(f32)
    column = from_own[:, heads : heads + 1] + from_own[:, heads + 1 : heads + 2]
    diagonal = lax.broadcasted_iota(jnp.int32, (own, own), 0) == lax.broadcasted_iota(
        jnp.int32, (own, own), 1
    )
    losses[...] = jnp.sum(jnp.where(diagonal, column, 0.0), axis=0, keepdims=True)
    for copy in copies:
        copy.wait()


def outer(heads, n, order, queries, info, latents, hiddens, parts):
    row_count, total = latents.shape
    width = heads * DI
    steps = 8
    hidden_count = hiddens.shape[1]
    return pl.pallas_call(
        functools.partial(outer_kernel, heads, n, order),
        out_shape=(
            jax.ShapeDtypeStruct((row_count, width), f32),
            jax.ShapeDtypeStruct((heads, hidden_count), f32),
            jax.ShapeDtypeStruct((1, queries), f32),
        ),
        in_specs=[in_smem()] + [in_vmem()] * (2 + len(parts)),
        out_specs=(pl.BlockSpec(memory_space=pl.ANY), in_vmem(), in_vmem()),
        scratch_shapes=[
            pltpu.VMEM((total, width + lanes), bf16),
            pltpu.VMEM((steps, row_count, width // steps), f32),
            pltpu.SemaphoreType.DMA((steps,)),
        ],
        compiler_params=params(),
        cost_estimate=pl.CostEstimate(
            flops=2 * total * row_count * width,
            bytes_accessed=4 * row_count * width + 2 * total * width,
            transcendentals=0,
        ),
        name="outer",
    )(info, latents, hiddens, *parts)


def per_device(
    q_latent, hidden, main_queries, main_keys, index_keys, positions, w_query, w_weights
):
    n = lax.axis_size("ctx")
    z = lax.axis_index("ctx")
    head_size = lax.axis_size("head")
    y = lax.axis_index("head")
    dp_size = lax.axis_size("dp")
    dp = lax.axis_index("dp")
    rows = main_keys.shape[1]
    half = rows // head_size
    rows_latent = w_query.shape[0]
    heads_here = w_weights.shape[1]
    queries_here = main_queries.shape[1]

    def shifted(x, t):
        return lax.ppermute(x, "ctx", [(k, (k + t) % n) for k in range(n)])

    def outward(x):
        return lax.ppermute(x, "ctx", [(1, 0), (2, 3)])

    def centre(x):
        return lax.ppermute(x, "ctx", [(1, 2), (2, 1)])

    def inward(x):
        return lax.ppermute(x, "ctx", [(0, 1), (3, 2)])

    def after(waited, *held):
        nonlocal token
        token, waited, held = lax.optimization_barrier((token, waited, held))
        return waited, *held

    def swap_head(x):
        return lax.ppermute(x, "head", [(0, 1), (1, 0)])

    def swap_dp(x, bit):
        return lax.ppermute(x, "dp", [(k, k ^ bit) for k in range(dp_size)])

    def over_dp(x):
        gathered, bit = [x], dp_size // 2
        while bit:
            gathered, bit = gathered + [swap_dp(one, bit) for one in gathered], bit // 2
        return gathered

    table = jnp.array(device_table(n, head_size, dp_size))
    info = lax.dynamic_index_in_dim(table, (z * head_size + y) * dp_size + dp, 0, False)

    token = positions[0]
    queries = main_queries[0]
    own_keys = lax.dynamic_slice_in_dim(main_keys[0].T, y * half, half, 1)
    index_part = lax.dynamic_slice_in_dim(index_keys[0], y * half, half)
    line = on_line(n)
    order_at = at_part(n, dp_size, 0) if line else None
    weights, tops, before = [], [], None

    def score_next(*options):
        nonlocal before
        t = len(weights)
        numer, top, *before = score(
            t, n, rows, at_option(n, dp_size, t), info, token, queries, other_queries, options, before
        )
        weights.append(numer)
        tops.append(top)

    if line:
        index_1, index_3 = shifted(index_part, 1), shifted(index_part, 3)
        keys = {left_1: lax.ppermute(own_keys, "ctx", [(1, 0), (2, 1), (3, 2)])}
        keys[right_1] = lax.ppermute(own_keys, "ctx", [(0, 1), (1, 2), (2, 3)])
        other_queries = swap_head(queries)
        partial, own_part, kept = project(
            info, order_at, queries_here, q_latent[0], w_query, hidden[0], w_weights.T
        )
        (index_1, index_3), far_part, index_again = after(
            (index_1, index_3), partial[3], index_part
        )
        far_in, index_2 = inward(far_part), shifted(index_again, 2)
        (keys,) = after(keys)
        keys[left_2] = lax.ppermute(keys[left_1], "ctx", [(1, 0), (2, 1)])
        keys[right_2] = lax.ppermute(keys[right_1], "ctx", [(1, 2), (2, 3)])
        (far_in, index_2, other_queries), near_parts = after(
            (far_in, index_2, other_queries), partial[1:3]
        )
        far_over = centre(far_part + far_in)
        near_in = inward(near_parts)
        index_own = jnp.concatenate([index_part, index_1, index_2, index_3])
        index_other = swap_head(index_own)
        (keys,) = after(keys)
        keys[last] = outward(jnp.where(z < n // 2, keys[left_2], keys[right_2]))
        (far_over, near_in), kept = after((far_over, near_in), kept)
        sum_out = outward(partial[0] + far_over)
        sum_over = centre(partial[2] + near_in[1])
        half_dp = swap_dp(kept, dp_size // 2)
        near_dp = swap_dp(jnp.stack([kept, half_dp]), dp_size // 4)
        kept = [kept, half_dp, near_dp[0], near_dp[1]]
        score_next(own_keys)
        for t in range(1, n - 1):
            score_next(*[keys[k] for k in line_options[t - 1]])
        before, sum_out, sum_over, near_in, kept = lax.optimization_barrier(
            (before, sum_out, sum_over, near_in, kept)
        )
        terms = [own_part, sum_out, sum_over, near_in[0]]
        last_keys = [keys[k] for k in line_options[n - 2]]
        latents, hiddens = arrange(n, info, rows_latent, kept)
    else:
        ring = folded_ring(n)
        partial, _, kept = project(
            info, order_at, queries_here, q_latent[0], w_query, hidden[0], w_weights.T
        )
        terms = [jnp.sum(lax.all_to_all(partial, "ctx", 0, 0), axis=0)]
        other_queries = swap_head(queries)
        index_own = jnp.concatenate([index_part] + [shifted(index_part, t) for t in range(1, n)])
        index_other = swap_head(index_own)
        latents, hiddens = arrange(n, info, rows_latent, over_dp(kept))
        keys = own_keys
        for _ in range(n - 1):
            score_next(keys)
            keys = lax.ppermute(keys, "ctx", [(ring[k], ring[(k + 1) % n]) for k in range(n)])
        last_keys = [keys]

    part = make_logits(heads_here, terms, index_own, index_other)
    far, last_keys = lax.optimization_barrier((swap_head(part), last_keys))
    probs, log_probs = make_softmax(
        n, rows, at_shift(n, dp_size, 0), info, token, part, far
    )
    score_next(*last_keys)
    delta_own, sent = make_delta(info, weights, tops, *before, swap_head(jnp.stack(before)), probs)
    piece = gradients(
        heads_here,
        n,
        terms,
        index_own,
        index_other,
        probs,
        log_probs,
        delta_own,
        sent,
        swap_head(sent),
    )[None]

    brought = []
    for t in range(1, n):
        pairs = [(k, (k + t) % n) for k in range(n)]
        brought.append(lax.ppermute(piece, "ctx", pairs))
    own_pieces = over_dp(piece)
    brought, own_pieces = lax.optimization_barrier((jnp.concatenate(brought), own_pieces))
    brought = over_dp(brought)
    parts_in = own_pieces + brought
    order = [(at_partner(n, k), at_shift(n, dp_size, 0)) for k in range(dp_size)]
    order += [
        (at_partner(n, k), at_shift(n, dp_size, t)) for k in range(dp_size) for t in range(1, n)
    ]
    if queries_here % 16:
        places = jnp.stack([info[a] * n + info[b] for a, b in order])
        flat = jnp.concatenate(parts_in)[jnp.argsort(places)]
        parts_in, order = [flat.reshape(1, -1, flat.shape[2])], None
    grad_query, grad_weights, losses = outer(
        heads_here, n, order, q_latent.shape[1], info, latents, hiddens, parts_in
    )
    return (grad_query, grad_weights.T, losses)


def solution(mesh):
    return jax.shard_map(
        per_device,
        mesh=mesh,
        in_specs=(
            P("dp", None, None),
            P("dp", None, None),
            P("dp", "ctx", "head", None),
            P("dp", "ctx", None),
            P("dp", "ctx", None),
            P("dp", None),
            P("ctx", "head"),
            P("ctx", "head"),
        ),
        out_specs=(P("ctx", "head"), P("ctx", "head"), P("dp", None)),
        check_vma=False,
    )
```

```python
import functools
import math

import jax
import jax.numpy as jnp
import numpy as np
from jax import lax
from jax.experimental import pallas as pl
from jax.experimental.pallas import tpu as pltpu
from jax.sharding import PartitionSpec as P

HI = 64
DI = 128
HM = 128

index_scale = (HI * DI) ** (-0.5)
exponent_scale = 192.0 ** (-0.5) / math.log(2.0)
masked_floor = -1e30
lanes = 128
f32 = jnp.float32
bf16 = jnp.bfloat16
vmem_limit = 24 * 2**20
group_size = 4


def folded_ring(size):
    return [0] + list(range(1, size, 2)) + list(range(2, size, 2))[::-1]


def params():
    return pltpu.CompilerParams(vmem_limit_bytes=vmem_limit)


def in_smem():
    return pl.BlockSpec(memory_space=pltpu.SMEM)


def in_vmem():
    return pl.BlockSpec(memory_space=pltpu.VMEM)


def times(a, b, axis_a, axis_b):
    return lax.dot_general(a, b, (((axis_a,), (axis_b,)), ((), ())), preferred_element_type=f32)


def device_table(n, heads, dp_size, rows):
    ring = folded_ring(n)
    half = rows // heads
    flips = dp_flips(dp_size)
    table = []
    for z in range(n):
        place = ring.index(z)
        behind = [ring[(place - t) % n] for t in range(n)]
        for y in range(heads):
            for dp in range(dp_size):
                row = [z] + [ring[(place - 1 - t) % n] for t in range(n)]
                row += [k * rows + y * half for k in behind]
                row += [k * rows + (1 - y) * half for k in behind]
                row += [(dp ^ k) * n + (z - t) % n for k in flips for t in range(n)]
                row += [dp ^ k for k in flips]
                table.append(row)
    return np.array(table, np.int32)


def dp_flips(dp_size):
    flips, bit = [0], dp_size // 2
    while bit:
        flips, bit = flips + [k ^ bit for k in flips], bit // 2
    return flips


def project_kernel(aligned, info, latent, weight, hidden, hidden_weight, *outs):
    *parts, kept = outs
    width = weight.shape[1]
    heads = hidden_weight.shape[0]
    count = parts[0].shape[0]
    if aligned:
        starts = [pl.multiple_of(info[1 + k] * count, count) for k in range(len(parts))]
        rows = jnp.concatenate([latent[pl.ds(k, count), :] for k in starts], axis=0)
        mixed_rows = jnp.concatenate([hidden[pl.ds(k, count), :] for k in starts], axis=0)
    else:
        rows, mixed_rows = latent[...], hidden[...]
    for at in range(0, width, 512):
        product = times(rows, weight[:, at : at + 512], 1, 0)
        for k, out in enumerate(parts):
            out[:, at : at + 512] = product[k * count : (k + 1) * count]
    mixed = times(mixed_rows, hidden_weight[...], 1, 1)
    for k, out in enumerate(parts):
        out[:, width : width + heads] = mixed[k * count : (k + 1) * count]
        out[:, width + heads :] = jnp.zeros((count, lanes - heads), f32)
    kept[:, : latent.shape[1]] = latent[...]
    kept[:, latent.shape[1] :] = hidden[...]


def project(info, count, latent, weight, hidden, hidden_weight):
    queries, width = latent.shape[0], weight.shape[1]
    depth, hidden_depth = weight.shape[0], hidden_weight.shape[1]
    blocks = queries // count
    aligned = count % 16 == 0 and depth % lanes == 0 and hidden_depth % lanes == 0
    columns = lambda i, info: (0, info[0])
    whole = lambda i, info: (0, 0)
    kept = None
    if not aligned:
        latent = lax.dynamic_slice_in_dim(latent, info[0] * depth, depth, 1)
        hidden = lax.dynamic_slice_in_dim(hidden, info[0] * hidden_depth, hidden_depth, 1)
        kept = jnp.concatenate([latent, hidden], axis=1)
        order = info[1 : 1 + blocks]
        latent = latent.reshape(blocks, count, depth)[order].reshape(queries, depth)
        hidden = hidden.reshape(blocks, count, hidden_depth)[order].reshape(queries, hidden_depth)
        columns = whole
    *parts, kept_here = pl.pallas_call(
        functools.partial(project_kernel, aligned),
        grid_spec=pltpu.PrefetchScalarGridSpec(
            num_scalar_prefetch=1,
            grid=(1,),
            in_specs=[
                pl.BlockSpec((queries, depth), columns),
                pl.BlockSpec((depth, width), whole),
                pl.BlockSpec((queries, hidden_depth), columns),
                pl.BlockSpec(hidden_weight.shape, whole),
            ],
            out_specs=[pl.BlockSpec((count, width + lanes), whole)] * blocks
            + [pl.BlockSpec((queries, depth + hidden_depth), whole)],
        ),
        out_shape=[jax.ShapeDtypeStruct((count, width + lanes), f32)] * blocks
        + [jax.ShapeDtypeStruct((queries, depth + hidden_depth), bf16)],
        compiler_params=params(),
        cost_estimate=pl.CostEstimate(
            flops=2 * queries * weight.size, bytes_accessed=2 * weight.size, transcendentals=0
        ),
        name="project",
    )(info, latent, weight, hidden, hidden_weight)
    return parts, kept_here if aligned else kept


def score_kernel(
    t,
    base_at,
    info,
    positions,
    mine,
    other,
    keys,
    top_before,
    mass_before,
    weights,
    top,
    top_all,
    mass_all,
    mass,
    even,
    odd,
):
    count, heads, depth = mine.shape
    limits = [positions[info[0] * count + q] - info[base_at] for q in range(count)]
    span = keys.shape[1]
    key_at = lax.broadcasted_iota(jnp.int32, (1, span), 1)
    row_at = lax.broadcasted_iota(jnp.int32, (heads, lanes), 0)
    lane_at = lax.broadcasted_iota(jnp.int32, (heads, lanes), 1)
    group = min(group_size, count)
    work = [(at, k) for at in range(0, count, group) for k in range(2)]
    held = (even, odd)

    def multiply(step):
        at, k = work[step]
        rows = (mine, other)[k][at : at + group].reshape(group * heads, depth)
        held[step % 2][...] = times(rows, keys[...], 1, 0)

    multiply(0)
    for step, (at, k) in enumerate(work):
        if step + 1 < len(work):
            multiply(step + 1)
        scores = held[step % 2]
        offset = k * heads
        diagonal = lane_at == row_at + offset
        for i in range(group):
            q = at + i
            one = jnp.where(
                key_at <= limits[q], scores[i * heads : (i + 1) * heads, :], masked_floor
            )
            high = jnp.max(one, axis=1, keepdims=True)
            shifted = jnp.exp2((one - high) * exponent_scale)
            total = jnp.sum(shifted, axis=1, keepdims=True)
            weights[q, offset : offset + heads] = shifted.astype(bf16)
            high_row = jnp.sum(jnp.where(diagonal, high, 0.0), axis=0, keepdims=True)
            total_row = jnp.sum(jnp.where(diagonal, total, 0.0), axis=0, keepdims=True)
            if k == 0:
                top[q : q + 1, :] = high_row
                mass[q : q + 1, :] = total_row
            else:
                top[q : q + 1, :] += high_row
                mass[q : q + 1, :] += total_row
    if t == 0:
        top_all[...] = top[...]
        mass_all[...] = mass[...]
    else:
        before, now = top_before[...], top[...]
        joint = jnp.maximum(before, now)
        top_all[...] = joint
        mass_all[...] = mass_before[...] * jnp.exp2((before - joint) * exponent_scale) + mass[
            ...
        ] * jnp.exp2((now - joint) * exponent_scale)


def score(t, n, info, positions, mine, other, keys, before):
    count, heads, depth = mine.shape
    span = keys.shape[1]
    stats = jax.ShapeDtypeStruct((count, lanes), f32)
    if before is None:
        before = (jnp.zeros((count, lanes), f32),) * 2
    return pl.pallas_call(
        functools.partial(score_kernel, t, 1 + n + t),
        out_shape=(jax.ShapeDtypeStruct((count, 2 * heads, span), bf16), stats, stats, stats),
        in_specs=[in_smem()] * 2 + [in_vmem()] * 5,
        out_specs=(in_vmem(),) * 4,
        scratch_shapes=[pltpu.VMEM((count, lanes), f32)]
        + [pltpu.VMEM((min(group_size, count) * heads, span), f32)] * 2,
        compiler_params=params(),
        cost_estimate=pl.CostEstimate(
            flops=4 * count * heads * depth * span,
            bytes_accessed=2 * (2 * mine.size + keys.size + 2 * count * heads * span),
            transcendentals=2 * count * heads * span,
        ),
        name="score",
    )(info, positions, mine, other, keys, *before)


def delta_kernel(blocks, *refs):
    weights, tops = refs[:blocks], refs[blocks : 2 * blocks]
    top, mass, far, probs, out, sent, held = refs[2 * blocks :]
    count, heads, span = weights[0].shape
    far_top = pltpu.roll(far[0], heads // 2, 1)
    far_mass = pltpu.roll(far[1], heads // 2, 1)
    joint = jnp.maximum(top[...], far_top)
    total = mass[...] * jnp.exp2((top[...] - joint) * exponent_scale) + far_mass * jnp.exp2(
        (far_top - joint) * exponent_scale
    )
    row_at = lax.broadcasted_iota(jnp.int32, (heads, lanes), 0)
    lane_at = lax.broadcasted_iota(jnp.int32, (heads, lanes), 1)
    diagonal = row_at == lane_at
    inverse = 1.0 / (total * HM)
    for t in range(blocks):
        factor = jnp.exp2((tops[t][...] - joint) * exponent_scale) * inverse
        for q in range(count):
            column = jnp.sum(
                jnp.where(diagonal, factor[q : q + 1, :], 0.0), axis=1, keepdims=True
            )
            mixed = weights[t][q].astype(f32) * column
            held[q : q + 1, t * span : (t + 1) * span] = jnp.sum(mixed, axis=0, keepdims=True)
    delta = probs[0] - held[...]
    out[...] = delta
    sent[...] = delta.astype(bf16)


def make_delta(weights, tops, top, mass, far, probs):
    blocks = len(weights)
    count, heads, span = weights[0].shape
    return pl.pallas_call(
        functools.partial(delta_kernel, blocks),
        out_shape=(
            jax.ShapeDtypeStruct((count, blocks * span), f32),
            jax.ShapeDtypeStruct((count, blocks * span), bf16),
        ),
        in_specs=[in_vmem()] * (2 * blocks + 4),
        out_specs=(in_vmem(),) * 2,
        scratch_shapes=[pltpu.VMEM((count, blocks * span), f32)],
        compiler_params=params(),
        cost_estimate=pl.CostEstimate(
            flops=2 * blocks * count * heads * span,
            bytes_accessed=2 * blocks * count * heads * span,
            transcendentals=0,
        ),
        name="delta",
    )(*weights, *tops, top, mass, far, probs)


def query_rows(total, heads):
    return jnp.concatenate(
        [total[:, j * DI : (j + 1) * DI].astype(bf16) for j in range(heads)], axis=0
    )


def logits_kernel(heads, received, here, own, other, out):
    count = received.shape[0]
    total = received[...] + here[...]
    query = query_rows(total, heads)
    columns = [total[:, heads * DI + j : heads * DI + j + 1] for j in range(heads)]
    span = 512
    for part, keys in enumerate((own, other)):
        for at in range(0, keys.shape[0], span):
            affinity = times(query, keys[at : at + span, :], 1, 1)
            running = jnp.zeros((count, span), f32)
            for j in range(heads):
                reached = jnp.maximum(affinity[j * count : (j + 1) * count], 0.0)
                running = running + columns[j] * reached
            out[part, :, at : at + span] = running * index_scale


def make_logits(heads, received, here, own, other):
    count, length = received.shape[0], own.shape[0]
    return pl.pallas_call(
        functools.partial(logits_kernel, heads),
        out_shape=jax.ShapeDtypeStruct((2, count, length), f32),
        in_specs=[in_vmem()] * 4,
        out_specs=in_vmem(),
        compiler_params=params(),
        cost_estimate=pl.CostEstimate(
            flops=4 * count * heads * DI * length,
            bytes_accessed=4 * (2 * received.size + 2 * count * length) + 4 * length * DI,
            transcendentals=0,
        ),
        name="logits",
    )(received, here, own, other)


def softmax_kernel(blocks, info, positions, part, far, probs, log_probs):
    _, count, length = part.shape
    span = length // blocks
    row_at = lax.broadcasted_iota(jnp.int32, (count, lanes), 0)
    position = jnp.zeros((count, lanes), jnp.int32)
    for q in range(count):
        position = jnp.where(row_at == q, positions[info[0] * count + q], position)
    position = position[:, 0:1]
    key_at = lax.broadcasted_iota(jnp.int32, (count, span), 1)

    def seen(side, t):
        return key_at + info[1 + (1 + side) * blocks + t] <= position

    highs = []
    for side in range(2):
        high = jnp.full((count, span), masked_floor, f32)
        for t in range(blocks):
            at = slice(t * span, (t + 1) * span)
            value = part[side, :, at] + far[1 - side, :, at]
            log_probs[side, :, at] = value
            high = jnp.maximum(high, jnp.where(seen(side, t), value, masked_floor))
        highs.append(jnp.max(high, axis=1, keepdims=True))
    high = jnp.maximum(highs[0], highs[1])
    sums = []
    for side in range(2):
        running = jnp.zeros((count, span), f32)
        for t in range(blocks):
            at = slice(t * span, (t + 1) * span)
            grown = jnp.where(seen(side, t), jnp.exp(log_probs[side, :, at] - high), 0.0)
            probs[side, :, at] = grown
            running = running + grown
        sums.append(jnp.sum(running, axis=1, keepdims=True))
    mass = sums[0] + sums[1]
    level = high + jnp.log(mass)
    inverse = 1.0 / mass
    for side in range(2):
        for t in range(blocks):
            at = slice(t * span, (t + 1) * span)
            probs[side, :, at] = probs[side, :, at] * inverse
            log_probs[side, :, at] = jnp.where(seen(side, t), log_probs[side, :, at] - level, 0.0)


def make_softmax(blocks, info, positions, part, far):
    return pl.pallas_call(
        functools.partial(softmax_kernel, blocks),
        out_shape=(jax.ShapeDtypeStruct(part.shape, f32),) * 2,
        in_specs=[in_smem()] * 2 + [in_vmem()] * 2,
        out_specs=(in_vmem(),) * 2,
        compiler_params=params(),
        cost_estimate=pl.CostEstimate(
            flops=8 * part.size, bytes_accessed=16 * part.size, transcendentals=part.size
        ),
        name="softmax",
    )(info, positions, part, far)


def gradient_kernel(
    heads,
    blocks,
    received,
    here,
    own,
    other,
    probs,
    log_probs,
    delta_own,
    sent,
    brought,
    out,
    flow,
    query_sum,
    grads,
    even,
    odd,
):
    count = received.shape[0]
    total = received[...] + here[...]
    span = own.shape[0] // blocks
    query = query_rows(total, heads)
    columns = [
        total[:, heads * DI + j : heads * DI + j + 1] * index_scale for j in range(heads)
    ]
    work = [(side, t) for side in range(2) for t in range(blocks)]
    held = (even, odd)

    def multiply(step):
        side, t = work[step]
        keys = (own, other)[side][t * span : (t + 1) * span, :]
        held[step % 2][...] = times(query, keys, 1, 1)

    multiply(0)
    flow[...] = jnp.zeros(flow.shape, f32)
    running = [jnp.zeros((count, span), f32)] * 2
    for step, (side, t) in enumerate(work):
        if step + 1 < len(work):
            multiply(step + 1)
        at = slice(t * span, (t + 1) * span)
        affinity = held[step % 2]
        rounded = (sent, brought)[side][:, at].astype(f32)
        delta = delta_own[:, at] if side == 0 else rounded
        wanted = probs[side, :, at] - rounded
        running[side] = running[side] + wanted * log_probs[side, :, at]
        for j in range(heads):
            rows = slice(j * count, (j + 1) * count)
            one = affinity[rows, :]
            reached = jnp.where(one > 0, delta, 0.0)
            grads[rows, :] = (reached * columns[j]).astype(bf16)
            product = reached * one
            folded = product[:, :lanes]
            for k in range(lanes, span, lanes):
                folded = folded + product[:, k : k + lanes]
            flow[rows, :] += folded
        keys = (own, other)[side][at, :]
        product = times(grads[...], keys, 1, 0)
        if step == 0:
            query_sum[...] = product
        else:
            query_sum[...] += product
    losses = [jnp.sum(one, axis=1, keepdims=True) for one in running]
    loss = -(losses[0] + losses[1])
    lane_at = lax.broadcasted_iota(jnp.int32, (count, lanes), 1)
    tail = jnp.zeros((count, lanes), f32)
    for j in range(heads):
        rows = slice(j * count, (j + 1) * count)
        out[:, j * DI : (j + 1) * DI] = query_sum[rows, :].astype(bf16)
        column = jnp.sum(flow[rows, :], axis=1, keepdims=True) * index_scale
        tail = jnp.where(lane_at == j, column, tail)
    loss_high = loss.astype(bf16).astype(f32)
    tail = jnp.where(lane_at == heads, loss_high, tail)
    tail = jnp.where(lane_at == heads + 1, loss - loss_high, tail)
    out[:, heads * DI :] = tail.astype(bf16)


def gradients(heads, blocks, received, here, own, other, probs, log_probs, delta_own, sent, brought):
    count, length = received.shape[0], own.shape[0]
    span = length // blocks
    return pl.pallas_call(
        functools.partial(gradient_kernel, heads, blocks),
        out_shape=jax.ShapeDtypeStruct((count, heads * DI + lanes), bf16),
        in_specs=[in_vmem()] * 9,
        out_specs=in_vmem(),
        scratch_shapes=[
            pltpu.VMEM((heads * count, lanes), f32),
            pltpu.VMEM((heads * count, DI), f32),
            pltpu.VMEM((heads * count, span), bf16),
            pltpu.VMEM((heads * count, span), f32),
            pltpu.VMEM((heads * count, span), f32),
        ],
        compiler_params=params(),
        cost_estimate=pl.CostEstimate(
            flops=8 * count * heads * DI * length,
            bytes_accessed=4 * (2 * received.size + 6 * count * length) + 4 * length * DI,
            transcendentals=0,
        ),
        name="gradient",
    )(received, here, own, other, probs, log_probs, delta_own, sent, brought)


def arrange_kernel(at, info, *refs):
    kept, (latents, hiddens, held) = refs[:-3], refs[-3:]
    queries, depth = kept[0].shape[0], latents.shape[0]
    for k, one in enumerate(kept):
        to = pl.ds(pl.multiple_of(info[at + k] * queries, queries), queries)
        held[to, :] = one[:, :depth].astype(f32)
        hiddens[to, :] = one[:, depth:]
    latents[...] = held[...].T.astype(bf16)


def arrange(at, info, depth, kept):
    queries, width = kept[0].shape
    total = queries * len(kept)
    return pl.pallas_call(
        functools.partial(arrange_kernel, at),
        out_shape=(
            jax.ShapeDtypeStruct((depth, total), bf16),
            jax.ShapeDtypeStruct((total, width - depth), bf16),
        ),
        in_specs=[in_smem()] + [in_vmem()] * len(kept),
        out_specs=(in_vmem(),) * 2,
        scratch_shapes=[pltpu.VMEM((total, depth), f32)],
        compiler_params=params(),
        cost_estimate=pl.CostEstimate(
            flops=0, bytes_accessed=4 * total * width, transcendentals=0
        ),
        name="arrange",
    )(info, *kept)


def outer_kernel(heads, order, dp_at, info, latents, hiddens, *refs):
    parts, (grad, grad_mixed, losses, rows, blocks, sems) = refs[:-6], refs[-6:]
    count = parts[0].shape[-2]
    width = heads * DI
    steps, _, span = blocks.shape
    k = 0
    for part in parts:
        for t in range(part.shape[0]):
            to = 0 if order is None else pl.multiple_of(info[order[k]] * count, count)
            rows[pl.ds(to, count), :] = part[t]
            k += 1
    copies = []
    for i in range(steps):
        at = slice(i * span, (i + 1) * span)
        blocks[i] = times(latents[...], rows[:, at], 1, 0)
        copies.append(pltpu.make_async_copy(blocks.at[i], grad.at[:, at], sems.at[i]))
        copies[-1].start()
    tails = rows[:, width:]
    grad_mixed[...] = times(tails, hiddens[...], 0, 0)[:heads]
    own = losses.shape[1]
    from_own = rows[pl.ds(pl.multiple_of(info[dp_at] * own, own), own), width:].astype(f32)
    column = from_own[:, heads : heads + 1] + from_own[:, heads + 1 : heads + 2]
    diagonal = lax.broadcasted_iota(jnp.int32, (own, own), 0) == lax.broadcasted_iota(
        jnp.int32, (own, own), 1
    )
    losses[...] = jnp.sum(jnp.where(diagonal, column, 0.0), axis=0, keepdims=True)
    for copy in copies:
        copy.wait()


def outer(heads, order, dp_at, queries, info, latents, hiddens, parts):
    row_count, total = latents.shape
    width = heads * DI
    steps = 8
    hidden_count = hiddens.shape[1]
    return pl.pallas_call(
        functools.partial(outer_kernel, heads, order, dp_at),
        out_shape=(
            jax.ShapeDtypeStruct((row_count, width), f32),
            jax.ShapeDtypeStruct((heads, hidden_count), f32),
            jax.ShapeDtypeStruct((1, queries), f32),
        ),
        in_specs=[in_smem()] + [in_vmem()] * (2 + len(parts)),
        out_specs=(pl.BlockSpec(memory_space=pl.ANY), in_vmem(), in_vmem()),
        scratch_shapes=[
            pltpu.VMEM((total, width + lanes), bf16),
            pltpu.VMEM((steps, row_count, width // steps), f32),
            pltpu.SemaphoreType.DMA((steps,)),
        ],
        compiler_params=params(),
        cost_estimate=pl.CostEstimate(
            flops=2 * total * row_count * width,
            bytes_accessed=4 * row_count * width + 2 * total * width,
            transcendentals=0,
        ),
        name="outer",
    )(info, latents, hiddens, *parts)


def per_device(
    q_latent, hidden, main_queries, main_keys, index_keys, positions, w_query, w_weights
):
    n = lax.axis_size("ctx")
    z = lax.axis_index("ctx")
    head_size = lax.axis_size("head")
    y = lax.axis_index("head")
    dp_size = lax.axis_size("dp")
    dp = lax.axis_index("dp")
    ring = folded_ring(n)
    rows = main_keys.shape[1]
    half = rows // head_size
    rows_latent = w_query.shape[0]
    heads_here = w_weights.shape[1]
    queries_here = main_queries.shape[1]
    sequence_positions = positions[0]

    def onward(x, t=1):
        return lax.ppermute(x, "ctx", [(ring[k], ring[(k + t) % n]) for k in range(n)])

    def swap_head(x):
        return lax.ppermute(x, "head", [(0, 1), (1, 0)])

    def swap_dp(x, bit):
        return lax.ppermute(x, "dp", [(k, k ^ bit) for k in range(dp_size)])

    def over_dp(x):
        gathered, bit = [x], dp_size // 2
        while bit:
            gathered, bit = gathered + [swap_dp(one, bit) for one in gathered], bit // 2
        return gathered

    table = jnp.array(device_table(n, head_size, dp_size, rows))
    info = lax.dynamic_index_in_dim(table, (z * head_size + y) * dp_size + dp, 0, False)

    keys_mine = [lax.dynamic_slice_in_dim(main_keys[0].T, y * half, half, 1)]
    keys_mine.append(onward(keys_mine[0]))
    queries = main_queries[0]
    other_queries = swap_head(queries)
    index_parts = [lax.dynamic_slice_in_dim(index_keys[0], y * half, half)] + [None] * (n - 1)
    index_parts[1] = onward(index_parts[0])
    index_parts[n - 1] = onward(index_parts[0], n - 1)
    parts, kept = project(info, queries_here, q_latent[0], w_query, hidden[0], w_weights.T)
    summed = onward(parts[0]) + parts[1]
    order_at = 1 + 3 * n
    dp_at = order_at + n * dp_size
    weights, tops, before = [], [], None

    def score_next(keys):
        nonlocal before
        t = len(weights)
        numer, top, *before = score(
            t, n, info, sequence_positions, queries, other_queries, keys, before
        )
        weights.append(numer)
        tops.append(top)

    index_own = index_other = None
    for t in range(1, n - 1):
        if t == 1:
            sent_on, summed, index_parts, kept, other_queries = lax.optimization_barrier(
                (keys_mine[t], summed, index_parts, kept, other_queries)
            )
            for k in range(2, n - 1):
                index_parts[k] = onward(index_parts[1]) if k == 2 else onward(index_parts[0], k)
            index_own = jnp.concatenate(index_parts)
            index_other = swap_head(index_own)
            over_half = swap_dp(kept, dp_size // 2)
            kept = [kept, over_half, swap_dp(kept, dp_size // 4)]
        elif t == 2:
            sent_on, summed, index_other, kept = lax.optimization_barrier(
                (keys_mine[t], summed, index_other, kept)
            )
            kept = kept + [swap_dp(kept[1], dp_size // 4)]
        else:
            sent_on, summed = lax.optimization_barrier((keys_mine[t], summed))
        keys_mine[t] = sent_on
        keys_mine.append(onward(sent_on))
        summed = onward(summed)
        if t + 1 < n - 1:
            summed = summed + parts[t + 1]
    received = summed
    latents, hiddens = arrange(dp_at, info, rows_latent, kept)
    other_queries, latents, hiddens = lax.optimization_barrier((other_queries, latents, hiddens))
    while len(weights) < n - 1:
        score_next(keys_mine[len(weights)])
    before, received = lax.optimization_barrier((before, received))

    part = make_logits(heads_here, received, parts[n - 1], index_own, index_other)
    probs, log_probs = make_softmax(n, info, sequence_positions, part, swap_head(part))

    before, probs, log_probs = lax.optimization_barrier((before, probs, log_probs))
    score_next(keys_mine[n - 1])
    delta_own, sent = make_delta(weights, tops, *before, swap_head(jnp.stack(before)), probs)
    piece = gradients(
        heads_here,
        n,
        received,
        parts[n - 1],
        index_own,
        index_other,
        probs,
        log_probs,
        delta_own,
        sent,
        swap_head(sent),
    )[None]

    brought = []
    for t in range(1, n):
        pairs = [(k, (k + t) % n) for k in range(n)]
        brought.append(lax.ppermute(piece, "ctx", pairs))
    own_pieces = over_dp(piece)
    brought, own_pieces = lax.optimization_barrier((jnp.concatenate(brought), own_pieces))
    brought = over_dp(brought)
    if queries_here % 16:
        flat = jnp.concatenate([jnp.concatenate([a, b]) for a, b in zip(own_pieces, brought)])
        order = jnp.argsort(info[order_at : order_at + n * dp_size])
        parts_in, order = [flat[order].reshape(1, -1, flat.shape[2])], None
    else:
        parts_in, order = own_pieces + brought, []
        order += [order_at + k * n for k in range(dp_size)]
        order += [order_at + k * n + t for k in range(dp_size) for t in range(1, n)]
    grad_query, grad_weights, losses = outer(
        heads_here,
        order,
        dp_at,
        q_latent.shape[1],
        info,
        latents,
        hiddens,
        parts_in,
    )
    return (grad_query, grad_weights.T, losses)


def solution(mesh):
    return jax.shard_map(
        per_device,
        mesh=mesh,
        in_specs=(
            P("dp", None, None),
            P("dp", None, None),
            P("dp", "ctx", "head", None),
            P("dp", "ctx", None),
            P("dp", "ctx", None),
            P("dp", None),
            P("ctx", "head"),
            P("ctx", "head"),
        ),
        out_specs=(P("ctx", "head"), P("ctx", "head"), P("dp", None)),
        check_vma=False,
    )
```

```python
import functools
import math

import jax
import jax.numpy as jnp
import numpy as np
from jax import lax
from jax.experimental import pallas as pl
from jax.experimental.pallas import tpu as pltpu
from jax.sharding import PartitionSpec as P

HI = 64
DI = 128
HM = 128

index_scale = (HI * DI) ** (-0.5)
exponent_scale = 192.0 ** (-0.5) / math.log(2.0)
masked_floor = -1e30
lanes = 128
f32 = jnp.float32
bf16 = jnp.bfloat16
vmem_limit = 24 * 2**20
group_size = 4


def folded_ring(size):
    return [0] + list(range(1, size, 2)) + list(range(2, size, 2))[::-1]


def params():
    return pltpu.CompilerParams(vmem_limit_bytes=vmem_limit)


def in_smem():
    return pl.BlockSpec(memory_space=pltpu.SMEM)


def in_vmem():
    return pl.BlockSpec(memory_space=pltpu.VMEM)


def times(a, b, axis_a, axis_b):
    return lax.dot_general(a, b, (((axis_a,), (axis_b,)), ((), ())), preferred_element_type=f32)


def device_table(n, heads, dp_size, rows):
    ring = folded_ring(n)
    half = rows // heads
    flips = dp_flips(dp_size)
    table = []
    for z in range(n):
        place = ring.index(z)
        behind = [ring[(place - t) % n] for t in range(n)]
        for y in range(heads):
            for dp in range(dp_size):
                row = [z] + [ring[(place - 1 - t) % n] for t in range(n)]
                row += [k * rows + y * half for k in behind]
                row += [k * rows + (1 - y) * half for k in behind]
                row += [(dp ^ k) * n + (z - t) % n for k in flips for t in range(n)]
                row += [dp ^ k for k in flips]
                table.append(row)
    return np.array(table, np.int32)


def dp_flips(dp_size):
    flips, bit = [0], dp_size // 2
    while bit:
        flips, bit = flips + [k ^ bit for k in flips], bit // 2
    return flips


def project_kernel(aligned, info, latent, weight, hidden, hidden_weight, *outs):
    *parts, kept = outs
    width = weight.shape[1]
    heads = hidden_weight.shape[0]
    count = parts[0].shape[0]
    if aligned:
        starts = [pl.multiple_of(info[1 + k] * count, count) for k in range(len(parts))]
        rows = jnp.concatenate([latent[pl.ds(k, count), :] for k in starts], axis=0)
        mixed_rows = jnp.concatenate([hidden[pl.ds(k, count), :] for k in starts], axis=0)
    else:
        rows, mixed_rows = latent[...], hidden[...]
    for at in range(0, width, 512):
        product = times(rows, weight[:, at : at + 512], 1, 0)
        for k, out in enumerate(parts):
            out[:, at : at + 512] = product[k * count : (k + 1) * count]
    mixed = times(mixed_rows, hidden_weight[...], 1, 1)
    for k, out in enumerate(parts):
        out[:, width : width + heads] = mixed[k * count : (k + 1) * count]
        out[:, width + heads :] = jnp.zeros((count, lanes - heads), f32)
    kept[:, : latent.shape[1]] = latent[...]
    kept[:, latent.shape[1] :] = hidden[...]


def project(info, count, latent, weight, hidden, hidden_weight):
    queries, width = latent.shape[0], weight.shape[1]
    depth, hidden_depth = weight.shape[0], hidden_weight.shape[1]
    blocks = queries // count
    aligned = count % 16 == 0 and depth % lanes == 0 and hidden_depth % lanes == 0
    columns = lambda i, info: (0, info[0])
    whole = lambda i, info: (0, 0)
    kept = None
    if not aligned:
        latent = lax.dynamic_slice_in_dim(latent, info[0] * depth, depth, 1)
        hidden = lax.dynamic_slice_in_dim(hidden, info[0] * hidden_depth, hidden_depth, 1)
        kept = jnp.concatenate([latent, hidden], axis=1)
        order = info[1 : 1 + blocks]
        latent = latent.reshape(blocks, count, depth)[order].reshape(queries, depth)
        hidden = hidden.reshape(blocks, count, hidden_depth)[order].reshape(queries, hidden_depth)
        columns = whole
    *parts, kept_here = pl.pallas_call(
        functools.partial(project_kernel, aligned),
        grid_spec=pltpu.PrefetchScalarGridSpec(
            num_scalar_prefetch=1,
            grid=(1,),
            in_specs=[
                pl.BlockSpec((queries, depth), columns),
                pl.BlockSpec((depth, width), whole),
                pl.BlockSpec((queries, hidden_depth), columns),
                pl.BlockSpec(hidden_weight.shape, whole),
            ],
            out_specs=[pl.BlockSpec((count, width + lanes), whole)] * blocks
            + [pl.BlockSpec((queries, depth + hidden_depth), whole)],
        ),
        out_shape=[jax.ShapeDtypeStruct((count, width + lanes), f32)] * blocks
        + [jax.ShapeDtypeStruct((queries, depth + hidden_depth), bf16)],
        compiler_params=params(),
        cost_estimate=pl.CostEstimate(
            flops=2 * queries * weight.size, bytes_accessed=2 * weight.size, transcendentals=0
        ),
        name="project",
    )(info, latent, weight, hidden, hidden_weight)
    return parts, kept_here if aligned else kept


def score_kernel(
    t,
    base_at,
    info,
    positions,
    mine,
    other,
    keys,
    top_before,
    mass_before,
    weights,
    top,
    top_all,
    mass_all,
    mass,
    even,
    odd,
):
    count, heads, depth = mine.shape
    limits = [positions[info[0] * count + q] - info[base_at] for q in range(count)]
    span = keys.shape[1]
    key_at = lax.broadcasted_iota(jnp.int32, (1, span), 1)
    row_at = lax.broadcasted_iota(jnp.int32, (heads, lanes), 0)
    lane_at = lax.broadcasted_iota(jnp.int32, (heads, lanes), 1)
    group = min(group_size, count)
    work = [(at, k) for at in range(0, count, group) for k in range(2)]
    held = (even, odd)

    def multiply(step):
        at, k = work[step]
        rows = (mine, other)[k][at : at + group].reshape(group * heads, depth)
        held[step % 2][...] = times(rows, keys[...], 1, 0)

    multiply(0)
    for step, (at, k) in enumerate(work):
        if step + 1 < len(work):
            multiply(step + 1)
        scores = held[step % 2]
        offset = k * heads
        diagonal = lane_at == row_at + offset
        for i in range(group):
            q = at + i
            one = jnp.where(
                key_at <= limits[q], scores[i * heads : (i + 1) * heads, :], masked_floor
            )
            high = jnp.max(one, axis=1, keepdims=True)
            shifted = jnp.exp2((one - high) * exponent_scale)
            total = jnp.sum(shifted, axis=1, keepdims=True)
            weights[q, offset : offset + heads] = shifted.astype(bf16)
            high_row = jnp.sum(jnp.where(diagonal, high, 0.0), axis=0, keepdims=True)
            total_row = jnp.sum(jnp.where(diagonal, total, 0.0), axis=0, keepdims=True)
            if k == 0:
                top[q : q + 1, :] = high_row
                mass[q : q + 1, :] = total_row
            else:
                top[q : q + 1, :] += high_row
                mass[q : q + 1, :] += total_row
    if t == 0:
        top_all[...] = top[...]
        mass_all[...] = mass[...]
    else:
        before, now = top_before[...], top[...]
        joint = jnp.maximum(before, now)
        top_all[...] = joint
        mass_all[...] = mass_before[...] * jnp.exp2((before - joint) * exponent_scale) + mass[
            ...
        ] * jnp.exp2((now - joint) * exponent_scale)


def score(t, n, info, positions, mine, other, keys, before):
    count, heads, depth = mine.shape
    span = keys.shape[1]
    stats = jax.ShapeDtypeStruct((count, lanes), f32)
    if before is None:
        before = (jnp.zeros((count, lanes), f32),) * 2
    return pl.pallas_call(
        functools.partial(score_kernel, t, 1 + n + t),
        out_shape=(jax.ShapeDtypeStruct((count, 2 * heads, span), bf16), stats, stats, stats),
        in_specs=[in_smem()] * 2 + [in_vmem()] * 5,
        out_specs=(in_vmem(),) * 4,
        scratch_shapes=[pltpu.VMEM((count, lanes), f32)]
        + [pltpu.VMEM((min(group_size, count) * heads, span), f32)] * 2,
        compiler_params=params(),
        cost_estimate=pl.CostEstimate(
            flops=4 * count * heads * depth * span,
            bytes_accessed=2 * (2 * mine.size + keys.size + 2 * count * heads * span),
            transcendentals=2 * count * heads * span,
        ),
        name="score",
    )(info, positions, mine, other, keys, *before)


def delta_kernel(blocks, *refs):
    weights, tops = refs[:blocks], refs[blocks : 2 * blocks]
    top, mass, far, probs, out, sent, held = refs[2 * blocks :]
    count, heads, span = weights[0].shape
    far_top = pltpu.roll(far[0], heads // 2, 1)
    far_mass = pltpu.roll(far[1], heads // 2, 1)
    joint = jnp.maximum(top[...], far_top)
    total = mass[...] * jnp.exp2((top[...] - joint) * exponent_scale) + far_mass * jnp.exp2(
        (far_top - joint) * exponent_scale
    )
    row_at = lax.broadcasted_iota(jnp.int32, (heads, lanes), 0)
    lane_at = lax.broadcasted_iota(jnp.int32, (heads, lanes), 1)
    diagonal = row_at == lane_at
    inverse = 1.0 / (total * HM)
    for t in range(blocks):
        factor = jnp.exp2((tops[t][...] - joint) * exponent_scale) * inverse
        for q in range(count):
            column = jnp.sum(
                jnp.where(diagonal, factor[q : q + 1, :], 0.0), axis=1, keepdims=True
            )
            mixed = weights[t][q].astype(f32) * column
            held[q : q + 1, t * span : (t + 1) * span] = jnp.sum(mixed, axis=0, keepdims=True)
    delta = probs[0] - held[...]
    out[...] = delta
    sent[...] = delta.astype(bf16)


def make_delta(weights, tops, top, mass, far, probs):
    blocks = len(weights)
    count, heads, span = weights[0].shape
    return pl.pallas_call(
        functools.partial(delta_kernel, blocks),
        out_shape=(
            jax.ShapeDtypeStruct((count, blocks * span), f32),
            jax.ShapeDtypeStruct((count, blocks * span), bf16),
        ),
        in_specs=[in_vmem()] * (2 * blocks + 4),
        out_specs=(in_vmem(),) * 2,
        scratch_shapes=[pltpu.VMEM((count, blocks * span), f32)],
        compiler_params=params(),
        cost_estimate=pl.CostEstimate(
            flops=2 * blocks * count * heads * span,
            bytes_accessed=2 * blocks * count * heads * span,
            transcendentals=0,
        ),
        name="delta",
    )(*weights, *tops, top, mass, far, probs)


def query_rows(total, heads):
    return jnp.concatenate(
        [total[:, j * DI : (j + 1) * DI].astype(bf16) for j in range(heads)], axis=0
    )


def logits_kernel(heads, received, here, own, other, out):
    count = received.shape[0]
    total = received[...] + here[...]
    query = query_rows(total, heads)
    columns = [total[:, heads * DI + j : heads * DI + j + 1] for j in range(heads)]
    span = 512
    for part, keys in enumerate((own, other)):
        for at in range(0, keys.shape[0], span):
            affinity = times(query, keys[at : at + span, :], 1, 1)
            running = jnp.zeros((count, span), f32)
            for j in range(heads):
                reached = jnp.maximum(affinity[j * count : (j + 1) * count], 0.0)
                running = running + columns[j] * reached
            out[part, :, at : at + span] = running * index_scale


def make_logits(heads, received, here, own, other):
    count, length = received.shape[0], own.shape[0]
    return pl.pallas_call(
        functools.partial(logits_kernel, heads),
        out_shape=jax.ShapeDtypeStruct((2, count, length), f32),
        in_specs=[in_vmem()] * 4,
        out_specs=in_vmem(),
        compiler_params=params(),
        cost_estimate=pl.CostEstimate(
            flops=4 * count * heads * DI * length,
            bytes_accessed=4 * (2 * received.size + 2 * count * length) + 4 * length * DI,
            transcendentals=0,
        ),
        name="logits",
    )(received, here, own, other)


def softmax_kernel(blocks, info, positions, part, far, probs, log_probs):
    _, count, length = part.shape
    span = length // blocks
    row_at = lax.broadcasted_iota(jnp.int32, (count, lanes), 0)
    position = jnp.zeros((count, lanes), jnp.int32)
    for q in range(count):
        position = jnp.where(row_at == q, positions[info[0] * count + q], position)
    position = position[:, 0:1]
    key_at = lax.broadcasted_iota(jnp.int32, (count, span), 1)

    def seen(side, t):
        return key_at + info[1 + (1 + side) * blocks + t] <= position

    highs = []
    for side in range(2):
        high = jnp.full((count, span), masked_floor, f32)
        for t in range(blocks):
            at = slice(t * span, (t + 1) * span)
            value = part[side, :, at] + far[1 - side, :, at]
            log_probs[side, :, at] = value
            high = jnp.maximum(high, jnp.where(seen(side, t), value, masked_floor))
        highs.append(jnp.max(high, axis=1, keepdims=True))
    high = jnp.maximum(highs[0], highs[1])
    sums = []
    for side in range(2):
        running = jnp.zeros((count, span), f32)
        for t in range(blocks):
            at = slice(t * span, (t + 1) * span)
            grown = jnp.where(seen(side, t), jnp.exp(log_probs[side, :, at] - high), 0.0)
            probs[side, :, at] = grown
            running = running + grown
        sums.append(jnp.sum(running, axis=1, keepdims=True))
    mass = sums[0] + sums[1]
    level = high + jnp.log(mass)
    inverse = 1.0 / mass
    for side in range(2):
        for t in range(blocks):
            at = slice(t * span, (t + 1) * span)
            probs[side, :, at] = probs[side, :, at] * inverse
            log_probs[side, :, at] = jnp.where(seen(side, t), log_probs[side, :, at] - level, 0.0)


def make_softmax(blocks, info, positions, part, far):
    return pl.pallas_call(
        functools.partial(softmax_kernel, blocks),
        out_shape=(jax.ShapeDtypeStruct(part.shape, f32),) * 2,
        in_specs=[in_smem()] * 2 + [in_vmem()] * 2,
        out_specs=(in_vmem(),) * 2,
        compiler_params=params(),
        cost_estimate=pl.CostEstimate(
            flops=8 * part.size, bytes_accessed=16 * part.size, transcendentals=part.size
        ),
        name="softmax",
    )(info, positions, part, far)


def gradient_kernel(
    heads,
    first,
    here_heads,
    blocks,
    received,
    here,
    own,
    other,
    probs,
    log_probs,
    delta_own,
    sent,
    brought,
    out,
    flow,
    query_sum,
    grads,
    even,
    odd,
):
    count = received.shape[0]
    total = received[...] + here[...]
    span = own.shape[0] // blocks
    query = query_rows(total[:, first * DI : (first + here_heads) * DI], here_heads)
    columns = [
        total[:, heads * DI + first + j : heads * DI + first + j + 1] * index_scale
        for j in range(here_heads)
    ]
    work = [(side, t) for side in range(2) for t in range(blocks)]
    held = (even, odd)

    def multiply(step):
        side, t = work[step]
        keys = (own, other)[side][t * span : (t + 1) * span, :]
        held[step % 2][...] = times(query, keys, 1, 1)

    multiply(0)
    flow[...] = jnp.zeros(flow.shape, f32)
    running = [jnp.zeros((count, span), f32)] * 2
    for step, (side, t) in enumerate(work):
        if step + 1 < len(work):
            multiply(step + 1)
        at = slice(t * span, (t + 1) * span)
        affinity = held[step % 2]
        rounded = (sent, brought)[side][:, at].astype(f32)
        delta = delta_own[:, at] if side == 0 else rounded
        wanted = probs[side, :, at] - rounded
        running[side] = running[side] + wanted * log_probs[side, :, at]
        for j in range(here_heads):
            rows = slice(j * count, (j + 1) * count)
            one = affinity[rows, :]
            reached = jnp.where(one > 0, delta, 0.0)
            grads[rows, :] = (reached * columns[j]).astype(bf16)
            product = reached * one
            folded = product[:, :lanes]
            for k in range(lanes, span, lanes):
                folded = folded + product[:, k : k + lanes]
            flow[rows, :] += folded
        keys = (own, other)[side][at, :]
        product = times(grads[...], keys, 1, 0)
        if step == 0:
            query_sum[...] = product
        else:
            query_sum[...] += product
    losses = [jnp.sum(one, axis=1, keepdims=True) for one in running]
    loss = -(losses[0] + losses[1])
    lane_at = lax.broadcasted_iota(jnp.int32, (count, lanes), 1)
    tail = jnp.zeros((count, lanes), f32)
    for j in range(here_heads):
        rows = slice(j * count, (j + 1) * count)
        out[:, j * DI : (j + 1) * DI] = query_sum[rows, :].astype(bf16)
        column = jnp.sum(flow[rows, :], axis=1, keepdims=True) * index_scale
        tail = jnp.where(lane_at == j, column, tail)
    loss_high = loss.astype(bf16).astype(f32)
    tail = jnp.where(lane_at == here_heads, loss_high, tail)
    tail = jnp.where(lane_at == here_heads + 1, loss - loss_high, tail)
    out[:, here_heads * DI :] = tail.astype(bf16)


def gradients(heads, first, here_heads, blocks, received, here, own, other, probs, log_probs, delta_own, sent, brought):
    count, length = received.shape[0], own.shape[0]
    span = length // blocks
    return pl.pallas_call(
        functools.partial(gradient_kernel, heads, first, here_heads, blocks),
        out_shape=jax.ShapeDtypeStruct((count, here_heads * DI + lanes), bf16),
        in_specs=[in_vmem()] * 9,
        out_specs=in_vmem(),
        scratch_shapes=[
            pltpu.VMEM((here_heads * count, lanes), f32),
            pltpu.VMEM((here_heads * count, DI), f32),
            pltpu.VMEM((here_heads * count, span), bf16),
            pltpu.VMEM((here_heads * count, span), f32),
            pltpu.VMEM((here_heads * count, span), f32),
        ],
        compiler_params=params(),
        cost_estimate=pl.CostEstimate(
            flops=8 * count * here_heads * DI * length,
            bytes_accessed=4 * (2 * received.size + 6 * count * length) + 4 * length * DI,
            transcendentals=0,
        ),
        name="gradient",
    )(received, here, own, other, probs, log_probs, delta_own, sent, brought)


def arrange_kernel(at, info, *refs):
    kept, (latents, hiddens, held) = refs[:-3], refs[-3:]
    queries, depth = kept[0].shape[0], latents.shape[0]
    for k, one in enumerate(kept):
        to = pl.ds(pl.multiple_of(info[at + k] * queries, queries), queries)
        held[to, :] = one[:, :depth].astype(f32)
        hiddens[to, :] = one[:, depth:]
    latents[...] = held[...].T.astype(bf16)


def arrange(at, info, depth, kept):
    queries, width = kept[0].shape
    total = queries * len(kept)
    return pl.pallas_call(
        functools.partial(arrange_kernel, at),
        out_shape=(
            jax.ShapeDtypeStruct((depth, total), bf16),
            jax.ShapeDtypeStruct((total, width - depth), bf16),
        ),
        in_specs=[in_smem()] + [in_vmem()] * len(kept),
        out_specs=(in_vmem(),) * 2,
        scratch_shapes=[pltpu.VMEM((total, depth), f32)],
        compiler_params=params(),
        cost_estimate=pl.CostEstimate(
            flops=0, bytes_accessed=4 * total * width, transcendentals=0
        ),
        name="arrange",
    )(info, *kept)


def outer_kernel(heads, order, dp_at, at_column, info, latents, hiddens, *refs):
    if at_column:
        _, mixed_before, *refs = refs
    parts, (grad, grad_mixed, losses, rows, blocks, sems) = refs[:-6], refs[-6:]
    count = parts[0].shape[-2]
    width = heads * DI
    steps, _, span = blocks.shape
    k = 0
    for part in parts:
        for t in range(part.shape[0]):
            to = 0 if order is None else pl.multiple_of(info[order[k]] * count, count)
            rows[pl.ds(to, count), :] = part[t]
            k += 1
    copies = []
    for i in range(steps):
        blocks[i] = times(latents[...], rows[:, i * span : (i + 1) * span], 1, 0)
        at = slice(at_column + i * span, at_column + (i + 1) * span)
        copies.append(pltpu.make_async_copy(blocks.at[i], grad.at[:, at], sems.at[i]))
        copies[-1].start()
    tails = rows[:, width:]
    mixed = times(tails, hiddens[...], 0, 0)[:heads]
    if at_column:
        before = mixed_before.shape[0]
        grad_mixed[:before] = mixed_before[...]
        grad_mixed[before:] = mixed
    else:
        grad_mixed[...] = mixed
    own = losses.shape[1]
    from_own = rows[pl.ds(pl.multiple_of(info[dp_at] * own, own), own), width:].astype(f32)
    column = from_own[:, heads : heads + 1] + from_own[:, heads + 1 : heads + 2]
    diagonal = lax.broadcasted_iota(jnp.int32, (own, own), 0) == lax.broadcasted_iota(
        jnp.int32, (own, own), 1
    )
    losses[...] = jnp.sum(jnp.where(diagonal, column, 0.0), axis=0, keepdims=True)
    for copy in copies:
        copy.wait()


def outer(heads, order, dp_at, queries, columns, at_column, before, info, latents, hiddens, parts):
    row_count, total = latents.shape
    width = heads * DI
    steps = 4
    hidden_count = hiddens.shape[1]
    heads_done = before[1].shape[0] if before else 0
    return pl.pallas_call(
        functools.partial(outer_kernel, heads, order, dp_at, at_column),
        out_shape=(
            jax.ShapeDtypeStruct((row_count, columns), f32),
            jax.ShapeDtypeStruct((heads_done + heads, hidden_count), f32),
            jax.ShapeDtypeStruct((1, queries), f32),
        ),
        in_specs=[in_smem()]
        + [in_vmem()] * 2
        + [pl.BlockSpec(memory_space=pl.ANY), in_vmem()][: len(before)]
        + [in_vmem()] * len(parts),
        out_specs=(pl.BlockSpec(memory_space=pl.ANY), in_vmem(), in_vmem()),
        input_output_aliases={3: 0} if before else {},
        scratch_shapes=[
            pltpu.VMEM((total, width + lanes), bf16),
            pltpu.VMEM((steps, row_count, width // steps), f32),
            pltpu.SemaphoreType.DMA((steps,)),
        ],
        compiler_params=params(),
        cost_estimate=pl.CostEstimate(flops=0, bytes_accessed=0, transcendentals=0),
        name="outer",
    )(info, latents, hiddens, *before, *parts)


def per_device(
    q_latent, hidden, main_queries, main_keys, index_keys, positions, w_query, w_weights
):
    n = lax.axis_size("ctx")
    z = lax.axis_index("ctx")
    head_size = lax.axis_size("head")
    y = lax.axis_index("head")
    dp_size = lax.axis_size("dp")
    dp = lax.axis_index("dp")
    ring = folded_ring(n)
    rows = main_keys.shape[1]
    half = rows // head_size
    rows_latent = w_query.shape[0]
    heads_here = w_weights.shape[1]
    queries_here = main_queries.shape[1]
    sequence_positions = positions[0]

    def onward(x, t=1):
        return lax.ppermute(x, "ctx", [(ring[k], ring[(k + t) % n]) for k in range(n)])

    def swap_head(x):
        return lax.ppermute(x, "head", [(0, 1), (1, 0)])

    def swap_dp(x, bit):
        return lax.ppermute(x, "dp", [(k, k ^ bit) for k in range(dp_size)])

    def over_dp(x, held=None):
        gathered, bit = [x], dp_size // 2
        while bit:
            if held is not None and len(gathered) > 1:
                gathered[1:], held = lax.optimization_barrier((gathered[1:], held))
            gathered, bit = gathered + [swap_dp(one, bit) for one in gathered], bit // 2
        return gathered

    table = jnp.array(device_table(n, head_size, dp_size, rows))
    info = lax.dynamic_index_in_dim(table, (z * head_size + y) * dp_size + dp, 0, False)

    keys_mine = [lax.dynamic_slice_in_dim(main_keys[0].T, y * half, half, 1)]
    keys_mine.append(onward(keys_mine[0]))
    queries = main_queries[0]
    other_queries = swap_head(queries)
    index_parts = [lax.dynamic_slice_in_dim(index_keys[0], y * half, half)] + [None] * (n - 1)
    index_parts[1] = onward(index_parts[0])
    index_parts[n - 1] = onward(index_parts[0], n - 1)
    parts, kept = project(info, queries_here, q_latent[0], w_query, hidden[0], w_weights.T)
    summed = onward(parts[0]) + parts[1]
    order_at = 1 + 3 * n
    dp_at = order_at + n * dp_size
    weights, tops, before = [], [], None

    def score_next(keys):
        nonlocal before
        t = len(weights)
        numer, top, *before = score(
            t, n, info, sequence_positions, queries, other_queries, keys, before
        )
        weights.append(numer)
        tops.append(top)

    index_own = index_other = None
    for t in range(1, n - 1):
        if t == 1:
            sent_on, summed, index_parts, kept, other_queries = lax.optimization_barrier(
                (keys_mine[t], summed, index_parts, kept, other_queries)
            )
            for k in range(2, n - 1):
                index_parts[k] = onward(index_parts[1]) if k == 2 else onward(index_parts[0], k)
            index_own = jnp.concatenate(index_parts)
            index_other = swap_head(index_own)
            over_half = swap_dp(kept, dp_size // 2)
            kept = [kept, over_half, swap_dp(kept, dp_size // 4)]
        elif t == 2:
            sent_on, summed, index_other, kept = lax.optimization_barrier(
                (keys_mine[t], summed, index_other, kept)
            )
            kept = kept + [swap_dp(kept[1], dp_size // 4)]
        else:
            sent_on, summed = lax.optimization_barrier((keys_mine[t], summed))
        keys_mine[t] = sent_on
        keys_mine.append(onward(sent_on))
        summed = onward(summed)
        if t + 1 < n - 1:
            summed = summed + parts[t + 1]
    received = summed
    latents, hiddens = arrange(dp_at, info, rows_latent, kept)
    other_queries, latents, hiddens = lax.optimization_barrier((other_queries, latents, hiddens))
    while len(weights) < n - 1:
        score_next(keys_mine[len(weights)])
    before, received = lax.optimization_barrier((before, received))

    part = make_logits(heads_here, received, parts[n - 1], index_own, index_other)
    probs, log_probs = make_softmax(n, info, sequence_positions, part, swap_head(part))

    before, probs, log_probs = lax.optimization_barrier((before, probs, log_probs))
    score_next(keys_mine[n - 1])
    delta_own, sent = make_delta(weights, tops, *before, swap_head(jnp.stack(before)), probs)
    delta_other = swap_head(sent)

    half_heads = heads_here // 2
    order = [order_at + k * n + t for k in range(dp_size) for t in range(n)]
    done, losses, shards = (), None, []
    for first in (0, half_heads):
        piece = gradients(
            heads_here,
            first,
            half_heads,
            n,
            received,
            parts[n - 1],
            index_own,
            index_other,
            probs,
            log_probs,
            delta_own,
            sent,
            delta_other,
        )[None]
        shards.append(piece)
    for half_at, first in enumerate((0, half_heads)):
        piece = shards[half_at]
        brought = [piece]
        for t in range(1, n):
            pairs = [(k, (k + t) % n) for k in range(n)]
            brought.append(lax.ppermute(piece, "ctx", pairs))
        stacked, _ = lax.optimization_barrier((jnp.concatenate(brought), shards))
        gathered = over_dp(stacked, losses)
        order_here = order
        if queries_here % 16:
            flat = jnp.concatenate(gathered)
            by_place = jnp.argsort(info[order_at : order_at + n * dp_size])
            gathered, order_here = [flat[by_place].reshape(1, -1, flat.shape[2])], None
        grad_query, grad_weights, losses_here = outer(
            half_heads,
            order_here,
            dp_at,
            q_latent.shape[1],
            heads_here * DI,
            first * DI,
            done,
            info,
            latents,
            hiddens,
            gathered,
        )
        done = (grad_query, grad_weights)
        losses = losses_here if losses is None else losses
    return (grad_query, grad_weights.T, losses)


def solution(mesh):
    return jax.shard_map(
        per_device,
        mesh=mesh,
        in_specs=(
            P("dp", None, None),
            P("dp", None, None),
            P("dp", "ctx", "head", None),
            P("dp", "ctx", None),
            P("dp", "ctx", None),
            P("dp", None),
            P("ctx", "head"),
            P("ctx", "head"),
        ),
        out_specs=(P("ctx", "head"), P("ctx", "head"), P("dp", None)),
        check_vma=False,
    )
```

```python
import functools
import math

import jax
import jax.numpy as jnp
import numpy as np
from jax import lax
from jax.experimental import pallas as pl
from jax.experimental.pallas import tpu as pltpu
from jax.sharding import PartitionSpec as P

HI = 64
DI = 128
HM = 128

index_scale = (HI * DI) ** (-0.5)
exponent_scale = 192.0 ** (-0.5) / math.log(2.0)
masked_floor = -1e30
lanes = 128
f32 = jnp.float32
bf16 = jnp.bfloat16
vmem_limit = 24 * 2**20
group_size = 4


def folded_ring(size):
    return [0] + list(range(1, size, 2)) + list(range(2, size, 2))[::-1]


def params():
    return pltpu.CompilerParams(vmem_limit_bytes=vmem_limit)


def in_smem():
    return pl.BlockSpec(memory_space=pltpu.SMEM)


def in_vmem():
    return pl.BlockSpec(memory_space=pltpu.VMEM)


def times(a, b, axis_a, axis_b):
    return lax.dot_general(a, b, (((axis_a,), (axis_b,)), ((), ())), preferred_element_type=f32)


def device_table(n, heads, dp_size, rows):
    ring = folded_ring(n)
    half = rows // heads
    flips = dp_flips(dp_size)
    table = []
    for z in range(n):
        place = ring.index(z)
        behind = [ring[(place - t) % n] for t in range(n)]
        for y in range(heads):
            for dp in range(dp_size):
                row = [z] + [ring[(place - 1 - t) % n] for t in range(n)]
                row += [k * rows + y * half for k in behind]
                row += [k * rows + (1 - y) * half for k in behind]
                row += [(dp ^ k) * n + (z - t) % n for k in flips for t in range(n)]
                row += [dp ^ k for k in flips]
                table.append(row)
    return np.array(table, np.int32)


def dp_flips(dp_size):
    flips, bit = [0], dp_size // 2
    while bit:
        flips, bit = flips + [k ^ bit for k in flips], bit // 2
    return flips


def project_kernel(aligned, info, latent, weight, hidden, hidden_weight, *outs):
    *parts, kept = outs
    width = weight.shape[1]
    heads = hidden_weight.shape[0]
    count = parts[0].shape[0]
    if aligned:
        starts = [pl.multiple_of(info[1 + k] * count, count) for k in range(len(parts))]
        rows = jnp.concatenate([latent[pl.ds(k, count), :] for k in starts], axis=0)
        mixed_rows = jnp.concatenate([hidden[pl.ds(k, count), :] for k in starts], axis=0)
    else:
        rows, mixed_rows = latent[...], hidden[...]
    for at in range(0, width, 512):
        product = times(rows, weight[:, at : at + 512], 1, 0)
        for k, out in enumerate(parts):
            out[:, at : at + 512] = product[k * count : (k + 1) * count]
    mixed = times(mixed_rows, hidden_weight[...], 1, 1)
    for k, out in enumerate(parts):
        out[:, width : width + heads] = mixed[k * count : (k + 1) * count]
        out[:, width + heads :] = jnp.zeros((count, lanes - heads), f32)
    kept[:, : latent.shape[1]] = latent[...]
    kept[:, latent.shape[1] :] = hidden[...]


def project(info, count, latent, weight, hidden, hidden_weight):
    queries, width = latent.shape[0], weight.shape[1]
    depth, hidden_depth = weight.shape[0], hidden_weight.shape[1]
    blocks = queries // count
    aligned = count % 16 == 0 and depth % lanes == 0 and hidden_depth % lanes == 0
    columns = lambda i, info: (0, info[0])
    whole = lambda i, info: (0, 0)
    kept = None
    if not aligned:
        latent = lax.dynamic_slice_in_dim(latent, info[0] * depth, depth, 1)
        hidden = lax.dynamic_slice_in_dim(hidden, info[0] * hidden_depth, hidden_depth, 1)
        kept = jnp.concatenate([latent, hidden], axis=1)
        order = info[1 : 1 + blocks]
        latent = latent.reshape(blocks, count, depth)[order].reshape(queries, depth)
        hidden = hidden.reshape(blocks, count, hidden_depth)[order].reshape(queries, hidden_depth)
        columns = whole
    *parts, kept_here = pl.pallas_call(
        functools.partial(project_kernel, aligned),
        grid_spec=pltpu.PrefetchScalarGridSpec(
            num_scalar_prefetch=1,
            grid=(1,),
            in_specs=[
                pl.BlockSpec((queries, depth), columns),
                pl.BlockSpec((depth, width), whole),
                pl.BlockSpec((queries, hidden_depth), columns),
                pl.BlockSpec(hidden_weight.shape, whole),
            ],
            out_specs=[pl.BlockSpec((count, width + lanes), whole)] * blocks
            + [pl.BlockSpec((queries, depth + hidden_depth), whole)],
        ),
        out_shape=[jax.ShapeDtypeStruct((count, width + lanes), f32)] * blocks
        + [jax.ShapeDtypeStruct((queries, depth + hidden_depth), bf16)],
        compiler_params=params(),
        cost_estimate=pl.CostEstimate(
            flops=2 * queries * weight.size, bytes_accessed=2 * weight.size, transcendentals=0
        ),
        name="project",
    )(info, latent, weight, hidden, hidden_weight)
    return parts, kept_here if aligned else kept


def score_kernel(
    t,
    base_at,
    info,
    positions,
    mine,
    other,
    keys,
    top_before,
    mass_before,
    weights,
    top,
    top_all,
    mass_all,
    mass,
    even,
    odd,
):
    count, heads, depth = mine.shape
    limits = [positions[info[0] * count + q] - info[base_at] for q in range(count)]
    span = keys.shape[1]
    key_at = lax.broadcasted_iota(jnp.int32, (1, span), 1)
    row_at = lax.broadcasted_iota(jnp.int32, (heads, lanes), 0)
    lane_at = lax.broadcasted_iota(jnp.int32, (heads, lanes), 1)
    group = min(group_size, count)
    work = [(at, k) for at in range(0, count, group) for k in range(2)]
    held = (even, odd)

    def multiply(step):
        at, k = work[step]
        rows = (mine, other)[k][at : at + group].reshape(group * heads, depth)
        held[step % 2][...] = times(rows, keys[...], 1, 0)

    multiply(0)
    for step, (at, k) in enumerate(work):
        if step + 1 < len(work):
            multiply(step + 1)
        scores = held[step % 2]
        offset = k * heads
        diagonal = lane_at == row_at + offset
        for i in range(group):
            q = at + i
            one = jnp.where(
                key_at <= limits[q], scores[i * heads : (i + 1) * heads, :], masked_floor
            )
            high = jnp.max(one, axis=1, keepdims=True)
            shifted = jnp.exp2((one - high) * exponent_scale)
            total = jnp.sum(shifted, axis=1, keepdims=True)
            weights[q, offset : offset + heads] = shifted.astype(bf16)
            high_row = jnp.sum(jnp.where(diagonal, high, 0.0), axis=0, keepdims=True)
            total_row = jnp.sum(jnp.where(diagonal, total, 0.0), axis=0, keepdims=True)
            if k == 0:
                top[q : q + 1, :] = high_row
                mass[q : q + 1, :] = total_row
            else:
                top[q : q + 1, :] += high_row
                mass[q : q + 1, :] += total_row
    if t == 0:
        top_all[...] = top[...]
        mass_all[...] = mass[...]
    else:
        before, now = top_before[...], top[...]
        joint = jnp.maximum(before, now)
        top_all[...] = joint
        mass_all[...] = mass_before[...] * jnp.exp2((before - joint) * exponent_scale) + mass[
            ...
        ] * jnp.exp2((now - joint) * exponent_scale)


def score(t, n, info, positions, mine, other, keys, before):
    count, heads, depth = mine.shape
    span = keys.shape[1]
    stats = jax.ShapeDtypeStruct((count, lanes), f32)
    if before is None:
        before = (jnp.zeros((count, lanes), f32),) * 2
    return pl.pallas_call(
        functools.partial(score_kernel, t, 1 + n + t),
        out_shape=(jax.ShapeDtypeStruct((count, 2 * heads, span), bf16), stats, stats, stats),
        in_specs=[in_smem()] * 2 + [in_vmem()] * 5,
        out_specs=(in_vmem(),) * 4,
        scratch_shapes=[pltpu.VMEM((count, lanes), f32)]
        + [pltpu.VMEM((min(group_size, count) * heads, span), f32)] * 2,
        compiler_params=params(),
        cost_estimate=pl.CostEstimate(
            flops=4 * count * heads * depth * span,
            bytes_accessed=2 * (2 * mine.size + keys.size + 2 * count * heads * span),
            transcendentals=2 * count * heads * span,
        ),
        name="score",
    )(info, positions, mine, other, keys, *before)


def delta_kernel(blocks, *refs):
    weights, tops = refs[:blocks], refs[blocks : 2 * blocks]
    top, mass, far, probs, out, sent, held = refs[2 * blocks :]
    count, heads, span = weights[0].shape
    far_top = pltpu.roll(far[0], heads // 2, 1)
    far_mass = pltpu.roll(far[1], heads // 2, 1)
    joint = jnp.maximum(top[...], far_top)
    total = mass[...] * jnp.exp2((top[...] - joint) * exponent_scale) + far_mass * jnp.exp2(
        (far_top - joint) * exponent_scale
    )
    row_at = lax.broadcasted_iota(jnp.int32, (heads, lanes), 0)
    lane_at = lax.broadcasted_iota(jnp.int32, (heads, lanes), 1)
    diagonal = row_at == lane_at
    inverse = 1.0 / (total * HM)
    for t in range(blocks):
        factor = jnp.exp2((tops[t][...] - joint) * exponent_scale) * inverse
        for q in range(count):
            column = jnp.sum(
                jnp.where(diagonal, factor[q : q + 1, :], 0.0), axis=1, keepdims=True
            )
            mixed = weights[t][q].astype(f32) * column
            held[q : q + 1, t * span : (t + 1) * span] = jnp.sum(mixed, axis=0, keepdims=True)
    delta = probs[0] - held[...]
    out[...] = delta
    sent[...] = delta.astype(bf16)


def make_delta(weights, tops, top, mass, far, probs):
    blocks = len(weights)
    count, heads, span = weights[0].shape
    return pl.pallas_call(
        functools.partial(delta_kernel, blocks),
        out_shape=(
            jax.ShapeDtypeStruct((count, blocks * span), f32),
            jax.ShapeDtypeStruct((count, blocks * span), bf16),
        ),
        in_specs=[in_vmem()] * (2 * blocks + 4),
        out_specs=(in_vmem(),) * 2,
        scratch_shapes=[pltpu.VMEM((count, blocks * span), f32)],
        compiler_params=params(),
        cost_estimate=pl.CostEstimate(
            flops=2 * blocks * count * heads * span,
            bytes_accessed=2 * blocks * count * heads * span,
            transcendentals=0,
        ),
        name="delta",
    )(*weights, *tops, top, mass, far, probs)


def query_rows(total, heads):
    return jnp.concatenate(
        [total[:, j * DI : (j + 1) * DI].astype(bf16) for j in range(heads)], axis=0
    )


def logits_kernel(heads, received, here, own, other, out):
    count = received.shape[0]
    total = received[...] + here[...]
    query = query_rows(total, heads)
    columns = [total[:, heads * DI + j : heads * DI + j + 1] for j in range(heads)]
    span = 512
    for part, keys in enumerate((own, other)):
        for at in range(0, keys.shape[0], span):
            affinity = times(query, keys[at : at + span, :], 1, 1)
            running = jnp.zeros((count, span), f32)
            for j in range(heads):
                reached = jnp.maximum(affinity[j * count : (j + 1) * count], 0.0)
                running = running + columns[j] * reached
            out[part, :, at : at + span] = running * index_scale


def make_logits(heads, received, here, own, other):
    count, length = received.shape[0], own.shape[0]
    return pl.pallas_call(
        functools.partial(logits_kernel, heads),
        out_shape=jax.ShapeDtypeStruct((2, count, length), f32),
        in_specs=[in_vmem()] * 4,
        out_specs=in_vmem(),
        compiler_params=params(),
        cost_estimate=pl.CostEstimate(
            flops=4 * count * heads * DI * length,
            bytes_accessed=4 * (2 * received.size + 2 * count * length) + 4 * length * DI,
            transcendentals=0,
        ),
        name="logits",
    )(received, here, own, other)


def softmax_kernel(blocks, info, positions, part, far, probs, log_probs):
    _, count, length = part.shape
    span = length // blocks
    row_at = lax.broadcasted_iota(jnp.int32, (count, lanes), 0)
    position = jnp.zeros((count, lanes), jnp.int32)
    for q in range(count):
        position = jnp.where(row_at == q, positions[info[0] * count + q], position)
    position = position[:, 0:1]
    key_at = lax.broadcasted_iota(jnp.int32, (count, span), 1)

    def seen(side, t):
        return key_at + info[1 + (1 + side) * blocks + t] <= position

    highs = []
    for side in range(2):
        high = jnp.full((count, span), masked_floor, f32)
        for t in range(blocks):
            at = slice(t * span, (t + 1) * span)
            value = part[side, :, at] + far[1 - side, :, at]
            log_probs[side, :, at] = value
            high = jnp.maximum(high, jnp.where(seen(side, t), value, masked_floor))
        highs.append(jnp.max(high, axis=1, keepdims=True))
    high = jnp.maximum(highs[0], highs[1])
    sums = []
    for side in range(2):
        running = jnp.zeros((count, span), f32)
        for t in range(blocks):
            at = slice(t * span, (t + 1) * span)
            grown = jnp.where(seen(side, t), jnp.exp(log_probs[side, :, at] - high), 0.0)
            probs[side, :, at] = grown
            running = running + grown
        sums.append(jnp.sum(running, axis=1, keepdims=True))
    mass = sums[0] + sums[1]
    level = high + jnp.log(mass)
    inverse = 1.0 / mass
    for side in range(2):
        for t in range(blocks):
            at = slice(t * span, (t + 1) * span)
            probs[side, :, at] = probs[side, :, at] * inverse
            log_probs[side, :, at] = jnp.where(seen(side, t), log_probs[side, :, at] - level, 0.0)


def make_softmax(blocks, info, positions, part, far):
    return pl.pallas_call(
        functools.partial(softmax_kernel, blocks),
        out_shape=(jax.ShapeDtypeStruct(part.shape, f32),) * 2,
        in_specs=[in_smem()] * 2 + [in_vmem()] * 2,
        out_specs=(in_vmem(),) * 2,
        compiler_params=params(),
        cost_estimate=pl.CostEstimate(
            flops=8 * part.size, bytes_accessed=16 * part.size, transcendentals=part.size
        ),
        name="softmax",
    )(info, positions, part, far)


def gradient_kernel(
    heads,
    blocks,
    received,
    here,
    own,
    other,
    probs,
    log_probs,
    delta_own,
    sent,
    brought,
    out,
    flow,
    query_sum,
    grads,
    even,
    odd,
):
    count = received.shape[0]
    total = received[...] + here[...]
    span = own.shape[0] // blocks
    query = query_rows(total, heads)
    columns = [
        total[:, heads * DI + j : heads * DI + j + 1] * index_scale for j in range(heads)
    ]
    work = [(side, t) for side in range(2) for t in range(blocks)]
    held = (even, odd)

    def multiply(step):
        side, t = work[step]
        keys = (own, other)[side][t * span : (t + 1) * span, :]
        held[step % 2][...] = times(query, keys, 1, 1)

    multiply(0)
    flow[...] = jnp.zeros(flow.shape, f32)
    running = [jnp.zeros((count, span), f32)] * 2
    for step, (side, t) in enumerate(work):
        if step + 1 < len(work):
            multiply(step + 1)
        at = slice(t * span, (t + 1) * span)
        affinity = held[step % 2]
        rounded = (sent, brought)[side][:, at].astype(f32)
        delta = delta_own[:, at] if side == 0 else rounded
        wanted = probs[side, :, at] - rounded
        running[side] = running[side] + wanted * log_probs[side, :, at]
        for j in range(heads):
            rows = slice(j * count, (j + 1) * count)
            one = affinity[rows, :]
            reached = jnp.where(one > 0, delta, 0.0)
            grads[rows, :] = (reached * columns[j]).astype(bf16)
            product = reached * one
            folded = product[:, :lanes]
            for k in range(lanes, span, lanes):
                folded = folded + product[:, k : k + lanes]
            flow[rows, :] += folded
        keys = (own, other)[side][at, :]
        product = times(grads[...], keys, 1, 0)
        if step == 0:
            query_sum[...] = product
        else:
            query_sum[...] += product
    losses = [jnp.sum(one, axis=1, keepdims=True) for one in running]
    loss = -(losses[0] + losses[1])
    lane_at = lax.broadcasted_iota(jnp.int32, (count, lanes), 1)
    tail = jnp.zeros((count, lanes), f32)
    for j in range(heads):
        rows = slice(j * count, (j + 1) * count)
        out[:, j * DI : (j + 1) * DI] = query_sum[rows, :].astype(bf16)
        column = jnp.sum(flow[rows, :], axis=1, keepdims=True) * index_scale
        tail = jnp.where(lane_at == j, column, tail)
    loss_high = loss.astype(bf16).astype(f32)
    tail = jnp.where(lane_at == heads, loss_high, tail)
    tail = jnp.where(lane_at == heads + 1, loss - loss_high, tail)
    out[:, heads * DI :] = tail.astype(bf16)


def gradients(heads, blocks, received, here, own, other, probs, log_probs, delta_own, sent, brought):
    count, length = received.shape[0], own.shape[0]
    span = length // blocks
    return pl.pallas_call(
        functools.partial(gradient_kernel, heads, blocks),
        out_shape=jax.ShapeDtypeStruct((count, heads * DI + lanes), bf16),
        in_specs=[in_vmem()] * 9,
        out_specs=in_vmem(),
        scratch_shapes=[
            pltpu.VMEM((heads * count, lanes), f32),
            pltpu.VMEM((heads * count, DI), f32),
            pltpu.VMEM((heads * count, span), bf16),
            pltpu.VMEM((heads * count, span), f32),
            pltpu.VMEM((heads * count, span), f32),
        ],
        compiler_params=params(),
        cost_estimate=pl.CostEstimate(
            flops=8 * count * heads * DI * length,
            bytes_accessed=4 * (2 * received.size + 6 * count * length) + 4 * length * DI,
            transcendentals=0,
        ),
        name="gradient",
    )(received, here, own, other, probs, log_probs, delta_own, sent, brought)


def arrange_kernel(at, info, *refs):
    kept, (latents, hiddens, held) = refs[:-3], refs[-3:]
    queries, depth = kept[0].shape[0], latents.shape[0]
    for k, one in enumerate(kept):
        to = pl.ds(pl.multiple_of(info[at + k] * queries, queries), queries)
        held[to, :] = one[:, :depth].astype(f32)
        hiddens[to, :] = one[:, depth:]
    latents[...] = held[...].T.astype(bf16)


def arrange(at, info, depth, kept):
    queries, width = kept[0].shape
    total = queries * len(kept)
    return pl.pallas_call(
        functools.partial(arrange_kernel, at),
        out_shape=(
            jax.ShapeDtypeStruct((depth, total), bf16),
            jax.ShapeDtypeStruct((total, width - depth), bf16),
        ),
        in_specs=[in_smem()] + [in_vmem()] * len(kept),
        out_specs=(in_vmem(),) * 2,
        scratch_shapes=[pltpu.VMEM((total, depth), f32)],
        compiler_params=params(),
        cost_estimate=pl.CostEstimate(
            flops=0, bytes_accessed=4 * total * width, transcendentals=0
        ),
        name="arrange",
    )(info, *kept)


def outer_kernel(heads, order, dp_at, info, latents, hiddens, *refs):
    parts, (grad, grad_mixed, losses, rows, blocks, sems) = refs[:-6], refs[-6:]
    count = parts[0].shape[-2]
    width = heads * DI
    steps, _, span = blocks.shape
    k = 0
    for part in parts:
        for t in range(part.shape[0]):
            to = 0 if order is None else pl.multiple_of(info[order[k]] * count, count)
            rows[pl.ds(to, count), :] = part[t]
            k += 1
    copies = []
    for i in range(steps):
        at = slice(i * span, (i + 1) * span)
        blocks[i] = times(latents[...], rows[:, at], 1, 0)
        copies.append(pltpu.make_async_copy(blocks.at[i], grad.at[:, at], sems.at[i]))
        copies[-1].start()
    tails = rows[:, width:]
    grad_mixed[...] = times(tails, hiddens[...], 0, 0)[:heads]
    own = losses.shape[1]
    from_own = rows[pl.ds(pl.multiple_of(info[dp_at] * own, own), own), width:].astype(f32)
    column = from_own[:, heads : heads + 1] + from_own[:, heads + 1 : heads + 2]
    diagonal = lax.broadcasted_iota(jnp.int32, (own, own), 0) == lax.broadcasted_iota(
        jnp.int32, (own, own), 1
    )
    losses[...] = jnp.sum(jnp.where(diagonal, column, 0.0), axis=0, keepdims=True)
    for copy in copies:
        copy.wait()


def outer(heads, order, dp_at, queries, info, latents, hiddens, parts):
    row_count, total = latents.shape
    width = heads * DI
    steps = 8
    hidden_count = hiddens.shape[1]
    return pl.pallas_call(
        functools.partial(outer_kernel, heads, order, dp_at),
        out_shape=(
            jax.ShapeDtypeStruct((row_count, width), f32),
            jax.ShapeDtypeStruct((heads, hidden_count), f32),
            jax.ShapeDtypeStruct((1, queries), f32),
        ),
        in_specs=[in_smem()] + [in_vmem()] * (2 + len(parts)),
        out_specs=(pl.BlockSpec(memory_space=pl.ANY), in_vmem(), in_vmem()),
        scratch_shapes=[
            pltpu.VMEM((total, width + lanes), bf16),
            pltpu.VMEM((steps, row_count, width // steps), f32),
            pltpu.SemaphoreType.DMA((steps,)),
        ],
        compiler_params=params(),
        cost_estimate=pl.CostEstimate(
            flops=2 * total * row_count * width,
            bytes_accessed=4 * row_count * width + 2 * total * width,
            transcendentals=0,
        ),
        name="outer",
    )(info, latents, hiddens, *parts)


def per_device(
    q_latent, hidden, main_queries, main_keys, index_keys, positions, w_query, w_weights
):
    n = lax.axis_size("ctx")
    z = lax.axis_index("ctx")
    head_size = lax.axis_size("head")
    y = lax.axis_index("head")
    dp_size = lax.axis_size("dp")
    dp = lax.axis_index("dp")
    ring = folded_ring(n)
    rows = main_keys.shape[1]
    half = rows // head_size
    rows_latent = w_query.shape[0]
    heads_here = w_weights.shape[1]
    queries_here = main_queries.shape[1]
    sequence_positions = positions[0]

    def onward(x, t=1):
        return lax.ppermute(x, "ctx", [(ring[k], ring[(k + t) % n]) for k in range(n)])

    def swap_head(x):
        return lax.ppermute(x, "head", [(0, 1), (1, 0)])

    def swap_dp(x, bit):
        return lax.ppermute(x, "dp", [(k, k ^ bit) for k in range(dp_size)])

    def over_dp(x):
        gathered, bit = [x], dp_size // 2
        while bit:
            gathered, bit = gathered + [swap_dp(one, bit) for one in gathered], bit // 2
        return gathered

    table = jnp.array(device_table(n, head_size, dp_size, rows))
    info = lax.dynamic_index_in_dim(table, (z * head_size + y) * dp_size + dp, 0, False)

    keys_mine = [lax.dynamic_slice_in_dim(main_keys[0].T, y * half, half, 1)]
    keys_mine.append(onward(keys_mine[0]))
    queries = main_queries[0]
    other_queries = swap_head(queries)
    index_parts = [lax.dynamic_slice_in_dim(index_keys[0], y * half, half)] + [None] * (n - 1)
    index_parts[1] = onward(index_parts[0])
    index_parts[n - 1] = onward(index_parts[0], n - 1)
    parts, kept = project(info, queries_here, q_latent[0], w_query, hidden[0], w_weights.T)
    summed = onward(parts[0]) + parts[1]
    order_at = 1 + 3 * n
    dp_at = order_at + n * dp_size
    weights, tops, before = [], [], None

    def score_next(keys):
        nonlocal before
        t = len(weights)
        numer, top, *before = score(
            t, n, info, sequence_positions, queries, other_queries, keys, before
        )
        weights.append(numer)
        tops.append(top)

    index_own = index_other = None
    for t in range(1, n - 1):
        if t == 1:
            sent_on, summed, index_parts, kept = lax.optimization_barrier(
                (keys_mine[t], summed, index_parts, kept)
            )
            for k in range(2, n - 1):
                index_parts[k] = onward(index_parts[1]) if k == 2 else onward(index_parts[0], k)
            index_own = jnp.concatenate(index_parts)
            index_own, other_queries = lax.optimization_barrier((index_own, other_queries))
            index_other = swap_head(index_own)
            over_half = swap_dp(kept, dp_size // 2)
            kept = [kept, over_half, swap_dp(kept, dp_size // 4)]
        elif t == 2:
            sent_on, summed, index_other, kept = lax.optimization_barrier(
                (keys_mine[t], summed, index_other, kept)
            )
            kept = kept + [swap_dp(kept[1], dp_size // 4)]
        else:
            sent_on, summed = lax.optimization_barrier((keys_mine[t], summed))
        keys_mine[t] = sent_on
        keys_mine.append(onward(sent_on))
        summed = onward(summed)
        if t + 1 < n - 1:
            summed = summed + parts[t + 1]
    received = summed
    latents, hiddens = arrange(dp_at, info, rows_latent, kept)
    other_queries, latents, hiddens = lax.optimization_barrier((other_queries, latents, hiddens))
    while len(weights) < n - 1:
        score_next(keys_mine[len(weights)])
    before, received = lax.optimization_barrier((before, received))

    part = make_logits(heads_here, received, parts[n - 1], index_own, index_other)
    probs, log_probs = make_softmax(n, info, sequence_positions, part, swap_head(part))

    before, probs, log_probs = lax.optimization_barrier((before, probs, log_probs))
    score_next(keys_mine[n - 1])
    delta_own, sent = make_delta(weights, tops, *before, swap_head(jnp.stack(before)), probs)
    piece = gradients(
        heads_here,
        n,
        received,
        parts[n - 1],
        index_own,
        index_other,
        probs,
        log_probs,
        delta_own,
        sent,
        swap_head(sent),
    )[None]

    brought = []
    for t in range(1, n):
        pairs = [(k, (k + t) % n) for k in range(n)]
        brought.append(lax.ppermute(piece, "ctx", pairs))
    own_pieces = over_dp(piece)
    brought, own_pieces = lax.optimization_barrier((jnp.concatenate(brought), own_pieces))
    brought = over_dp(brought)
    if queries_here % 16:
        flat = jnp.concatenate([jnp.concatenate([a, b]) for a, b in zip(own_pieces, brought)])
        order = jnp.argsort(info[order_at : order_at + n * dp_size])
        parts_in, order = [flat[order].reshape(1, -1, flat.shape[2])], None
    else:
        parts_in, order = own_pieces + brought, []
        order += [order_at + k * n for k in range(dp_size)]
        order += [order_at + k * n + t for k in range(dp_size) for t in range(1, n)]
    grad_query, grad_weights, losses = outer(
        heads_here,
        order,
        dp_at,
        q_latent.shape[1],
        info,
        latents,
        hiddens,
        parts_in,
    )
    return (grad_query, grad_weights.T, losses)


def solution(mesh):
    return jax.shard_map(
        per_device,
        mesh=mesh,
        in_specs=(
            P("dp", None, None),
            P("dp", None, None),
            P("dp", "ctx", "head", None),
            P("dp", "ctx", None),
            P("dp", "ctx", None),
            P("dp", None),
            P("ctx", "head"),
            P("ctx", "head"),
        ),
        out_specs=(P("ctx", "head"), P("ctx", "head"), P("dp", None)),
        check_vma=False,
    )
```

```python
import functools
import math

import jax
import jax.numpy as jnp
import numpy as np
from jax import lax
from jax.experimental import pallas as pl
from jax.experimental.pallas import tpu as pltpu
from jax.sharding import PartitionSpec as P

HI = 64
DI = 128
HM = 128

index_scale = (HI * DI) ** (-0.5)
exponent_scale = 192.0 ** (-0.5) / math.log(2.0)
masked_floor = -1e30
lanes = 128
f32 = jnp.float32
bf16 = jnp.bfloat16
vmem_limit = 24 * 2**20
group_size = 4


def folded_ring(size):
    return [0] + list(range(1, size, 2)) + list(range(2, size, 2))[::-1]


def params():
    return pltpu.CompilerParams(vmem_limit_bytes=vmem_limit)


def in_smem():
    return pl.BlockSpec(memory_space=pltpu.SMEM)


def in_vmem():
    return pl.BlockSpec(memory_space=pltpu.VMEM)


def times(a, b, axis_a, axis_b):
    return lax.dot_general(a, b, (((axis_a,), (axis_b,)), ((), ())), preferred_element_type=f32)


def device_table(n, heads, dp_size, rows):
    ring = folded_ring(n)
    half = rows // heads
    flips = dp_flips(dp_size)
    table = []
    for z in range(n):
        place = ring.index(z)
        behind = [ring[(place - t) % n] for t in range(n)]
        for y in range(heads):
            for dp in range(dp_size):
                row = [z] + [ring[(place - 1 - t) % n] for t in range(n)]
                row += [k * rows + y * half for k in behind]
                row += [k * rows + (1 - y) * half for k in behind]
                row += [(dp ^ k) * n + (z - t) % n for k in flips for t in range(n)]
                row += [dp ^ k for k in flips]
                table.append(row)
    return np.array(table, np.int32)


def dp_flips(dp_size):
    flips, bit = [0], dp_size // 2
    while bit:
        flips, bit = flips + [k ^ bit for k in flips], bit // 2
    return flips


def project_kernel(aligned, info, latent, weight, hidden, hidden_weight, *outs):
    *parts, kept = outs
    width = weight.shape[1]
    heads = hidden_weight.shape[0]
    count = parts[0].shape[0]
    if aligned:
        starts = [pl.multiple_of(info[1 + k] * count, count) for k in range(len(parts))]
        rows = jnp.concatenate([latent[pl.ds(k, count), :] for k in starts], axis=0)
        mixed_rows = jnp.concatenate([hidden[pl.ds(k, count), :] for k in starts], axis=0)
    else:
        rows, mixed_rows = latent[...], hidden[...]
    for at in range(0, width, 512):
        product = times(rows, weight[:, at : at + 512], 1, 0)
        for k, out in enumerate(parts):
            out[:, at : at + 512] = product[k * count : (k + 1) * count]
    mixed = times(mixed_rows, hidden_weight[...], 1, 1)
    for k, out in enumerate(parts):
        out[:, width : width + heads] = mixed[k * count : (k + 1) * count]
        out[:, width + heads :] = jnp.zeros((count, lanes - heads), f32)
    kept[:, : latent.shape[1]] = latent[...]
    kept[:, latent.shape[1] :] = hidden[...]


def project(info, count, latent, weight, hidden, hidden_weight):
    queries, width = latent.shape[0], weight.shape[1]
    depth, hidden_depth = weight.shape[0], hidden_weight.shape[1]
    blocks = queries // count
    aligned = count % 16 == 0 and depth % lanes == 0 and hidden_depth % lanes == 0
    columns = lambda i, info: (0, info[0])
    whole = lambda i, info: (0, 0)
    kept = None
    if not aligned:
        latent = lax.dynamic_slice_in_dim(latent, info[0] * depth, depth, 1)
        hidden = lax.dynamic_slice_in_dim(hidden, info[0] * hidden_depth, hidden_depth, 1)
        kept = jnp.concatenate([latent, hidden], axis=1)
        order = info[1 : 1 + blocks]
        latent = latent.reshape(blocks, count, depth)[order].reshape(queries, depth)
        hidden = hidden.reshape(blocks, count, hidden_depth)[order].reshape(queries, hidden_depth)
        columns = whole
    *parts, kept_here = pl.pallas_call(
        functools.partial(project_kernel, aligned),
        grid_spec=pltpu.PrefetchScalarGridSpec(
            num_scalar_prefetch=1,
            grid=(1,),
            in_specs=[
                pl.BlockSpec((queries, depth), columns),
                pl.BlockSpec((depth, width), whole),
                pl.BlockSpec((queries, hidden_depth), columns),
                pl.BlockSpec(hidden_weight.shape, whole),
            ],
            out_specs=[pl.BlockSpec((count, width + lanes), whole)] * blocks
            + [pl.BlockSpec((queries, depth + hidden_depth), whole)],
        ),
        out_shape=[jax.ShapeDtypeStruct((count, width + lanes), f32)] * blocks
        + [jax.ShapeDtypeStruct((queries, depth + hidden_depth), bf16)],
        compiler_params=params(),
        cost_estimate=pl.CostEstimate(
            flops=2 * queries * weight.size, bytes_accessed=2 * weight.size, transcendentals=0
        ),
        name="project",
    )(info, latent, weight, hidden, hidden_weight)
    return parts, kept_here if aligned else kept


def score_kernel(
    t,
    base_at,
    info,
    positions,
    mine,
    other,
    keys,
    top_before,
    mass_before,
    weights,
    top,
    top_all,
    mass_all,
    mass,
    even,
    odd,
):
    count, heads, depth = mine.shape
    limits = [positions[info[0] * count + q] - info[base_at] for q in range(count)]
    span = keys.shape[1]
    key_at = lax.broadcasted_iota(jnp.int32, (1, span), 1)
    row_at = lax.broadcasted_iota(jnp.int32, (heads, lanes), 0)
    lane_at = lax.broadcasted_iota(jnp.int32, (heads, lanes), 1)
    group = min(group_size, count)
    work = [(at, k) for at in range(0, count, group) for k in range(2)]
    held = (even, odd)

    def multiply(step):
        at, k = work[step]
        rows = (mine, other)[k][at : at + group].reshape(group * heads, depth)
        held[step % 2][...] = times(rows, keys[...], 1, 0)

    multiply(0)
    for step, (at, k) in enumerate(work):
        if step + 1 < len(work):
            multiply(step + 1)
        scores = held[step % 2]
        offset = k * heads
        diagonal = lane_at == row_at + offset
        for i in range(group):
            q = at + i
            one = jnp.where(
                key_at <= limits[q], scores[i * heads : (i + 1) * heads, :], masked_floor
            )
            high = jnp.max(one, axis=1, keepdims=True)
            shifted = jnp.exp2((one - high) * exponent_scale)
            total = jnp.sum(shifted, axis=1, keepdims=True)
            weights[q, offset : offset + heads] = shifted.astype(bf16)
            high_row = jnp.sum(jnp.where(diagonal, high, 0.0), axis=0, keepdims=True)
            total_row = jnp.sum(jnp.where(diagonal, total, 0.0), axis=0, keepdims=True)
            if k == 0:
                top[q : q + 1, :] = high_row
                mass[q : q + 1, :] = total_row
            else:
                top[q : q + 1, :] += high_row
                mass[q : q + 1, :] += total_row
    if t == 0:
        top_all[...] = top[...]
        mass_all[...] = mass[...]
    else:
        before, now = top_before[...], top[...]
        joint = jnp.maximum(before, now)
        top_all[...] = joint
        mass_all[...] = mass_before[...] * jnp.exp2((before - joint) * exponent_scale) + mass[
            ...
        ] * jnp.exp2((now - joint) * exponent_scale)


def score(t, n, info, positions, mine, other, keys, before):
    count, heads, depth = mine.shape
    span = keys.shape[1]
    stats = jax.ShapeDtypeStruct((count, lanes), f32)
    if before is None:
        before = (jnp.zeros((count, lanes), f32),) * 2
    return pl.pallas_call(
        functools.partial(score_kernel, t, 1 + n + t),
        out_shape=(jax.ShapeDtypeStruct((count, 2 * heads, span), bf16), stats, stats, stats),
        in_specs=[in_smem()] * 2 + [in_vmem()] * 5,
        out_specs=(in_vmem(),) * 4,
        scratch_shapes=[pltpu.VMEM((count, lanes), f32)]
        + [pltpu.VMEM((min(group_size, count) * heads, span), f32)] * 2,
        compiler_params=params(),
        cost_estimate=pl.CostEstimate(
            flops=4 * count * heads * depth * span,
            bytes_accessed=2 * (2 * mine.size + keys.size + 2 * count * heads * span),
            transcendentals=2 * count * heads * span,
        ),
        name="score",
    )(info, positions, mine, other, keys, *before)


def delta_kernel(blocks, *refs):
    weights, tops = refs[:blocks], refs[blocks : 2 * blocks]
    top, mass, far, probs, out, sent, held = refs[2 * blocks :]
    count, heads, span = weights[0].shape
    far_top = pltpu.roll(far[0], heads // 2, 1)
    far_mass = pltpu.roll(far[1], heads // 2, 1)
    joint = jnp.maximum(top[...], far_top)
    total = mass[...] * jnp.exp2((top[...] - joint) * exponent_scale) + far_mass * jnp.exp2(
        (far_top - joint) * exponent_scale
    )
    row_at = lax.broadcasted_iota(jnp.int32, (heads, lanes), 0)
    lane_at = lax.broadcasted_iota(jnp.int32, (heads, lanes), 1)
    diagonal = row_at == lane_at
    inverse = 1.0 / (total * HM)
    for t in range(blocks):
        factor = jnp.exp2((tops[t][...] - joint) * exponent_scale) * inverse
        for q in range(count):
            column = jnp.sum(
                jnp.where(diagonal, factor[q : q + 1, :], 0.0), axis=1, keepdims=True
            )
            mixed = weights[t][q].astype(f32) * column
            held[q : q + 1, t * span : (t + 1) * span] = jnp.sum(mixed, axis=0, keepdims=True)
    delta = probs[0] - held[...]
    out[...] = delta
    sent[...] = delta.astype(bf16)


def make_delta(weights, tops, top, mass, far, probs):
    blocks = len(weights)
    count, heads, span = weights[0].shape
    return pl.pallas_call(
        functools.partial(delta_kernel, blocks),
        out_shape=(
            jax.ShapeDtypeStruct((count, blocks * span), f32),
            jax.ShapeDtypeStruct((count, blocks * span), bf16),
        ),
        in_specs=[in_vmem()] * (2 * blocks + 4),
        out_specs=(in_vmem(),) * 2,
        scratch_shapes=[pltpu.VMEM((count, blocks * span), f32)],
        compiler_params=params(),
        cost_estimate=pl.CostEstimate(
            flops=2 * blocks * count * heads * span,
            bytes_accessed=2 * blocks * count * heads * span,
            transcendentals=0,
        ),
        name="delta",
    )(*weights, *tops, top, mass, far, probs)


def query_rows(total, heads):
    return jnp.concatenate(
        [total[:, j * DI : (j + 1) * DI].astype(bf16) for j in range(heads)], axis=0
    )


def logits_kernel(heads, received, here, own, other, out):
    count = received.shape[0]
    total = received[...] + here[...]
    query = query_rows(total, heads)
    columns = [total[:, heads * DI + j : heads * DI + j + 1] for j in range(heads)]
    span = 512
    for part, keys in enumerate((own, other)):
        for at in range(0, keys.shape[0], span):
            affinity = times(query, keys[at : at + span, :], 1, 1)
            running = jnp.zeros((count, span), f32)
            for j in range(heads):
                reached = jnp.maximum(affinity[j * count : (j + 1) * count], 0.0)
                running = running + columns[j] * reached
            out[part, :, at : at + span] = running * index_scale


def make_logits(heads, received, here, own, other):
    count, length = received.shape[0], own.shape[0]
    return pl.pallas_call(
        functools.partial(logits_kernel, heads),
        out_shape=jax.ShapeDtypeStruct((2, count, length), f32),
        in_specs=[in_vmem()] * 4,
        out_specs=in_vmem(),
        compiler_params=params(),
        cost_estimate=pl.CostEstimate(
            flops=4 * count * heads * DI * length,
            bytes_accessed=4 * (2 * received.size + 2 * count * length) + 4 * length * DI,
            transcendentals=0,
        ),
        name="logits",
    )(received, here, own, other)


def softmax_kernel(blocks, info, positions, part, far, probs, log_probs):
    _, count, length = part.shape
    span = length // blocks
    row_at = lax.broadcasted_iota(jnp.int32, (count, lanes), 0)
    position = jnp.zeros((count, lanes), jnp.int32)
    for q in range(count):
        position = jnp.where(row_at == q, positions[info[0] * count + q], position)
    position = position[:, 0:1]
    key_at = lax.broadcasted_iota(jnp.int32, (count, span), 1)

    def seen(side, t):
        return key_at + info[1 + (1 + side) * blocks + t] <= position

    highs = []
    for side in range(2):
        high = jnp.full((count, span), masked_floor, f32)
        for t in range(blocks):
            at = slice(t * span, (t + 1) * span)
            value = part[side, :, at] + far[1 - side, :, at]
            log_probs[side, :, at] = value
            high = jnp.maximum(high, jnp.where(seen(side, t), value, masked_floor))
        highs.append(jnp.max(high, axis=1, keepdims=True))
    high = jnp.maximum(highs[0], highs[1])
    sums = []
    for side in range(2):
        running = jnp.zeros((count, span), f32)
        for t in range(blocks):
            at = slice(t * span, (t + 1) * span)
            grown = jnp.where(seen(side, t), jnp.exp(log_probs[side, :, at] - high), 0.0)
            probs[side, :, at] = grown
            running = running + grown
        sums.append(jnp.sum(running, axis=1, keepdims=True))
    mass = sums[0] + sums[1]
    level = high + jnp.log(mass)
    inverse = 1.0 / mass
    for side in range(2):
        for t in range(blocks):
            at = slice(t * span, (t + 1) * span)
            probs[side, :, at] = probs[side, :, at] * inverse
            log_probs[side, :, at] = jnp.where(seen(side, t), log_probs[side, :, at] - level, 0.0)


def make_softmax(blocks, info, positions, part, far):
    return pl.pallas_call(
        functools.partial(softmax_kernel, blocks),
        out_shape=(jax.ShapeDtypeStruct(part.shape, f32),) * 2,
        in_specs=[in_smem()] * 2 + [in_vmem()] * 2,
        out_specs=(in_vmem(),) * 2,
        compiler_params=params(),
        cost_estimate=pl.CostEstimate(
            flops=8 * part.size, bytes_accessed=16 * part.size, transcendentals=part.size
        ),
        name="softmax",
    )(info, positions, part, far)


def gradient_kernel(
    heads,
    blocks,
    received,
    here,
    own,
    other,
    probs,
    log_probs,
    delta_own,
    sent,
    brought,
    out,
    flow,
    query_sum,
    grads,
    even,
    odd,
):
    count = received.shape[0]
    total = received[...] + here[...]
    span = own.shape[0] // blocks
    query = query_rows(total, heads)
    columns = [
        total[:, heads * DI + j : heads * DI + j + 1] * index_scale for j in range(heads)
    ]
    work = [(side, t) for side in range(2) for t in range(blocks)]
    held = (even, odd)

    def multiply(step):
        side, t = work[step]
        keys = (own, other)[side][t * span : (t + 1) * span, :]
        held[step % 2][...] = times(query, keys, 1, 1)

    multiply(0)
    flow[...] = jnp.zeros(flow.shape, f32)
    running = [jnp.zeros((count, span), f32)] * 2
    for step, (side, t) in enumerate(work):
        if step + 1 < len(work):
            multiply(step + 1)
        at = slice(t * span, (t + 1) * span)
        affinity = held[step % 2]
        rounded = (sent, brought)[side][:, at].astype(f32)
        delta = delta_own[:, at] if side == 0 else rounded
        wanted = probs[side, :, at] - rounded
        running[side] = running[side] + wanted * log_probs[side, :, at]
        for j in range(heads):
            rows = slice(j * count, (j + 1) * count)
            one = affinity[rows, :]
            reached = jnp.where(one > 0, delta, 0.0)
            grads[rows, :] = (reached * columns[j]).astype(bf16)
            product = reached * one
            folded = product[:, :lanes]
            for k in range(lanes, span, lanes):
                folded = folded + product[:, k : k + lanes]
            flow[rows, :] += folded
        keys = (own, other)[side][at, :]
        product = times(grads[...], keys, 1, 0)
        if step == 0:
            query_sum[...] = product
        else:
            query_sum[...] += product
    losses = [jnp.sum(one, axis=1, keepdims=True) for one in running]
    loss = -(losses[0] + losses[1])
    lane_at = lax.broadcasted_iota(jnp.int32, (count, lanes), 1)
    tail = jnp.zeros((count, lanes), f32)
    for j in range(heads):
        rows = slice(j * count, (j + 1) * count)
        out[:, j * DI : (j + 1) * DI] = query_sum[rows, :].astype(bf16)
        column = jnp.sum(flow[rows, :], axis=1, keepdims=True) * index_scale
        tail = jnp.where(lane_at == j, column, tail)
    loss_high = loss.astype(bf16).astype(f32)
    tail = jnp.where(lane_at == heads, loss_high, tail)
    tail = jnp.where(lane_at == heads + 1, loss - loss_high, tail)
    out[:, heads * DI :] = tail.astype(bf16)


def gradients(heads, blocks, received, here, own, other, probs, log_probs, delta_own, sent, brought):
    count, length = received.shape[0], own.shape[0]
    span = length // blocks
    return pl.pallas_call(
        functools.partial(gradient_kernel, heads, blocks),
        out_shape=jax.ShapeDtypeStruct((count, heads * DI + lanes), bf16),
        in_specs=[in_vmem()] * 9,
        out_specs=in_vmem(),
        scratch_shapes=[
            pltpu.VMEM((heads * count, lanes), f32),
            pltpu.VMEM((heads * count, DI), f32),
            pltpu.VMEM((heads * count, span), bf16),
            pltpu.VMEM((heads * count, span), f32),
            pltpu.VMEM((heads * count, span), f32),
        ],
        compiler_params=params(),
        cost_estimate=pl.CostEstimate(
            flops=8 * count * heads * DI * length,
            bytes_accessed=4 * (2 * received.size + 6 * count * length) + 4 * length * DI,
            transcendentals=0,
        ),
        name="gradient",
    )(received, here, own, other, probs, log_probs, delta_own, sent, brought)


def arrange_kernel(at, info, *refs):
    kept, (latents, hiddens, held) = refs[:-3], refs[-3:]
    queries, depth = kept[0].shape[0], latents.shape[0]
    for k, one in enumerate(kept):
        to = pl.ds(pl.multiple_of(info[at + k] * queries, queries), queries)
        held[to, :] = one[:, :depth].astype(f32)
        hiddens[to, :] = one[:, depth:]
    latents[...] = held[...].T.astype(bf16)


def arrange(at, info, depth, kept):
    queries, width = kept[0].shape
    total = queries * len(kept)
    return pl.pallas_call(
        functools.partial(arrange_kernel, at),
        out_shape=(
            jax.ShapeDtypeStruct((depth, total), bf16),
            jax.ShapeDtypeStruct((total, width - depth), bf16),
        ),
        in_specs=[in_smem()] + [in_vmem()] * len(kept),
        out_specs=(in_vmem(),) * 2,
        scratch_shapes=[pltpu.VMEM((total, depth), f32)],
        compiler_params=params(),
        cost_estimate=pl.CostEstimate(
            flops=0, bytes_accessed=4 * total * width, transcendentals=0
        ),
        name="arrange",
    )(info, *kept)


def outer_kernel(heads, order, dp_at, info, latents, hiddens, *refs):
    parts, (grad, grad_mixed, losses, rows, blocks, sems) = refs[:-6], refs[-6:]
    count = parts[0].shape[-2]
    width = heads * DI
    steps, _, span = blocks.shape
    k = 0
    for part in parts:
        for t in range(part.shape[0]):
            to = 0 if order is None else pl.multiple_of(info[order[k]] * count, count)
            rows[pl.ds(to, count), :] = part[t]
            k += 1
    copies = []
    for i in range(steps):
        at = slice(i * span, (i + 1) * span)
        blocks[i] = times(latents[...], rows[:, at], 1, 0)
        copies.append(pltpu.make_async_copy(blocks.at[i], grad.at[:, at], sems.at[i]))
        copies[-1].start()
    tails = rows[:, width:]
    grad_mixed[...] = times(tails, hiddens[...], 0, 0)[:heads]
    own = losses.shape[1]
    from_own = rows[pl.ds(pl.multiple_of(info[dp_at] * own, own), own), width:].astype(f32)
    column = from_own[:, heads : heads + 1] + from_own[:, heads + 1 : heads + 2]
    diagonal = lax.broadcasted_iota(jnp.int32, (own, own), 0) == lax.broadcasted_iota(
        jnp.int32, (own, own), 1
    )
    losses[...] = jnp.sum(jnp.where(diagonal, column, 0.0), axis=0, keepdims=True)
    for copy in copies:
        copy.wait()


def outer(heads, order, dp_at, queries, info, latents, hiddens, parts):
    row_count, total = latents.shape
    width = heads * DI
    steps = 8
    hidden_count = hiddens.shape[1]
    return pl.pallas_call(
        functools.partial(outer_kernel, heads, order, dp_at),
        out_shape=(
            jax.ShapeDtypeStruct((row_count, width), f32),
            jax.ShapeDtypeStruct((heads, hidden_count), f32),
            jax.ShapeDtypeStruct((1, queries), f32),
        ),
        in_specs=[in_smem()] + [in_vmem()] * (2 + len(parts)),
        out_specs=(pl.BlockSpec(memory_space=pl.ANY), in_vmem(), in_vmem()),
        scratch_shapes=[
            pltpu.VMEM((total, width + lanes), bf16),
            pltpu.VMEM((steps, row_count, width // steps), f32),
            pltpu.SemaphoreType.DMA((steps,)),
        ],
        compiler_params=params(),
        cost_estimate=pl.CostEstimate(
            flops=2 * total * row_count * width,
            bytes_accessed=4 * row_count * width + 2 * total * width,
            transcendentals=0,
        ),
        name="outer",
    )(info, latents, hiddens, *parts)


def per_device(
    q_latent, hidden, main_queries, main_keys, index_keys, positions, w_query, w_weights
):
    n = lax.axis_size("ctx")
    z = lax.axis_index("ctx")
    head_size = lax.axis_size("head")
    y = lax.axis_index("head")
    dp_size = lax.axis_size("dp")
    dp = lax.axis_index("dp")
    ring = folded_ring(n)
    rows = main_keys.shape[1]
    half = rows // head_size
    rows_latent = w_query.shape[0]
    heads_here = w_weights.shape[1]
    queries_here = main_queries.shape[1]
    sequence_positions = positions[0]

    def onward(x, t=1):
        return lax.ppermute(x, "ctx", [(ring[k], ring[(k + t) % n]) for k in range(n)])

    def swap_head(x):
        return lax.ppermute(x, "head", [(0, 1), (1, 0)])

    def swap_dp(x, bit):
        return lax.ppermute(x, "dp", [(k, k ^ bit) for k in range(dp_size)])

    def over_dp(x):
        gathered, bit = [x], dp_size // 2
        while bit:
            gathered, bit = gathered + [swap_dp(one, bit) for one in gathered], bit // 2
        return gathered

    table = jnp.array(device_table(n, head_size, dp_size, rows))
    info = lax.dynamic_index_in_dim(table, (z * head_size + y) * dp_size + dp, 0, False)

    keys_mine = [lax.dynamic_slice_in_dim(main_keys[0].T, y * half, half, 1)]
    keys_mine.append(onward(keys_mine[0]))
    queries = main_queries[0]
    other_queries = swap_head(queries)
    index_parts = [lax.dynamic_slice_in_dim(index_keys[0], y * half, half)] + [None] * (n - 1)
    index_parts[1] = onward(index_parts[0])
    index_parts[n - 1] = onward(index_parts[0], n - 1)
    parts, kept = project(info, queries_here, q_latent[0], w_query, hidden[0], w_weights.T)
    summed = onward(parts[0]) + parts[1]
    order_at = 1 + 3 * n
    dp_at = order_at + n * dp_size
    weights, tops, before = [], [], None

    def score_next(keys):
        nonlocal before
        t = len(weights)
        numer, top, *before = score(
            t, n, info, sequence_positions, queries, other_queries, keys, before
        )
        weights.append(numer)
        tops.append(top)

    index_own = index_other = None
    for t in range(1, n - 1):
        if t == 1:
            sent_on, summed, index_parts, kept = lax.optimization_barrier(
                (keys_mine[t], summed, index_parts, kept)
            )
            for k in range(2, n - 1):
                index_parts[k] = onward(index_parts[1]) if k == 2 else onward(index_parts[0], k)
            index_own = jnp.concatenate(index_parts)
            index_own, other_queries = lax.optimization_barrier((index_own, other_queries))
            index_other = swap_head(index_own)
            over_half = swap_dp(kept, dp_size // 2)
            kept = [kept, over_half, swap_dp(kept, dp_size // 4)]
        elif t == 2:
            sent_on, summed, index_other, kept = lax.optimization_barrier(
                (keys_mine[t], summed, index_other, kept)
            )
            kept = kept + [swap_dp(kept[1], dp_size // 4)]
        else:
            sent_on, summed = lax.optimization_barrier((keys_mine[t], summed))
        keys_mine[t] = sent_on
        keys_mine.append(onward(sent_on))
        summed = onward(summed)
        if t + 1 < n - 1:
            summed = summed + parts[t + 1]
    received = summed
    latents, hiddens = arrange(dp_at, info, rows_latent, kept)
    other_queries, latents, hiddens = lax.optimization_barrier((other_queries, latents, hiddens))
    while len(weights) < n - 1:
        score_next(keys_mine[len(weights)])
    before, received = lax.optimization_barrier((before, received))

    part = make_logits(heads_here, received, parts[n - 1], index_own, index_other)
    far = swap_head(part)
    before, far = lax.optimization_barrier((before, far))
    probs, log_probs = make_softmax(n, info, sequence_positions, part, far)

    score_next(keys_mine[n - 1])
    delta_own, sent = make_delta(weights, tops, *before, swap_head(jnp.stack(before)), probs)
    piece = gradients(
        heads_here,
        n,
        received,
        parts[n - 1],
        index_own,
        index_other,
        probs,
        log_probs,
        delta_own,
        sent,
        swap_head(sent),
    )[None]

    brought = []
    for t in range(1, n):
        pairs = [(k, (k + t) % n) for k in range(n)]
        brought.append(lax.ppermute(piece, "ctx", pairs))
    own_pieces = over_dp(piece)
    brought, own_pieces = lax.optimization_barrier((jnp.concatenate(brought), own_pieces))
    brought = over_dp(brought)
    if queries_here % 16:
        flat = jnp.concatenate([jnp.concatenate([a, b]) for a, b in zip(own_pieces, brought)])
        order = jnp.argsort(info[order_at : order_at + n * dp_size])
        parts_in, order = [flat[order].reshape(1, -1, flat.shape[2])], None
    else:
        parts_in, order = own_pieces + brought, []
        order += [order_at + k * n for k in range(dp_size)]
        order += [order_at + k * n + t for k in range(dp_size) for t in range(1, n)]
    grad_query, grad_weights, losses = outer(
        heads_here,
        order,
        dp_at,
        q_latent.shape[1],
        info,
        latents,
        hiddens,
        parts_in,
    )
    return (grad_query, grad_weights.T, losses)


def solution(mesh):
    return jax.shard_map(
        per_device,
        mesh=mesh,
        in_specs=(
            P("dp", None, None),
            P("dp", None, None),
            P("dp", "ctx", "head", None),
            P("dp", "ctx", None),
            P("dp", "ctx", None),
            P("dp", None),
            P("ctx", "head"),
            P("ctx", "head"),
        ),
        out_specs=(P("ctx", "head"), P("ctx", "head"), P("dp", None)),
        check_vma=False,
    )
```
